32 devices in a mesh: dp: 16 (over z, y, x), twin: 2 (over core).
Axes of the slice: x: 2, y: 2, z: 4, core: 2. Of those that a mesh axis runs over, the one named last changes fastest.
Arguments:
- states: float32 [17, 262144], P(None, 'dp'), may hold values from -6 to 6
- actions: float32 [6, 262144], P(None, 'dp'), may hold values from -1 to 1
- rewards: float32 [262144], P('dp'), may hold values from -10 to 10
- next_states: float32 [17, 262144], P(None, 'dp'), may hold values from -6 to 6
- done_flags: int32 [262144], P('dp'), may hold values 0 or 1
- smoothing: float32 [6, 262144], P(None, 'dp'), may hold values from -6 to 6
- actor_weights: float32 [71942], replicated, may hold values from -1 to 1
- actor_first: float32 [71942], replicated, may hold values from -0.046875 to 0.046875
- actor_second: float32 [71942], replicated, may hold values from 5e-07 to 8e-06
- critic_weights: float32 [2, 72193], P('twin'), may hold values from -1 to 1
- critic_first: float32 [2, 72193], P('twin'), may hold values from -0.0034179688 to 0.0034179688
- critic_second: float32 [2, 72193], P('twin'), may hold values from 1.9073487e-09 to 3.051758e-08
- target_actor: float32 [71942], replicated, may hold values from -1 to 1
- target_critic: float32 [2, 72193], P('twin'), may hold values from -1 to 1
Outputs:
- new_actor: float32 [71942], replicated
- new_actor_first: float32 [71942], replicated
- new_actor_second: float32 [71942], replicated
- new_critic: float32 [2, 72193], P('twin')
- new_critic_first: float32 [2, 72193], P('twin')
- new_critic_second: float32 [2, 72193], P('twin')
- new_target_actor: float32 [71942], replicated
- new_target_critic: float32 [2, 72193], P('twin')
- critic_loss: float32 [2], P('twin')
- actor_loss: float32 [], replicated
The draws below stay inside these ranges and needn't reach their ends.
All inputs are finite; a program needn't handle non-finite values. No bound on the sum of `done_flags` on one device may be relied on, other than what follows from the above.
Results may differ from the reference program's by a relative error of at most 0.0003.
The reference program's roundings to bfloat16 on the way count: a program that leaves them out, or rounds other values in their place, can miss the bound.
Values sent between devices are 32-bit elements; how exact they have to be, the bound alone decides.
No kernel may reach another device: no remote copies, remote signals or barrier semaphores. Data moves between devices by JAX's collectives and lax.ppermute only.
A program may use at most 192 MiB of HBM per device.

```python
import math
import jax
import jax.numpy as jnp
from jax import lax

SDIM = 17
ADIM = 6
HID = 256
RB = 4096
MB = 4
STEP = 10
TOTAL = 262144
PA = 71942
PC = 72193
N_DP = 16


def actor_layers_drawn():
    return ((HID, SDIM), (HID, HID), (ADIM, HID))


def critic_layers_drawn():
    return ((HID, SDIM + ADIM), (HID, HID), (1, HID))


def flat_net(key, layers):
    pieces = []
    for layer_index, (out_size, in_size) in enumerate(layers):
        weight_key = jax.random.fold_in(key, 2 * layer_index)
        bias_key = jax.random.fold_in(key, 2 * layer_index + 1)
        weight = jnp.clip(jax.random.normal(weight_key, (out_size * in_size,), jnp.float32), -4.0, 4.0) * in_size ** (-0.5)
        bias_term = 0.2 * jnp.clip(jax.random.normal(bias_key, (out_size,), jnp.float32), -4.0, 4.0)
        pieces += [weight, bias_term]
    return jnp.concatenate(pieces)


def draw_rewards(key, part):
    key = jax.random.fold_in(key, 5)
    position = jnp.arange(TOTAL, dtype=jnp.float32) / max(TOTAL - 1, 1)
    values = jnp.clip(jax.random.normal(key, (TOTAL,), jnp.float32), -3.0, 3.0)
    return values * (1.0 + 2.0 * position)


def draw_actor_weights(key, part):
    key = jax.random.fold_in(key, 1)
    return flat_net(key, actor_layers_drawn())


def draw_critic_weights(key, part):
    key = jax.random.fold_in(key, 2)
    return jnp.stack([flat_net(jax.random.fold_in(key, 10), critic_layers_drawn()), flat_net(jax.random.fold_in(key, 11), critic_layers_drawn())])


def draw_target_actor(key, part):
    key = jax.random.fold_in(key, 3)
    return flat_net(key, actor_layers_drawn())


def draw_target_critic(key, part):
    key = jax.random.fold_in(key, 4)
    return jnp.stack([flat_net(jax.random.fold_in(key, 10), critic_layers_drawn()), flat_net(jax.random.fold_in(key, 11), critic_layers_drawn())])


def place_ends(result, own_key, smallest, top_value):
    longest = result.shape.index(max(result.shape))
    spots = []
    for shift in (0, 1):
        where = [jax.random.randint(jax.random.fold_in(own_key, axis), (), 0, length) for axis, length in enumerate(result.shape)]
        where[longest] = (where[longest] + shift) % result.shape[longest]
        spots.append(tuple(where))
    return result.at[spots[0]].set(smallest).at[spots[1]].set(top_value)


def shard_levels(rng, shape, shards, least, largest):
    def one(dim, shards_of):
        steps = jax.random.uniform(jax.random.fold_in(jax.random.fold_in(rng, 6), dim), (shards_of,), jnp.float32, least / len(shards), largest / len(shards))
        return jnp.repeat(jnp.exp(steps), shape[dim] // shards_of).reshape((-1,) + (1,) * (len(shape) - dim - 1))

    gain = one(*shards[0])
    for cut in shards[1:]:
        gain = gain * one(*cut)
    return gain


def centred(key, dims, width, most, cuts=(), kind=jnp.bfloat16):
    values = jax.random.normal(key, dims, jnp.float32) * width
    if len(cuts) > 0:
        values = shard_levels(key, dims, cuts, -0.22, 0.18) * values
    return jnp.clip(values, min=-most, max=most).astype(kind)


def setup_inputs(seed: int = 0) -> dict:
    key_list = jax.random.split(jax.random.key(seed), 15)
    states = centred(key_list[0], (SDIM, TOTAL), 1.0, 6.0, ((1, 16),), jnp.float32)
    actions = jnp.clip(jax.random.uniform(key_list[1], (ADIM, TOTAL), jnp.float32, -1.0, 1.0) * shard_levels(key_list[1], (ADIM, TOTAL), ((1, 16),), -0.4, 0.0), -1.0, 1.0)
    rewards = draw_rewards(jax.random.fold_in(key_list[14], 71), 0)
    next_states = centred(key_list[3], (SDIM, TOTAL), 1.0, 6.0, ((1, 16),), jnp.float32)
    done_flags = place_ends((jax.random.randint(key_list[4], (TOTAL,), 0, 20) < 1).astype(jnp.int32), jax.random.fold_in(key_list[4], 1), 0, 1)
    smoothing = centred(key_list[5], (ADIM, TOTAL), 1.0, 6.0, ((1, 16),), jnp.float32)
    actor_weights = draw_actor_weights(jax.random.fold_in(key_list[14], 71), 0)
    actor_first = centred(key_list[7], (PA,), 0.003, 0.046875, (), jnp.float32)
    actor_second = jnp.clip(jnp.exp(jax.random.uniform(key_list[8], (PA,), jnp.float32, math.log(4.999999987376214e-07), math.log(7.999999979801942e-06))), 4.999999987376214e-07, 7.999999979801942e-06)
    critic_weights = draw_critic_weights(jax.random.fold_in(key_list[14], 71), 0)
    critic_first = centred(key_list[10], (2, PC), (0.11 * (RB * MB * N_DP) ** -0.5), 0.0034179688, ((0, 2),), jnp.float32)
    critic_second = jnp.clip(jnp.exp(math.log(3.051757957450718e-08) - 2.7725887 * jax.random.uniform(key_list[11], (2, PC), jnp.float32) ** shard_levels(key_list[11], (2, PC), ((0, 2),), -0.2, 0.2)), 1.907348723406699e-09, 3.051757957450718e-08)
    target_actor = draw_target_actor(jax.random.fold_in(key_list[14], 71), 0)
    target_critic = draw_target_critic(jax.random.fold_in(key_list[14], 71), 0)
    return dict(states=states, actions=actions, rewards=rewards, next_states=next_states, done_flags=done_flags, smoothing=smoothing, actor_weights=actor_weights, actor_first=actor_first, actor_second=actor_second, critic_weights=critic_weights, critic_first=critic_first, critic_second=critic_second, target_actor=target_actor, target_critic=target_critic)


DISCOUNT = 0.99
POLYAK_RATE = 0.005
LEARN_RATE = 0.05
BETA_ONE = 0.9
BETA_TWO = 0.999
EPSILON = 1e-08
WEIGHT_DECAY = 0.01
NOISE_SCALE = 0.2
NOISE_CLIP = 0.5

@jax.custom_vjp
def low(v):
    return lax.optimization_barrier(v.astype(jnp.bfloat16)).astype(jnp.float32)

@jax.custom_vjp
def low_back(v):
    return v

def low_keep(v):
    return (low(v), None)

def low_pass(kept, grad):
    return (grad,)

def back_keep(v):
    return (v, None)

def back_low(kept, grad):
    return (low(grad),)
low.defvjp(low_keep, low_pass)
low_back.defvjp(back_keep, back_low)

def actor_layers():
    return ((HID, SDIM), (HID, HID), (ADIM, HID))

def critic_layers():
    return ((HID, SDIM + ADIM), (HID, HID), (1, HID))

def unchanged(value):
    return value

def unpack(flat_vec, layers):
    params = []
    position = 0
    for out_size, in_size in layers:
        weight = flat_vec[position:position + out_size * in_size].reshape(out_size, in_size)
        position += out_size * in_size
        params.append((weight, flat_vec[position:position + out_size][:, None]))
        position += out_size
    return params

def network(flat_vec, layers, inputs, final_act):
    hidden = inputs
    params = unpack(flat_vec, layers)
    for layer_index, (weight, bias_term) in enumerate(params):
        pre_act = low_back(jnp.dot(low(weight), low(hidden), precision=lax.Precision.HIGHEST) + bias_term)
        hidden = final_act(pre_act) if layer_index == len(params) - 1 else jax.nn.silu(pre_act)
    return hidden

def blocks(array):
    block_count = array.shape[-1] // RB
    return jnp.moveaxis(array.reshape(array.shape[:-1] + (block_count, RB)), -2, 0)

def target_values(target_actor, target_critic, next_rows, jitter_rows, reward_rows, done_rows):
    lagged_out = network(target_actor, actor_layers(), next_rows, jnp.tanh)
    jitter = jnp.clip(NOISE_SCALE * jitter_rows, -NOISE_CLIP, NOISE_CLIP)
    next_action = jnp.clip(lagged_out + jitter, -1.0, 1.0)
    joined = jnp.concatenate([next_rows, next_action], 0)
    lagged_one = network(target_critic[0], critic_layers(), joined, unchanged)[0]
    lagged_two = network(target_critic[1], critic_layers(), joined, unchanged)[0]
    keep_going = 1.0 - done_rows.astype(jnp.float32)
    return reward_rows + DISCOUNT * keep_going * jnp.minimum(lagged_one, lagged_two)

def adamw_step(weight, gradient, moment_one, moment_two):
    moment_one = BETA_ONE * moment_one + (1.0 - BETA_ONE) * gradient
    moment_two = BETA_TWO * moment_two + (1.0 - BETA_TWO) * gradient * gradient
    corrected_one = moment_one / (1.0 - BETA_ONE ** STEP)
    corrected_two = moment_two / (1.0 - BETA_TWO ** STEP)
    weight = weight - LEARN_RATE * (corrected_one / (jnp.sqrt(corrected_two) + EPSILON) + WEIGHT_DECAY * weight)
    return (weight, moment_one, moment_two)

def polyak_mix(lagged, fresh):
    return POLYAK_RATE * fresh + (1.0 - POLYAK_RATE) * lagged

def reference(states, actions, rewards, next_states, done_flags, smoothing, actor_weights, actor_first, actor_second, critic_weights, critic_first, critic_second, target_actor, target_critic):
    batches = (blocks(states), blocks(actions), blocks(rewards), blocks(next_states), blocks(done_flags), blocks(smoothing))
    row_total = states.shape[1]

    def critic_objective(weights_now):

        def scan_step(running, batch):
            state_rows, action_rows, reward_rows, next_rows, done_rows, jitter_rows = batch
            target = target_values(target_actor, target_critic, next_rows, jitter_rows, reward_rows, done_rows)
            joined = jnp.concatenate([state_rows, action_rows], 0)
            losses = [jnp.sum((network(weights_now[critic_index], critic_layers(), joined, unchanged)[0] - target) ** 2) for critic_index in range(2)]
            return (running + jnp.stack(losses), None)
        loss_pair, unused = lax.scan(jax.checkpoint(scan_step), jnp.zeros((2,), jnp.float32), batches)
        return (jnp.sum(loss_pair) / row_total, loss_pair)
    objective, pullback, critic_loss = jax.vjp(critic_objective, critic_weights, has_aux=True)
    critic_grad, = pullback(jnp.ones_like(objective))
    new_critic, critic_one, critic_two = adamw_step(critic_weights, critic_grad, critic_first, critic_second)
    judge = new_critic[0]

    def actor_objective(weights_now):

        def scan_step(running, state_rows):
            action_out = network(weights_now, actor_layers(), state_rows, jnp.tanh)
            first_q = network(judge, critic_layers(), jnp.concatenate([state_rows, action_out], 0), unchanged)
            return (running - jnp.sum(first_q), None)
        loss_sum, unused = lax.scan(jax.checkpoint(scan_step), jnp.zeros((), jnp.float32), batches[0])
        return (loss_sum / row_total, loss_sum)
    objective, pullback, actor_loss = jax.vjp(actor_objective, actor_weights, has_aux=True)
    actor_grad, = pullback(jnp.ones_like(objective))
    new_actor, actor_one, actor_two = adamw_step(actor_weights, actor_grad, actor_first, actor_second)
    lagged_actor = polyak_mix(target_actor, new_actor)
    lagged_critic = polyak_mix(target_critic, new_critic)
    return (new_actor, actor_one, actor_two, new_critic, critic_one, critic_two, lagged_actor, lagged_critic, critic_loss, actor_loss)
```

```python
import jax
import jax.numpy as jnp
from jax import lax
from jax.experimental import pallas as pl
from jax.experimental.pallas import tpu as pltpu
from jax.sharding import PartitionSpec as P

SDIM = 17
ADIM = 6
HID = 256
STEP = 10

DISCOUNT = 0.99
POLYAK_RATE = 0.005
LEARN_RATE = 0.05
BETA_ONE = 0.9
BETA_TWO = 0.999
EPSILON = 1e-08
WEIGHT_DECAY = 0.01
NOISE_SCALE = 0.2
NOISE_CLIP = 0.5

LANES = 128
TILE = 2048
ONES_ROW = 17
ACTION_ROW = 24
IN_ROWS = 32
FLAT_ROWS = 576
HALF_ROWS = FLAT_ROWS // 2
VMEM_BYTES = 56 * 2**20

F32 = jnp.float32
BF16 = jnp.bfloat16


class Net:
    def __init__(self, in_size, out_size):
        self.in_size = in_size
        self.out_size = out_size
        self.bias1 = 2 * in_size
        self.weight2 = self.bias1 + 2
        self.bias2 = self.weight2 + 2 * HID
        self.weight3 = self.bias2 + 2
        self.rows = self.weight3 + 2 * out_size
        self.size = self.rows * LANES + out_size


ACTOR = Net(SDIM, ADIM)
CRITIC = Net(SDIM + ADIM, 1)


def dot(a, b):
    return jnp.dot(a, b, preferred_element_type=F32)


def dot_nt(a, b):
    return lax.dot_general(a, b, (((1,), (1,)), ((), ())), preferred_element_type=F32)


def wide(column, width):
    return jnp.concatenate([column] * (width // LANES), axis=1)


def iota(shape, axis):
    return lax.broadcasted_iota(jnp.int32, shape, axis)


def rows_to_lanes(block):
    return jnp.concatenate([block[row : row + 1] for row in range(block.shape[0])], axis=1)


def place_mask(net):
    shape = (IN_ROWS, LANES * net.in_size)
    position = iota(shape, 1).astype(F32)
    phase = position - net.in_size * jnp.floor((position + 0.5) * (1.0 / net.in_size))
    row = iota(shape, 0)
    source = jnp.where(row < SDIM, row, jnp.where(row >= ACTION_ROW, row - ACTION_ROW + SDIM, -1))
    source = jnp.where(source < net.in_size, source, -1)
    return phase == source.astype(F32)


def place_units(net):
    shape = (LANES * net.in_size, LANES)
    gap = iota(shape, 0) - net.in_size * iota(shape, 1)
    return jnp.where((gap >= 0) & (gap < net.in_size), 1.0, 0.0).astype(BF16)


def three_parts(value):
    high = value.astype(BF16).astype(F32)
    rest = value - high
    middle = rest.astype(BF16).astype(F32)
    return high, middle, rest - middle


def unpack_first(net, flat, mask, units):
    halves = []
    for half in range(2):
        pieces = [
            jnp.broadcast_to(
                flat[half * net.in_size + row : half * net.in_size + row + 1, :],
                (IN_ROWS, LANES),
            )
            for row in range(net.in_size)
        ]
        spread = jnp.where(mask, jnp.concatenate(pieces, axis=1), 0.0).astype(BF16)
        halves.append(dot(spread, units))
    return jnp.concatenate(halves, axis=1)


def flatten_first(net, transposed, out, mask, units):
    for half in range(2):
        block = transposed[:, half * LANES : (half + 1) * LANES]
        parts = jnp.concatenate(three_parts(block), axis=0).astype(BF16)
        spread = dot_nt(parts, units)
        spread = spread[:IN_ROWS] + (spread[IN_ROWS : 2 * IN_ROWS] + spread[2 * IN_ROWS :])
        line = jnp.sum(jnp.where(mask, spread, 0.0), axis=0, keepdims=True)
        for row in range(net.in_size):
            target = half * net.in_size + row
            out[target : target + 1, :] = line[:, row * LANES : (row + 1) * LANES]


def as_column(row):
    return jnp.transpose(jnp.broadcast_to(row, (LANES, HID)))


def flat_row(flat, start):
    return jnp.concatenate([flat[start : start + 1, :], flat[start + 1 : start + 2, :]], axis=1)


class Weights:
    shapes = (
        ((HID, IN_ROWS), BF16),
        ((HID, HID), BF16),
        ((HID, LANES), F32),
        ((16, HID), BF16),
    )
    back_shapes = (
        ((HID, HID), BF16),
        ((HID, LANES), F32),
        ((16, HID), BF16),
        ((HID, 16), BF16),
    )


def scratch_of(shapes):
    return [pltpu.VMEM(shape, dtype) for shape, dtype in shapes]


def unpack_net(net, flat, mask, units, refs, back=None):
    first, second, bias2, third = refs
    first_t = 0.5 * unpack_first(net, flat, mask, units)
    bias1 = three_parts(0.5 * flat_row(flat, net.bias1))
    row = iota((IN_ROWS, HID), 0)
    for part in range(3):
        first_t = jnp.where(row == ONES_ROW + part, bias1[part], first_t)
    first[...] = jnp.transpose(first_t).astype(BF16)
    left = flat[pl.ds(net.weight2, HID, stride=2), :]
    right = flat[pl.ds(net.weight2 + 1, HID, stride=2), :]
    second_value = 0.5 * jnp.concatenate([left, right], axis=1)
    second[...] = second_value.astype(BF16)
    bias2[...] = as_column(0.5 * flat_row(flat, net.bias2))
    left = flat[pl.ds(net.weight3, 8, stride=2), :]
    right = flat[pl.ds(net.weight3 + 1, 8, stride=2), :]
    third_value = jnp.concatenate([left, right], axis=1)
    third_value = jnp.where(iota((8, HID), 0) < net.out_size, third_value, 0.0)
    third_value = jnp.concatenate([third_value, jnp.zeros((8, HID), F32)], axis=0)
    third[...] = third_value.astype(BF16)
    if back is not None:
        second_t, third_column, action_rows, third_t = back
        second_t[...] = jnp.transpose(second_value).astype(BF16)
        third_low = 0.5 * third_value.astype(BF16).astype(F32)
        third_column[...] = as_column(third_low[0:1])
        action_rows[...] = first_t[16:32].astype(BF16)
        third_t[...] = jnp.transpose(third_low).astype(BF16)


def load_flat(net, flat, value):
    flat[0 : net.rows, :] = value.reshape(net.rows, LANES)
    flat[net.rows : FLAT_ROWS, :] = jnp.zeros((FLAT_ROWS - net.rows, LANES), F32)


def body_of(net, ref):
    return ref[pl.ds(0, net.rows * LANES)]


def tail_of(net, ref):
    return ref[pl.ds(net.rows * LANES, net.out_size)].reshape(1, net.out_size)


def tail_column(tail):
    size = tail.shape[1]
    eye = iota((8, size), 0) == iota((8, size), 1)
    return jnp.sum(jnp.where(eye, jnp.broadcast_to(tail, (8, size)), 0.0), axis=1, keepdims=True)


def start_inputs(inputs):
    inputs[...] = jnp.zeros_like(inputs)
    row = iota((8, inputs.shape[1]), 0) + 16
    inputs[16:24, :] = jnp.where((row >= ONES_ROW) & (row < ONES_ROW + 3), 1.0, 0.0)


def silu_low(half_pre):
    wave = jnp.tanh(half_pre)
    return (half_pre * wave + half_pre).astype(BF16)


def silu_and_slope(half_pre):
    wave = jnp.tanh(half_pre)
    above = 1.0 + wave
    return (half_pre * above).astype(BF16), above + half_pre * (1.0 - wave * wave)


def forward(refs, inputs):
    first, second, bias2, third = refs
    width = inputs.shape[1]
    hidden = silu_low(dot(first[...], inputs))
    hidden = silu_low(dot(second[...], hidden) + wide(bias2[...], width))
    return dot(third[...], hidden)[0:8]


def forward_kept(refs, inputs, hidden1):
    first, second, bias2, third = refs
    width = inputs.shape[1]
    low1, slope1 = silu_and_slope(dot(first[...], inputs))
    hidden1[0:HID, :] = low1
    low2, slope2 = silu_and_slope(dot(second[...], low1) + wide(bias2[...], width))
    return dot(third[...], low2)[0:8], slope1, low2, slope2


def write_gradient(net, sums, last_row, flat, mask, units):
    sum1, sum2, sum3 = sums
    flatten_first(net, sum1[...], flat, mask, units)
    bias1 = sum1[ONES_ROW : ONES_ROW + 1, :]
    bias2 = sum2[HID : HID + 1, :]
    weight2 = jnp.transpose(sum2[0:HID, :])
    for side in range(2):
        lanes = slice(side * LANES, (side + 1) * LANES)
        flat[net.bias1 + side : net.bias1 + side + 1, :] = bias1[:, lanes]
        flat[pl.ds(net.weight2 + side, HID, stride=2), :] = weight2[:, lanes]
        flat[net.bias2 + side : net.bias2 + side + 1, :] = bias2[:, lanes]
        for unit in range(net.out_size):
            row = net.weight3 + 2 * unit + side
            flat[row : row + 1, :] = sum3[unit : unit + 1, lanes]
    flat[net.rows : net.rows + 1, :] = last_row
    rest = FLAT_ROWS - net.rows - 1
    flat[net.rows + 1 : FLAT_ROWS, :] = jnp.zeros((rest, LANES), F32)


def split_halves(flat, core, keep, send):
    low = flat[0:HALF_ROWS, :]
    high = flat[HALF_ROWS:FLAT_ROWS, :]
    keep[...] = jnp.where(core == 0, low, high)
    send[...] = jnp.where(core == 0, high, low)


def join_halves(core, mine, other, flat):
    flat[0:HALF_ROWS, :] = jnp.where(core == 0, mine[...], other[...])
    flat[HALF_ROWS:FLAT_ROWS, :] = jnp.where(core == 0, other[...], mine[...])


def adamw_step(weight, gradient, moment_one, moment_two):
    moment_one = BETA_ONE * moment_one + (1.0 - BETA_ONE) * gradient
    moment_two = BETA_TWO * moment_two + (1.0 - BETA_TWO) * gradient * gradient
    corrected_one = moment_one / (1.0 - BETA_ONE**STEP)
    corrected_two = moment_two / (1.0 - BETA_TWO**STEP)
    weight = weight - LEARN_RATE * (
        corrected_one / (jnp.sqrt(corrected_two) + EPSILON) + WEIGHT_DECAY * weight
    )
    return (weight, moment_one, moment_two)


def polyak_mix(lagged, fresh):
    return POLYAK_RATE * fresh + (1.0 - POLYAK_RATE) * lagged


def clear(refs):
    for ref in refs:
        ref[...] = jnp.zeros_like(ref)


SUM_SHAPES = (((IN_ROWS, HID), F32), ((HID + 16, HID), F32), ((16, HID), F32))


def critic_tile(refs, back, bias3, inputs, target, scale, hidden1, sums, tail_sums):
    second_t, third_column = back[0], back[1]
    width = inputs.shape[1]
    out, slope1, low2, slope2 = forward_kept(refs, inputs, hidden1)
    error = out[0:1] + bias3 - target
    grad3_low = (scale * error).astype(BF16)
    grad3 = grad3_low.astype(F32)
    tail_sums[0:1, :] += grad3
    tail_sums[1:2, :] += error * error
    sums[2][...] += dot_nt(jnp.broadcast_to(grad3, (16, width)).astype(BF16), low2)
    grad2 = (wide(third_column[...], width) * grad3 * slope2).astype(BF16)
    sums[1][...] += dot_nt(hidden1[...], grad2)
    grad1 = (dot(second_t[...], grad2) * slope1).astype(BF16)
    sums[0][...] += dot_nt(inputs, grad1)


def critic_last_row(tail_sums):
    totals = jnp.sum(tail_sums[...], axis=1, keepdims=True)
    lane = iota((1, LANES), 1)
    return jnp.where(lane == 0, totals[0:1], jnp.where(lane == 1, totals[1:2], 0.0))


def target_kernel(
    row_total,
    core_ref,
    states,
    actions,
    rewards,
    next_states,
    done_flags,
    smoothing,
    target_actor,
    own_lagged,
    far_lagged,
    own_critic,
    far_critic,
    target_out,
    keep,
    send,
    inputs,
    hidden1,
    tail_sums,
    flat,
    units_actor,
    units_critic,
    *rest,
):
    actor, lag_one, lag_two, critic = rest[0:4], rest[4:8], rest[8:12], rest[12:16]
    back = rest[16:20]
    sums = rest[20:23]
    tails = rest[23]
    core = core_ref[0]
    step = pl.program_id(0)

    @pl.when(step == 0)
    def _():
        start_inputs(inputs)
        hidden1[HID : HID + 16, :] = jnp.ones((16, TILE), BF16)
        clear(sums)
        clear([tail_sums])
        units_actor[...] = place_units(ACTOR)
        units_critic[...] = place_units(CRITIC)
        mask = place_mask(ACTOR)
        load_flat(ACTOR, flat, body_of(ACTOR, target_actor))
        unpack_net(ACTOR, flat, mask, units_actor[...], actor)
        mask = place_mask(CRITIC)
        load_flat(CRITIC, flat, body_of(CRITIC, own_lagged))
        unpack_net(CRITIC, flat, mask, units_critic[...], lag_one)
        load_flat(CRITIC, flat, body_of(CRITIC, far_lagged))
        unpack_net(CRITIC, flat, mask, units_critic[...], lag_two)
        chosen = jnp.where(core == 0, body_of(CRITIC, own_critic), body_of(CRITIC, far_critic))
        load_flat(CRITIC, flat, chosen)
        unpack_net(CRITIC, flat, mask, units_critic[...], critic, back)
        tail = jnp.where(core == 0, tail_of(CRITIC, own_critic), tail_of(CRITIC, far_critic))
        tails[0:8, 0:1] = tail_column(tail_of(ACTOR, target_actor))
        tails[8:16, 0:1] = tail_column(tail_of(CRITIC, own_lagged))
        tails[16:24, 0:1] = tail_column(tail_of(CRITIC, far_lagged))
        tails[24:32, 0:1] = tail_column(tail)

    inputs[0:SDIM, :] = next_states[...]
    lagged_action = jnp.tanh(forward(actor, inputs[...].astype(BF16)) + tails[0:8, 0:1])
    jitter = jnp.clip(NOISE_SCALE * smoothing[...], -NOISE_CLIP, NOISE_CLIP)
    next_action = jnp.clip(lagged_action[0:ADIM] + jitter, -1.0, 1.0)
    inputs[ACTION_ROW : ACTION_ROW + ADIM, :] = next_action
    joined = inputs[...].astype(BF16)
    value_one = forward(lag_one, joined)[0:1] + tails[8:9, 0:1]
    value_two = forward(lag_two, joined)[0:1] + tails[16:17, 0:1]
    keep_going = 1.0 - done_flags[...].astype(F32)
    target = rewards[...] + DISCOUNT * keep_going * jnp.minimum(value_one, value_two)
    target_out[...] = target

    inputs[0:SDIM, :] = states[...]
    inputs[ACTION_ROW : ACTION_ROW + ADIM, :] = actions[...]
    joined = inputs[...].astype(BF16)
    critic_tile(
        critic, back, tails[24:25, 0:1], joined, target, 2.0 / row_total, hidden1, sums, tail_sums
    )

    @pl.when(step == pl.num_programs(0) - 1)
    def _():
        last = critic_last_row(tail_sums)
        write_gradient(CRITIC, sums, last, flat, place_mask(CRITIC), units_critic[...])
        split_halves(flat, core, keep, send)


def critic_kernel(
    row_total,
    core_ref,
    states,
    actions,
    target,
    own_critic,
    far_critic,
    keep,
    send,
    inputs,
    hidden1,
    tail_sums,
    flat,
    units_critic,
    *rest,
):
    critic, back, sums, tails = rest[0:4], rest[4:8], rest[8:11], rest[11]
    core = core_ref[0]
    step = pl.program_id(0)

    @pl.when(step == 0)
    def _():
        start_inputs(inputs)
        hidden1[HID : HID + 16, :] = jnp.ones((16, TILE), BF16)
        clear(sums)
        clear([tail_sums])
        units_critic[...] = place_units(CRITIC)
        chosen = jnp.where(core == 1, body_of(CRITIC, own_critic), body_of(CRITIC, far_critic))
        load_flat(CRITIC, flat, chosen)
        unpack_net(CRITIC, flat, place_mask(CRITIC), units_critic[...], critic, back)
        tail = jnp.where(core == 1, tail_of(CRITIC, own_critic), tail_of(CRITIC, far_critic))
        tails[0:8, 0:1] = tail_column(tail)

    inputs[0:SDIM, :] = states[...]
    inputs[ACTION_ROW : ACTION_ROW + ADIM, :] = actions[...]
    joined = inputs[...].astype(BF16)
    critic_tile(
        critic, back, tails[0:1, 0:1], joined, target[...], 2.0 / row_total, hidden1, sums, tail_sums
    )

    @pl.when(step == pl.num_programs(0) - 1)
    def _():
        last = critic_last_row(tail_sums)
        write_gradient(CRITIC, sums, last, flat, place_mask(CRITIC), units_critic[...])
        split_halves(flat, core, keep, send)


def actor_kernel(
    row_total,
    core_ref,
    states,
    actor_weights,
    mine,
    other,
    own_critic,
    far_critic,
    own_first,
    far_first,
    own_second,
    far_second,
    keep,
    send,
    inputs,
    hidden1,
    tail_sums,
    flat,
    gradient,
    units_actor,
    units_critic,
    *rest,
):
    actor, actor_back = rest[0:4], rest[4:8]
    judge, judge_back = rest[8:12], rest[12:16]
    sums, tails = rest[16:19], rest[19]
    core = core_ref[0]
    step = pl.program_id(0)

    @pl.when(step == 0)
    def _():
        start_inputs(inputs)
        hidden1[HID : HID + 16, :] = jnp.ones((16, TILE), BF16)
        clear(sums)
        clear([tail_sums])
        units_actor[...] = place_units(ACTOR)
        units_critic[...] = place_units(CRITIC)
        load_flat(ACTOR, flat, body_of(ACTOR, actor_weights))
        unpack_net(ACTOR, flat, place_mask(ACTOR), units_actor[...], actor, actor_back)
        tails[0:8, 0:1] = tail_column(tail_of(ACTOR, actor_weights))
        join_halves(core, mine, other, gradient)

        def chosen(part, own, far):
            return jnp.where(core == 0, part(CRITIC, own), part(CRITIC, far))

        def fresh(part, grad):
            return adamw_step(
                chosen(part, own_critic, far_critic),
                grad,
                chosen(part, own_first, far_first),
                chosen(part, own_second, far_second),
            )[0]

        body = gradient[0 : CRITIC.rows, :].reshape(CRITIC.rows * LANES)
        load_flat(CRITIC, flat, fresh(body_of, body))
        unpack_net(CRITIC, flat, place_mask(CRITIC), units_critic[...], judge, judge_back)
        tail = fresh(tail_of, gradient[CRITIC.rows : CRITIC.rows + 1, 0:1])
        tails[8:16, 0:1] = tail_column(tail)

    inputs[0:SDIM, :] = states[...]
    state_low = inputs[...].astype(BF16)
    out, slope1, low2, slope2 = forward_kept(actor, state_low, hidden1)
    action = jnp.tanh(out + tails[0:8, 0:1])
    inputs[ACTION_ROW:IN_ROWS, :] = action
    joined = inputs[...].astype(BF16)
    first, second, bias2, third = judge
    judge_low, judge_slope1 = silu_and_slope(dot(first[...], joined))
    judge_low, judge_slope2 = silu_and_slope(dot(second[...], judge_low) + wide(bias2[...], TILE))
    value = dot(third[...], judge_low)[0:1] + tails[8:9, 0:1]
    tail_sums[8:9, :] += value
    start = jnp.full((HID, LANES), -1.0 / row_total, F32).astype(BF16).astype(F32)
    judge_second_t, judge_column, judge_rows, unused = judge_back
    grad2 = (wide(judge_column[...] * start, TILE) * judge_slope2).astype(BF16)
    grad1 = (dot(judge_second_t[...], grad2) * judge_slope1).astype(BF16)
    grad_action = 2.0 * dot(judge_rows[...], grad1)[8:16]
    grad3 = (grad_action * (1.0 - action * action)).astype(BF16).astype(F32)
    tail_sums[0:8, :] += grad3
    grad3_low = jnp.concatenate([grad3, jnp.zeros_like(grad3)], axis=0).astype(BF16)
    actor_second_t, unused, unused, actor_third_t = actor_back
    sums[2][...] += dot_nt(grad3_low, low2)
    grad2 = (dot(actor_third_t[...], grad3_low) * slope2).astype(BF16)
    sums[1][...] += dot_nt(hidden1[...], grad2)
    grad1 = (dot(actor_second_t[...], grad2) * slope1).astype(BF16)
    sums[0][...] += dot_nt(state_low, grad1)

    @pl.when(step == pl.num_programs(0) - 1)
    def _():
        totals = jnp.sum(tail_sums[...], axis=1, keepdims=True)
        lane = iota((8, LANES), 1)
        biases = jnp.where(lane == iota((8, LANES), 0), totals[0:8], 0.0)
        last = jnp.sum(biases, axis=0, keepdims=True)
        last = jnp.where(iota((1, LANES), 1) == 8, -totals[8:9], last)
        write_gradient(ACTOR, sums, last, flat, place_mask(ACTOR), units_actor[...])
        split_halves(flat, core, keep, send)


def step_kernel(
    core_ref,
    actor_mine,
    actor_other,
    one_mine,
    one_other,
    two_mine,
    two_other,
    actor_weights,
    actor_first,
    actor_second,
    target_actor,
    critic_weights,
    critic_first,
    critic_second,
    target_critic,
    new_actor,
    new_actor_first,
    new_actor_second,
    new_target_actor,
    new_critic,
    new_critic_first,
    new_critic_second,
    new_target_critic,
    losses,
    gradient,
    second_gradient,
):
    core = core_ref[0]

    def update(net, grad_ref, sources, outs):
        for part, where, grad in (
            (body_of, pl.ds(0, net.rows * LANES), grad_ref[0 : net.rows, :]),
            (
                tail_of,
                pl.ds(net.rows * LANES, net.out_size),
                grad_ref[net.rows : net.rows + 1, 0 : net.out_size],
            ),
        ):
            weight, first, second, lagged = [part(net, source) for source in sources]
            grad = grad.reshape(weight.shape)
            fresh, first, second = adamw_step(weight, grad, first, second)
            results = (fresh, first, second, polyak_mix(lagged, fresh))
            for out, result in zip(outs, results):
                out[where] = result.reshape(result.size)

    join_halves(core, actor_mine, actor_other, gradient)
    update(
        ACTOR,
        gradient,
        (actor_weights, actor_first, actor_second, target_actor),
        (new_actor, new_actor_first, new_actor_second, new_target_actor),
    )
    lane = iota((1, LANES), 1)
    actor_row = jnp.where(lane == 8, gradient[ACTOR.rows : ACTOR.rows + 1, :], 0.0)
    actor_loss = jnp.sum(actor_row, axis=1, keepdims=True)
    join_halves(core, one_mine, one_other, gradient)
    join_halves(core, two_mine, two_other, second_gradient)
    gradient[...] = jnp.where(core == 0, gradient[...], second_gradient[...])
    update(
        CRITIC,
        gradient,
        (critic_weights, critic_first, critic_second, target_critic),
        (new_critic, new_critic_first, new_critic_second, new_target_critic),
    )
    critic_row = jnp.where(lane == 1, gradient[CRITIC.rows : CRITIC.rows + 1, :], 0.0)
    critic_loss = jnp.sum(critic_row, axis=1, keepdims=True)
    losses[...] = jnp.where(lane == 0, critic_loss, jnp.where(lane == 1, actor_loss, 0.0))


def twin_swap(value):
    return lax.ppermute(value, "twin", [(0, 1), (1, 0)])


def sum_over_chips(value):
    size = lax.axis_size("dp")
    mask = 1
    while mask < size:
        pairs = [(source, source ^ mask) for source in range(size)]
        value = value + lax.ppermute(value, "dp", pairs)
        mask *= 2
    return value


def sum_halves(keep, send):
    mine = sum_over_chips(keep + twin_swap(send))
    return mine, twin_swap(mine)


def whole(shape):
    return pl.BlockSpec(shape, lambda *unused: (0,) * len(shape))


def on_device(
    states,
    actions,
    rewards,
    next_states,
    done_flags,
    smoothing,
    actor_weights,
    actor_first,
    actor_second,
    critic_weights,
    critic_first,
    critic_second,
    target_actor,
    target_critic,
):
    core = lax.axis_index("twin").astype(jnp.int32).reshape(1)
    local_rows = states.shape[1]
    tiles = local_rows // 2 // TILE
    row_total = local_rows * lax.axis_size("dp")
    rewards = rewards.reshape(1, local_rows)
    done_flags = done_flags.reshape(1, local_rows)
    critic_weights = critic_weights.reshape(-1)
    critic_first = critic_first.reshape(-1)
    critic_second = critic_second.reshape(-1)
    target_critic = target_critic.reshape(-1)
    far_weights = twin_swap(critic_weights)
    far_lagged = twin_swap(target_critic)
    far_first = twin_swap(critic_first)
    far_second = twin_swap(critic_second)

    def mine(rows):
        return pl.BlockSpec((rows, TILE), lambda i, core_ref: (0, core_ref[0] * tiles + i))

    def local(rows):
        return pl.BlockSpec((rows, TILE), lambda i, core_ref: (0, i))

    actor_flat = whole((ACTOR.size,))
    critic_flat = whole((CRITIC.size,))
    half = whole((HALF_ROWS, LANES))
    half_shape = jax.ShapeDtypeStruct((HALF_ROWS, LANES), F32)
    common = [
        pltpu.VMEM((IN_ROWS, TILE), F32),
        pltpu.VMEM((HID + 16, TILE), BF16),
        pltpu.VMEM((16, TILE), F32),
        pltpu.VMEM((FLAT_ROWS + 8, LANES), F32),
    ]
    units_actor = pltpu.VMEM((LANES * ACTOR.in_size, LANES), BF16)
    units_critic = pltpu.VMEM((LANES * CRITIC.in_size, LANES), BF16)
    net = scratch_of(Weights.shapes)
    back = scratch_of(Weights.back_shapes)
    sums = scratch_of(SUM_SHAPES)
    tails = pltpu.VMEM((32, LANES), F32)
    params = pltpu.CompilerParams(vmem_limit_bytes=VMEM_BYTES)

    def call(kernel, in_specs, out_specs, out_shape, scratch, name):
        return pl.pallas_call(
            kernel,
            grid_spec=pltpu.PrefetchScalarGridSpec(
                num_scalar_prefetch=1,
                grid=(tiles,),
                in_specs=in_specs,
                out_specs=out_specs,
                scratch_shapes=scratch,
            ),
            out_shape=out_shape,
            compiler_params=params,
            name=name,
        )

    target, keep_one, send_one = call(
        lambda *refs: target_kernel(row_total, *refs),
        [mine(SDIM), mine(ADIM), mine(1), mine(SDIM), mine(1), mine(ADIM), actor_flat]
        + [critic_flat] * 4,
        [local(1), half, half],
        [jax.ShapeDtypeStruct((1, local_rows // 2), F32), half_shape, half_shape],
        common + [units_actor, units_critic] + net * 4 + back + sums + [tails],
        "target_and_first_critic",
    )(
        core,
        states,
        actions,
        rewards,
        next_states,
        done_flags,
        smoothing,
        target_actor,
        target_critic,
        far_lagged,
        critic_weights,
        far_weights,
    )
    keep_two, send_two = call(
        lambda *refs: critic_kernel(row_total, *refs),
        [mine(SDIM), mine(ADIM), local(1), critic_flat, critic_flat],
        [half, half],
        [half_shape, half_shape],
        common + [units_critic] + net + back + sums + [tails],
        "second_critic",
    )(core, states, actions, target, critic_weights, far_weights)
    one_mine, one_other = sum_halves(keep_one, send_one)
    keep_actor, send_actor = call(
        lambda *refs: actor_kernel(row_total, *refs),
        [mine(SDIM), actor_flat, half, half] + [critic_flat] * 6,
        [half, half],
        [half_shape, half_shape],
        common
        + [pltpu.VMEM((FLAT_ROWS, LANES), F32), units_actor, units_critic]
        + (net + back) * 2
        + sums
        + [tails],
        "actor",
    )(
        core,
        states,
        actor_weights,
        one_mine,
        one_other,
        critic_weights,
        far_weights,
        critic_first,
        far_first,
        critic_second,
        far_second,
    )
    both_mine, both_other = sum_halves(
        jnp.stack([keep_actor, keep_two]), jnp.stack([send_actor, send_two])
    )
    actor_mine, two_mine = both_mine[0], both_mine[1]
    actor_other, two_other = both_other[0], both_other[1]
    vector = pl.BlockSpec(memory_space=pltpu.VMEM)
    scalar = pl.BlockSpec(memory_space=pltpu.SMEM)
    actor_out = jax.ShapeDtypeStruct((ACTOR.size,), F32)
    critic_out = jax.ShapeDtypeStruct((CRITIC.size,), F32)
    results = pl.pallas_call(
        step_kernel,
        in_specs=[scalar] + [vector] * 14,
        out_specs=[vector] * 9,
        out_shape=[actor_out] * 4
        + [critic_out] * 4
        + [jax.ShapeDtypeStruct((1, LANES), F32)],
        scratch_shapes=[pltpu.VMEM((FLAT_ROWS, LANES), F32)] * 2,
        compiler_params=params,
        name="step",
    )(
        core,
        actor_mine,
        actor_other,
        one_mine,
        one_other,
        two_mine,
        two_other,
        actor_weights,
        actor_first,
        actor_second,
        target_actor,
        critic_weights,
        critic_first,
        critic_second,
        target_critic,
    )
    new_actor, new_actor_first, new_actor_second, new_target_actor = results[0:4]
    new_critic, new_critic_first, new_critic_second, new_target_critic = [
        result.reshape(1, -1) for result in results[4:8]
    ]
    losses = results[8]
    return (
        new_actor,
        new_actor_first,
        new_actor_second,
        new_critic,
        new_critic_first,
        new_critic_second,
        new_target_actor,
        new_target_critic,
        losses[0, 0:1],
        losses[0, 1],
    )


def solution(mesh):
    columns = P(None, "dp")
    critic = P("twin", None)
    return jax.shard_map(
        on_device,
        mesh=mesh,
        in_specs=(
            columns,
            columns,
            P("dp"),
            columns,
            P("dp"),
            columns,
            P(),
            P(),
            P(),
            critic,
            critic,
            critic,
            P(),
            critic,
        ),
        out_specs=(P(), P(), P(), critic, critic, critic, P(), critic, P("twin"), P()),
        check_vma=False,
    )
```

```python
import jax
import jax.numpy as jnp
from jax import lax
from jax.experimental import pallas as pl
from jax.experimental.pallas import tpu as pltpu
from jax.sharding import PartitionSpec as P

SDIM = 17
ADIM = 6
HID = 256
STEP = 10

DISCOUNT = 0.99
POLYAK_RATE = 0.005
LEARN_RATE = 0.05
BETA_ONE = 0.9
BETA_TWO = 0.999
EPSILON = 1e-08
WEIGHT_DECAY = 0.01
NOISE_SCALE = 0.2
NOISE_CLIP = 0.5

LANES = 128
TILE = 2048
ONES_ROW = 17
ACTION_ROW = 24
IN_ROWS = 32
FLAT_ROWS = 576
HALF_ROWS = FLAT_ROWS // 2
VMEM_BYTES = 24 * 2**20

F32 = jnp.float32
BF16 = jnp.bfloat16


class Net:
    def __init__(self, in_size, out_size):
        self.in_size = in_size
        self.out_size = out_size
        self.bias1 = 2 * in_size
        self.weight2 = self.bias1 + 2
        self.bias2 = self.weight2 + 2 * HID
        self.weight3 = self.bias2 + 2
        self.rows = self.weight3 + 2 * out_size
        self.size = self.rows * LANES + out_size


ACTOR = Net(SDIM, ADIM)
CRITIC = Net(SDIM + ADIM, 1)


def dot(a, b):
    return jnp.dot(a, b, preferred_element_type=F32)


def dot_nt(a, b):
    return lax.dot_general(a, b, (((1,), (1,)), ((), ())), preferred_element_type=F32)


def wide(column, width):
    return jnp.concatenate([column] * (width // LANES), axis=1)


def iota(shape, axis):
    return lax.broadcasted_iota(jnp.int32, shape, axis)


def rows_to_lanes(block):
    return jnp.concatenate([block[row : row + 1] for row in range(block.shape[0])], axis=1)


def place_mask(net):
    shape = (IN_ROWS, LANES * net.in_size)
    position = iota(shape, 1).astype(F32)
    phase = position - net.in_size * jnp.floor((position + 0.5) * (1.0 / net.in_size))
    row = iota(shape, 0)
    source = jnp.where(row < SDIM, row, jnp.where(row >= ACTION_ROW, row - ACTION_ROW + SDIM, -1))
    source = jnp.where(source < net.in_size, source, -1)
    return phase == source.astype(F32)


def place_units(net):
    shape = (LANES * net.in_size, LANES)
    gap = iota(shape, 0) - net.in_size * iota(shape, 1)
    return jnp.where((gap >= 0) & (gap < net.in_size), 1.0, 0.0).astype(BF16)


def three_parts(value):
    high = value.astype(BF16).astype(F32)
    rest = value - high
    middle = rest.astype(BF16).astype(F32)
    return high, middle, rest - middle


def unpack_first(net, flat, mask, units):
    halves = []
    for half in range(2):
        pieces = [
            jnp.broadcast_to(
                flat[half * net.in_size + row : half * net.in_size + row + 1, :],
                (IN_ROWS, LANES),
            )
            for row in range(net.in_size)
        ]
        spread = jnp.where(mask, jnp.concatenate(pieces, axis=1), 0.0).astype(BF16)
        halves.append(dot(spread, units))
    return jnp.concatenate(halves, axis=1)


def flatten_first(net, transposed, out, mask, units):
    for half in range(2):
        block = transposed[:, half * LANES : (half + 1) * LANES]
        parts = jnp.concatenate(three_parts(block), axis=0).astype(BF16)
        spread = dot_nt(parts, units)
        spread = spread[:IN_ROWS] + (spread[IN_ROWS : 2 * IN_ROWS] + spread[2 * IN_ROWS :])
        line = jnp.sum(jnp.where(mask, spread, 0.0), axis=0, keepdims=True)
        for row in range(net.in_size):
            target = half * net.in_size + row
            out[target : target + 1, :] = line[:, row * LANES : (row + 1) * LANES]


def as_column(row):
    return jnp.transpose(jnp.broadcast_to(row, (LANES, HID)))


def flat_row(flat, start):
    return jnp.concatenate([flat[start : start + 1, :], flat[start + 1 : start + 2, :]], axis=1)


class Weights:
    shapes = (
        ((HID, IN_ROWS), BF16),
        ((HID, HID), BF16),
        ((HID, LANES), F32),
        ((16, HID), BF16),
    )
    back_shapes = (
        ((HID, HID), BF16),
        ((HID, LANES), F32),
        ((16, HID), BF16),
        ((HID, 16), BF16),
    )


def scratch_of(shapes):
    return [pltpu.VMEM(shape, dtype) for shape, dtype in shapes]


def unpack_net(net, flat, mask, units, refs, back=None):
    first, second, bias2, third = refs
    first_t = 0.5 * unpack_first(net, flat, mask, units)
    bias1 = three_parts(0.5 * flat_row(flat, net.bias1))
    row = iota((IN_ROWS, HID), 0)
    for part in range(3):
        first_t = jnp.where(row == ONES_ROW + part, bias1[part], first_t)
    first[...] = jnp.transpose(first_t).astype(BF16)
    left = flat[pl.ds(net.weight2, HID, stride=2), :]
    right = flat[pl.ds(net.weight2 + 1, HID, stride=2), :]
    second_value = 0.5 * jnp.concatenate([left, right], axis=1)
    second[...] = second_value.astype(BF16)
    bias2[...] = as_column(0.5 * flat_row(flat, net.bias2))
    left = flat[pl.ds(net.weight3, 8, stride=2), :]
    right = flat[pl.ds(net.weight3 + 1, 8, stride=2), :]
    third_value = jnp.concatenate([left, right], axis=1)
    third_value = jnp.where(iota((8, HID), 0) < net.out_size, third_value, 0.0)
    third_value = jnp.concatenate([third_value, jnp.zeros((8, HID), F32)], axis=0)
    third[...] = third_value.astype(BF16)
    if back is not None:
        second_t, third_column, action_rows, third_t = back
        second_t[...] = jnp.transpose(second_value).astype(BF16)
        third_low = 0.5 * third_value.astype(BF16).astype(F32)
        if third_column is not None:
            third_column[...] = as_column(third_low[0:1])
        if action_rows is not None:
            action_rows[...] = first_t[16:32].astype(BF16)
        if third_t is not None:
            third_t[...] = jnp.transpose(third_low).astype(BF16)


def load_flat(net, flat, value):
    flat[0 : net.rows, :] = value
    flat[net.rows : FLAT_ROWS, :] = jnp.zeros((FLAT_ROWS - net.rows, LANES), F32)


def span_of(net, ref, tail):
    where = pl.ds(net.rows * LANES, net.out_size) if tail else pl.ds(0, net.rows * LANES)
    return (where,) if len(ref.shape) == 1 else (slice(0, 1), where)


def body_of(net, ref):
    return ref[span_of(net, ref, False)].reshape(net.rows, LANES)


def tail_of(net, ref):
    return ref[span_of(net, ref, True)].reshape(1, net.out_size)


def tail_column(tail):
    size = tail.shape[1]
    eye = iota((8, size), 0) == iota((8, size), 1)
    return jnp.sum(jnp.where(eye, jnp.broadcast_to(tail, (8, size)), 0.0), axis=1, keepdims=True)


def start_inputs(inputs):
    inputs[...] = jnp.zeros_like(inputs)
    row = iota((8, inputs.shape[1]), 0) + 16
    inputs[16:24, :] = jnp.where((row >= ONES_ROW) & (row < ONES_ROW + 3), 1.0, 0.0)


def silu_low(half_pre):
    wave = jnp.tanh(half_pre)
    return (half_pre * wave + half_pre).astype(BF16)


def silu_and_slope(half_pre):
    wave = jnp.tanh(half_pre)
    above = 1.0 + wave
    return (half_pre * above).astype(BF16), above + half_pre * (1.0 - wave * wave)


def forward(refs, inputs):
    first, second, bias2, third = refs
    width = inputs.shape[1]
    hidden = silu_low(dot(first[...], inputs))
    hidden = silu_low(dot(second[...], hidden) + wide(bias2[...], width))
    return dot(third[...], hidden)[0:8]


def forward_kept(refs, inputs, hidden1):
    first, second, bias2, third = refs
    width = inputs.shape[1]
    low1, slope1 = silu_and_slope(dot(first[...], inputs))
    hidden1[0:HID, :] = low1
    low2, slope2 = silu_and_slope(dot(second[...], low1) + wide(bias2[...], width))
    return dot(third[...], low2)[0:8], slope1, low2, slope2


def write_gradient(net, sums, last_row, flat, mask, units):
    sum1, sum2, sum3 = sums
    flatten_first(net, sum1[...], flat, mask, units)
    bias1 = sum1[ONES_ROW : ONES_ROW + 1, :]
    bias2 = sum2[HID : HID + 1, :]
    weight2 = jnp.transpose(sum2[0:HID, :])
    for side in range(2):
        lanes = slice(side * LANES, (side + 1) * LANES)
        flat[net.bias1 + side : net.bias1 + side + 1, :] = bias1[:, lanes]
        flat[pl.ds(net.weight2 + side, HID, stride=2), :] = weight2[:, lanes]
        flat[net.bias2 + side : net.bias2 + side + 1, :] = bias2[:, lanes]
        for unit in range(net.out_size):
            row = net.weight3 + 2 * unit + side
            flat[row : row + 1, :] = sum3[unit : unit + 1, lanes]
    flat[net.rows : net.rows + 1, :] = last_row
    rest = FLAT_ROWS - net.rows - 1
    flat[net.rows + 1 : FLAT_ROWS, :] = jnp.zeros((rest, LANES), F32)


def split_halves(flat, core, keep, send):
    low = flat[0:HALF_ROWS, :]
    high = flat[HALF_ROWS:FLAT_ROWS, :]
    keep[...] = jnp.where(core == 0, low, high)
    send[...] = jnp.where(core == 0, high, low)


def join_halves(core, mine, other, flat):
    flat[0:HALF_ROWS, :] = jnp.where(core == 0, mine[...], other[...])
    flat[HALF_ROWS:FLAT_ROWS, :] = jnp.where(core == 0, other[...], mine[...])


def adamw_step(weight, gradient, moment_one, moment_two):
    moment_one = BETA_ONE * moment_one + (1.0 - BETA_ONE) * gradient
    moment_two = BETA_TWO * moment_two + (1.0 - BETA_TWO) * gradient * gradient
    corrected_one = moment_one / (1.0 - BETA_ONE**STEP)
    corrected_two = moment_two / (1.0 - BETA_TWO**STEP)
    weight = weight - LEARN_RATE * (
        corrected_one / (jnp.sqrt(corrected_two) + EPSILON) + WEIGHT_DECAY * weight
    )
    return (weight, moment_one, moment_two)


def polyak_mix(lagged, fresh):
    return POLYAK_RATE * fresh + (1.0 - POLYAK_RATE) * lagged


def clear(refs):
    for ref in refs:
        ref[...] = jnp.zeros_like(ref)


SUM_SHAPES = (((IN_ROWS, HID), F32), ((HID + 16, HID), F32), ((16, HID), F32))


def critic_tile(refs, back, bias3, inputs, target, scale, hidden1, sums, tail_sums):
    second_t, third_column = back[0], back[1]
    width = inputs.shape[1]
    out, slope1, low2, slope2 = forward_kept(refs, inputs, hidden1)
    error = out[0:1] + bias3 - target
    grad3_low = (scale * error).astype(BF16)
    grad3 = grad3_low.astype(F32)
    tail_sums[0:1, :] += grad3
    tail_sums[1:2, :] += error * error
    sums[2][...] += dot_nt(jnp.broadcast_to(grad3, (16, width)).astype(BF16), low2)
    grad2 = (wide(third_column[...], width) * grad3 * slope2).astype(BF16)
    sums[1][...] += dot_nt(hidden1[...], grad2)
    grad1 = (dot(second_t[...], grad2) * slope1).astype(BF16)
    sums[0][...] += dot_nt(inputs, grad1)


def critic_last_row(tail_sums):
    totals = jnp.sum(tail_sums[...], axis=1, keepdims=True)
    lane = iota((1, LANES), 1)
    return jnp.where(lane == 0, totals[0:1], jnp.where(lane == 1, totals[1:2], 0.0))


def target_kernel(
    row_total,
    core_ref,
    states,
    actions,
    rewards,
    next_states,
    done_flags,
    smoothing,
    target_actor,
    own_lagged,
    far_lagged,
    own_critic,
    far_critic,
    target_out,
    keep,
    send,
    *rest,
):
    next_critic, next_second_t, next_column, next_tail = rest[0:4], rest[4], rest[5], rest[6]
    inputs, hidden1, tail_sums, flat, units_actor, units_critic = rest[7:13]
    actor, lag_one, lag_two, critic = rest[13:17], rest[17:21], rest[21:25], rest[25:29]
    back = (rest[29], rest[30], None, None)
    sums = rest[31:34]
    tails = rest[34]
    core = core_ref[0]
    step = pl.program_id(0)

    @pl.when(step == 0)
    def _():
        start_inputs(inputs)
        hidden1[HID : HID + 16, :] = jnp.ones((16, TILE), BF16)
        clear(sums)
        clear([tail_sums])
        units_actor[...] = place_units(ACTOR)
        units_critic[...] = place_units(CRITIC)
        mask = place_mask(ACTOR)
        load_flat(ACTOR, flat, body_of(ACTOR, target_actor))
        unpack_net(ACTOR, flat, mask, units_actor[...], actor)
        mask = place_mask(CRITIC)
        load_flat(CRITIC, flat, body_of(CRITIC, own_lagged))
        unpack_net(CRITIC, flat, mask, units_critic[...], lag_one)
        load_flat(CRITIC, flat, body_of(CRITIC, far_lagged))
        unpack_net(CRITIC, flat, mask, units_critic[...], lag_two)
        chosen = jnp.where(core == 0, body_of(CRITIC, own_critic), body_of(CRITIC, far_critic))
        load_flat(CRITIC, flat, chosen)
        unpack_net(CRITIC, flat, mask, units_critic[...], critic, back)
        tail = jnp.where(core == 0, tail_of(CRITIC, own_critic), tail_of(CRITIC, far_critic))
        tails[0:8, 0:1] = tail_column(tail_of(ACTOR, target_actor))
        tails[8:16, 0:1] = tail_column(tail_of(CRITIC, own_lagged))
        tails[16:24, 0:1] = tail_column(tail_of(CRITIC, far_lagged))
        tails[24:32, 0:1] = tail_column(tail)
        chosen = jnp.where(core == 1, body_of(CRITIC, own_critic), body_of(CRITIC, far_critic))
        load_flat(CRITIC, flat, chosen)
        next_back = (next_second_t, next_column, None, None)
        unpack_net(CRITIC, flat, mask, units_critic[...], next_critic, next_back)
        tail = jnp.where(core == 1, tail_of(CRITIC, own_critic), tail_of(CRITIC, far_critic))
        next_tail[...] = jnp.broadcast_to(tail_column(tail), (8, LANES))

    inputs[0:SDIM, :] = next_states[...]
    lagged_action = jnp.tanh(forward(actor, inputs[...].astype(BF16)) + tails[0:8, 0:1])
    jitter = jnp.clip(NOISE_SCALE * smoothing[...], -NOISE_CLIP, NOISE_CLIP)
    next_action = jnp.clip(lagged_action[0:ADIM] + jitter, -1.0, 1.0)
    inputs[ACTION_ROW : ACTION_ROW + ADIM, :] = next_action
    joined = inputs[...].astype(BF16)
    value_one = forward(lag_one, joined)[0:1] + tails[8:9, 0:1]
    value_two = forward(lag_two, joined)[0:1] + tails[16:17, 0:1]
    keep_going = 1.0 - done_flags[...].astype(F32)
    target = rewards[...] + DISCOUNT * keep_going * jnp.minimum(value_one, value_two)
    target_out[...] = target

    inputs[0:SDIM, :] = states[...]
    inputs[ACTION_ROW : ACTION_ROW + ADIM, :] = actions[...]
    joined = inputs[...].astype(BF16)
    critic_tile(
        critic, back, tails[24:25, 0:1], joined, target, 2.0 / row_total, hidden1, sums, tail_sums
    )

    @pl.when(step == pl.num_programs(0) - 1)
    def _():
        last = critic_last_row(tail_sums)
        write_gradient(CRITIC, sums, last, flat, place_mask(CRITIC), units_critic[...])
        split_halves(flat, core, keep, send)


def critic_kernel(row_total, is_first, is_last, core_ref, *refs):
    states, actions, target = refs[0:3]
    critic, second_t, third_column, tail = refs[3:7], refs[7], refs[8], refs[9]
    refs = refs[10:]
    before = () if is_first else refs[0:4]
    refs = refs[len(before) :]
    if is_last:
        keep, send, inputs, hidden1 = refs[0:4]
        sums, tail_sums, flat, units = refs[4:7], refs[7], refs[8], refs[9]
    else:
        sums, tail_sums, inputs, hidden1 = refs[0:3], refs[3], refs[4], refs[5]
    start_inputs(inputs)
    hidden1[HID : HID + 16, :] = jnp.ones((16, TILE), BF16)
    if is_first:
        clear([*sums, tail_sums])
    for after, value in zip([*sums, tail_sums], before):
        after[...] = value[...]
    inputs[0:SDIM, :] = states[...]
    inputs[ACTION_ROW : ACTION_ROW + ADIM, :] = actions[...]
    joined = inputs[...].astype(BF16)
    critic_tile(
        critic,
        (second_t, third_column),
        tail[0:1, 0:1],
        joined,
        target[...],
        2.0 / row_total,
        hidden1,
        sums,
        tail_sums,
    )
    if is_last:
        units[...] = place_units(CRITIC)
        last = critic_last_row(tail_sums)
        write_gradient(CRITIC, sums, last, flat, place_mask(CRITIC), units[...])
        split_halves(flat, core_ref[0], keep, send)


def actor_kernel(
    row_total,
    core_ref,
    states,
    actor_weights,
    mine,
    other,
    own_critic,
    far_critic,
    own_first,
    far_first,
    own_second,
    far_second,
    keep,
    send,
    inputs,
    hidden1,
    tail_sums,
    flat,
    gradient,
    units_actor,
    units_critic,
    *rest,
):
    actor, actor_back = rest[0:4], rest[4:8]
    judge, judge_back = rest[8:12], rest[12:16]
    sums, tails = rest[16:19], rest[19]
    core = core_ref[0]
    step = pl.program_id(0)

    @pl.when(step == 0)
    def _():
        start_inputs(inputs)
        hidden1[HID : HID + 16, :] = jnp.ones((16, TILE), BF16)
        clear(sums)
        clear([tail_sums])
        units_actor[...] = place_units(ACTOR)
        units_critic[...] = place_units(CRITIC)
        load_flat(ACTOR, flat, body_of(ACTOR, actor_weights))
        unpack_net(ACTOR, flat, place_mask(ACTOR), units_actor[...], actor, actor_back)
        tails[0:8, 0:1] = tail_column(tail_of(ACTOR, actor_weights))
        join_halves(core, mine, other, gradient)

        def chosen(part, own, far):
            return jnp.where(core == 0, part(CRITIC, own), part(CRITIC, far))

        def fresh(part, grad):
            return adamw_step(
                chosen(part, own_critic, far_critic),
                grad,
                chosen(part, own_first, far_first),
                chosen(part, own_second, far_second),
            )[0]

        load_flat(CRITIC, flat, fresh(body_of, gradient[0 : CRITIC.rows, :]))
        unpack_net(CRITIC, flat, place_mask(CRITIC), units_critic[...], judge, judge_back)
        tail = fresh(tail_of, gradient[CRITIC.rows : CRITIC.rows + 1, 0:1])
        tails[8:16, 0:1] = tail_column(tail)

    inputs[0:SDIM, :] = states[...]
    state_low = inputs[...].astype(BF16)
    out, slope1, low2, slope2 = forward_kept(actor, state_low, hidden1)
    action = jnp.tanh(out + tails[0:8, 0:1])
    inputs[ACTION_ROW:IN_ROWS, :] = action
    joined = inputs[...].astype(BF16)
    first, second, bias2, third = judge
    judge_low, judge_slope1 = silu_and_slope(dot(first[...], joined))
    judge_low, judge_slope2 = silu_and_slope(dot(second[...], judge_low) + wide(bias2[...], TILE))
    value = dot(third[...], judge_low)[0:1] + tails[8:9, 0:1]
    tail_sums[8:9, :] += value
    start = jnp.full((HID, LANES), -1.0 / row_total, F32).astype(BF16).astype(F32)
    judge_second_t, judge_column, judge_rows, unused = judge_back
    grad2 = (wide(judge_column[...] * start, TILE) * judge_slope2).astype(BF16)
    grad1 = (dot(judge_second_t[...], grad2) * judge_slope1).astype(BF16)
    grad_action = 2.0 * dot(judge_rows[...], grad1)[8:16]
    grad3 = (grad_action * (1.0 - action * action)).astype(BF16).astype(F32)
    tail_sums[0:8, :] += grad3
    grad3_low = jnp.concatenate([grad3, jnp.zeros_like(grad3)], axis=0).astype(BF16)
    actor_second_t, unused, unused, actor_third_t = actor_back
    sums[2][...] += dot_nt(grad3_low, low2)
    grad2 = (dot(actor_third_t[...], grad3_low) * slope2).astype(BF16)
    sums[1][...] += dot_nt(hidden1[...], grad2)
    grad1 = (dot(actor_second_t[...], grad2) * slope1).astype(BF16)
    sums[0][...] += dot_nt(state_low, grad1)

    @pl.when(step == pl.num_programs(0) - 1)
    def _():
        totals = jnp.sum(tail_sums[...], axis=1, keepdims=True)
        lane = iota((8, LANES), 1)
        biases = jnp.where(lane == iota((8, LANES), 0), totals[0:8], 0.0)
        last = jnp.sum(biases, axis=0, keepdims=True)
        last = jnp.where(iota((1, LANES), 1) == 8, -totals[8:9], last)
        write_gradient(ACTOR, sums, last, flat, place_mask(ACTOR), units_actor[...])
        split_halves(flat, core, keep, send)


def step_kernel(
    core_ref,
    actor_mine,
    actor_other,
    one_mine,
    one_other,
    two_mine,
    two_other,
    actor_weights,
    actor_first,
    actor_second,
    target_actor,
    critic_weights,
    critic_first,
    critic_second,
    target_critic,
    new_actor,
    new_actor_first,
    new_actor_second,
    new_target_actor,
    new_critic,
    new_critic_first,
    new_critic_second,
    new_target_critic,
    critic_loss,
    actor_loss,
    gradient,
    second_gradient,
):
    core = core_ref[0]

    def update(net, grad_ref, sources, outs):
        for part, tail, grad in (
            (body_of, False, grad_ref[0 : net.rows, :]),
            (tail_of, True, grad_ref[net.rows : net.rows + 1, 0 : net.out_size]),
        ):
            weight, first, second, lagged = [part(net, source) for source in sources]
            fresh, first, second = adamw_step(weight, grad, first, second)
            results = (fresh, first, second, polyak_mix(lagged, fresh))
            for out, result in zip(outs, results):
                shape = (1, result.size) if len(out.shape) == 2 else (result.size,)
                out[span_of(net, out, tail)] = result.reshape(shape)

    join_halves(core, actor_mine, actor_other, gradient)
    update(
        ACTOR,
        gradient,
        (actor_weights, actor_first, actor_second, target_actor),
        (new_actor, new_actor_first, new_actor_second, new_target_actor),
    )
    lane = iota((1, LANES), 1)
    actor_row = jnp.where(lane == 8, gradient[ACTOR.rows : ACTOR.rows + 1, :], 0.0)
    actor_loss[0] = jnp.sum(actor_row)
    join_halves(core, one_mine, one_other, gradient)
    join_halves(core, two_mine, two_other, second_gradient)
    gradient[...] = jnp.where(core == 0, gradient[...], second_gradient[...])
    update(
        CRITIC,
        gradient,
        (critic_weights, critic_first, critic_second, target_critic),
        (new_critic, new_critic_first, new_critic_second, new_target_critic),
    )
    critic_row = jnp.where(lane == 1, gradient[CRITIC.rows : CRITIC.rows + 1, :], 0.0)
    critic_loss[0] = jnp.sum(critic_row)


def twin_swap(value):
    return lax.ppermute(value, "twin", [(0, 1), (1, 0)])


def to_second(value):
    return lax.ppermute(value, "twin", [(0, 1)])


def chip_masks():
    return [1 << bit for bit in range((lax.axis_size("dp") - 1).bit_length())]


def partner(value, mask):
    pairs = [(source, source ^ mask) for source in range(lax.axis_size("dp"))]
    return lax.ppermute(value, "dp", pairs)


def in_hbm(value):
    return pltpu.with_memory_space_constraint(value, pltpu.HBM)


def whole(shape):
    return pl.BlockSpec(shape, lambda *unused: (0,) * len(shape))


def on_device(
    states,
    actions,
    rewards,
    next_states,
    done_flags,
    smoothing,
    actor_weights,
    actor_first,
    actor_second,
    critic_weights,
    critic_first,
    critic_second,
    target_actor,
    target_critic,
):
    core = lax.axis_index("twin").astype(jnp.int32).reshape(1)
    local_rows = states.shape[1]
    tiles = local_rows // 2 // TILE
    row_total = local_rows * lax.axis_size("dp")
    rewards = rewards.reshape(1, local_rows)
    done_flags = done_flags.reshape(1, local_rows)
    far_lagged = twin_swap(target_critic)
    far_weights = twin_swap(critic_weights)
    far_first = twin_swap(critic_first)
    far_second = twin_swap(critic_second)
    far_lagged, far_weights, far_first, far_second = lax.optimization_barrier(
        (far_lagged, far_weights, far_first, far_second)
    )

    def mine(rows, tile=None):
        if tile is None:
            return pl.BlockSpec((rows, TILE), lambda i, core_ref: (0, core_ref[0] * tiles + i))
        return pl.BlockSpec((rows, TILE), lambda i, core_ref: (0, core_ref[0] * tiles + tile))

    def local(rows, tile=None):
        return pl.BlockSpec((rows, TILE), lambda i, core_ref: (0, i if tile is None else tile))

    actor_flat = whole((ACTOR.size,))
    critic_flat = whole((1, CRITIC.size))
    half = whole((HALF_ROWS, LANES))
    half_shape = jax.ShapeDtypeStruct((HALF_ROWS, LANES), F32)
    inputs = pltpu.VMEM((IN_ROWS, TILE), F32)
    hidden1 = pltpu.VMEM((HID + 16, TILE), BF16)
    tail_shapes = (((16, TILE), F32),)
    flat = pltpu.VMEM((FLAT_ROWS + 8, LANES), F32)
    common = [inputs, hidden1] + scratch_of(tail_shapes) + [flat]
    units_actor = pltpu.VMEM((LANES * ACTOR.in_size, LANES), BF16)
    units_critic = pltpu.VMEM((LANES * CRITIC.in_size, LANES), BF16)
    net = scratch_of(Weights.shapes)
    back = scratch_of(Weights.back_shapes)
    sums = scratch_of(SUM_SHAPES)
    tails = pltpu.VMEM((32, LANES), F32)
    params = pltpu.CompilerParams(vmem_limit_bytes=VMEM_BYTES)

    def call(
        kernel, steps, in_specs, out_specs, out_shape, scratch, name, flops, aliases=(), vmem=VMEM_BYTES
    ):
        return pl.pallas_call(
            kernel,
            grid_spec=pltpu.PrefetchScalarGridSpec(
                num_scalar_prefetch=1,
                grid=(steps,),
                in_specs=in_specs,
                out_specs=out_specs,
                scratch_shapes=scratch,
            ),
            out_shape=out_shape,
            input_output_aliases=dict(aliases),
            compiler_params=pltpu.CompilerParams(vmem_limit_bytes=vmem),
            cost_estimate=pl.CostEstimate(flops=flops, bytes_accessed=10**6, transcendentals=0),
            name=name,
        )

    unit_flops = 2 * HID * HID * TILE
    passed = Weights.shapes + Weights.back_shapes[0:2] + (((8, LANES), F32),)
    passed_specs = [whole(shape) for shape, dtype in passed]
    passed_shapes = [jax.ShapeDtypeStruct(shape, dtype) for shape, dtype in passed]
    target, keep_one, send_one, *critic_two = call(
        lambda *refs: target_kernel(row_total, *refs),
        tiles,
        [mine(SDIM), mine(ADIM), mine(1), mine(SDIM), mine(1), mine(ADIM), actor_flat]
        + [critic_flat] * 4,
        [local(1), half, half] + passed_specs,
        [jax.ShapeDtypeStruct((1, local_rows // 2), F32), half_shape, half_shape] + passed_shapes,
        common + [units_actor, units_critic] + net * 4 + back[0:2] + sums + [tails],
        "target_and_first_critic",
        16 * tiles * unit_flops,
    )(
        core,
        in_hbm(states),
        in_hbm(actions),
        in_hbm(rewards),
        in_hbm(next_states),
        in_hbm(done_flags),
        in_hbm(smoothing),
        target_actor,
        target_critic,
        far_lagged,
        critic_weights,
        far_weights,
    )

    carried = SUM_SHAPES + tail_shapes
    carried_specs = [whole(shape) for shape, dtype in carried]
    carried_shapes = [jax.ShapeDtypeStruct(shape, dtype) for shape, dtype in carried]

    def second_critic(tile, tied_target, state):
        is_first, is_last = tile == 0, tile == tiles - 1
        in_specs = [mine(SDIM, tile), mine(ADIM, tile), local(1, tile)] + passed_specs
        scratch = [inputs, hidden1]
        out_specs, out_shape = carried_specs, carried_shapes
        aliases = []
        if not is_first:
            aliases = [(1 + len(in_specs) + i, i) for i in range(len(carried))]
            in_specs = in_specs + carried_specs
        if is_last:
            out_specs, out_shape, aliases = [half, half], [half_shape, half_shape], []
            scratch = scratch + sums + scratch_of(tail_shapes) + [flat, units_critic]
        return call(
            lambda *refs: critic_kernel(row_total, is_first, is_last, *refs),
            1,
            in_specs,
            out_specs,
            out_shape,
            scratch,
            "second_critic",
            8 * unit_flops,
            aliases,
        )(core, states, actions, tied_target, *critic_two, *state)

    masks = chip_masks()
    state = ()
    one = keep_one + twin_swap(send_one)
    tile = 0
    for mask in masks:
        moved = partner(one, mask)
        if tile < tiles:
            one, tied_target = lax.optimization_barrier((one, target))
            state = second_critic(tile, tied_target, state)
            tile += 1
        one = one + moved
        one, state = lax.optimization_barrier((one, state))
    while tile < tiles:
        state = second_critic(tile, target, state)
        tile += 1
    keep_two, send_two = state
    one_other = twin_swap(one)
    two = keep_two + twin_swap(send_two)
    two_moved = partner(two, masks[-1])
    two, one, one_other = lax.optimization_barrier((two, one, one_other))
    keep_actor, send_actor = call(
        lambda *refs: actor_kernel(row_total, *refs),
        tiles,
        [mine(SDIM), actor_flat, half, half] + [critic_flat] * 6,
        [half, half],
        [half_shape, half_shape],
        common
        + [pltpu.VMEM((FLAT_ROWS, LANES), F32), units_actor, units_critic]
        + (net + back) * 2
        + sums
        + [tails],
        "actor",
        10 * tiles * unit_flops,
    )(
        core,
        states,
        actor_weights,
        one,
        one_other,
        critic_weights,
        far_weights,
        critic_first,
        far_first,
        critic_second,
        far_second,
    )
    actor_moved = twin_swap(send_actor)
    two = two + two_moved
    two, keep_actor, actor_moved = lax.optimization_barrier((two, keep_actor, actor_moved))
    actor = keep_actor + actor_moved
    for mask, other_mask in zip(masks, masks[-2:-1] + masks[:-2] + [None]):
        moved = partner(actor, mask)
        if other_mask is not None:
            two = two + partner(two, other_mask)
        actor = actor + moved
    actor_other = twin_swap(actor)
    two_other = to_second(two)
    vector = pl.BlockSpec(memory_space=pltpu.VMEM)
    scalar = pl.BlockSpec(memory_space=pltpu.SMEM)
    actor_out = jax.ShapeDtypeStruct((ACTOR.size,), F32)
    critic_out = jax.ShapeDtypeStruct((1, CRITIC.size), F32)
    loss_out = jax.ShapeDtypeStruct((1,), F32)
    (
        new_actor,
        new_actor_first,
        new_actor_second,
        new_target_actor,
        new_critic,
        new_critic_first,
        new_critic_second,
        new_target_critic,
        critic_loss,
        actor_loss,
    ) = pl.pallas_call(
        step_kernel,
        in_specs=[scalar] + [vector] * 14,
        out_specs=[vector] * 8 + [scalar] * 2,
        out_shape=[actor_out] * 4 + [critic_out] * 4 + [loss_out] * 2,
        scratch_shapes=[pltpu.VMEM((FLAT_ROWS, LANES), F32)] * 2,
        compiler_params=params,
        name="step",
    )(
        core,
        actor,
        actor_other,
        one,
        one_other,
        two,
        two_other,
        actor_weights,
        actor_first,
        actor_second,
        target_actor,
        critic_weights,
        critic_first,
        critic_second,
        target_critic,
    )
    return (
        new_actor,
        new_actor_first,
        new_actor_second,
        new_critic,
        new_critic_first,
        new_critic_second,
        new_target_actor,
        new_target_critic,
        critic_loss,
        actor_loss.reshape(()),
    )


def solution(mesh):
    columns = P(None, "dp")
    critic = P("twin", None)
    return jax.shard_map(
        on_device,
        mesh=mesh,
        in_specs=(
            columns,
            columns,
            P("dp"),
            columns,
            P("dp"),
            columns,
            P(),
            P(),
            P(),
            critic,
            critic,
            critic,
            P(),
            critic,
        ),
        out_specs=(P(), P(), P(), critic, critic, critic, P(), critic, P("twin"), P()),
        check_vma=False,
    )
```

```python
import jax
import jax.numpy as jnp
from jax import lax
from jax.experimental import pallas as pl
from jax.experimental.pallas import tpu as pltpu
from jax.sharding import PartitionSpec as P

SDIM = 17
ADIM = 6
HID = 256
STEP = 10

DISCOUNT = 0.99
POLYAK_RATE = 0.005
LEARN_RATE = 0.05
BETA_ONE = 0.9
BETA_TWO = 0.999
EPSILON = 1e-08
WEIGHT_DECAY = 0.01
NOISE_SCALE = 0.2
NOISE_CLIP = 0.5

LANES = 128
TILE = 2048
ACTION_PART = 2048
LAG = 1
TARGET_TILE = 2048
TARGET_PART = 2048
TARGET_LAG = 1
CRITIC_PART = 1024
CRITIC_LAG = 3
ACTOR_TILE = 2048
ACTOR_PART = 1024
ACTOR_LAG = 3
ONES_ROW = 17
ACTION_ROW = 24
IN_ROWS = 32
FLAT_ROWS = 576
HALF_ROWS = FLAT_ROWS // 2
VMEM_BYTES = 24 * 2**20

F32 = jnp.float32
BF16 = jnp.bfloat16


class Net:
    def __init__(self, in_size, out_size):
        self.in_size = in_size
        self.out_size = out_size
        self.bias1 = 2 * in_size
        self.weight2 = self.bias1 + 2
        self.bias2 = self.weight2 + 2 * HID
        self.weight3 = self.bias2 + 2
        self.rows = self.weight3 + 2 * out_size
        self.size = self.rows * LANES + out_size


ACTOR = Net(SDIM, ADIM)
CRITIC = Net(SDIM + ADIM, 1)


def dot(a, b):
    return jnp.dot(a, b, preferred_element_type=F32)


def dot_nt(a, b):
    return lax.dot_general(a, b, (((1,), (1,)), ((), ())), preferred_element_type=F32)


def wide(column, width):
    return jnp.concatenate([column] * (width // LANES), axis=1)


def iota(shape, axis):
    return lax.broadcasted_iota(jnp.int32, shape, axis)


def rows_to_lanes(block):
    return jnp.concatenate([block[row : row + 1] for row in range(block.shape[0])], axis=1)


def place_mask(net):
    width = LANES * net.in_size
    position = iota((8, width), 1).astype(F32)
    phase = position - net.in_size * jnp.floor((position + 0.5) * (1.0 / net.in_size))
    blocks = []
    for start in range(0, IN_ROWS, 8):
        row = iota((8, width), 0) + start
        source = jnp.where(row < SDIM, row, jnp.where(row >= ACTION_ROW, row - ACTION_ROW + SDIM, -1))
        source = jnp.where(source < net.in_size, source, -1).astype(F32)
        blocks.append(jnp.where(phase == source, 1.0, 0.0))
    return jnp.concatenate(blocks, axis=0)


def place_units(net):
    shape = (LANES * net.in_size, LANES)
    gap = iota(shape, 0) - net.in_size * iota(shape, 1)
    return jnp.where(gap.astype(jnp.uint32) < net.in_size, 1.0, 0.0).astype(BF16)


def three_parts(value):
    high = value.astype(BF16).astype(F32)
    rest = value - high
    middle = rest.astype(BF16).astype(F32)
    return high, middle, rest - middle


def spread_first(net, flat, mask, spread, slot):
    for half in range(2):
        pieces = [
            jnp.broadcast_to(
                flat[half * net.in_size + row : half * net.in_size + row + 1, :],
                (IN_ROWS, LANES),
            )
            for row in range(net.in_size)
        ]
        start = (2 * slot + half) * IN_ROWS
        spread[start : start + IN_ROWS, :] = (
            jnp.concatenate(pieces, axis=1) * mask[...]
        ).astype(BF16)


def gather_first(spread, units, nets):
    gathered = dot(spread[0 : 2 * IN_ROWS * nets, :], units[...])
    halves = [gathered[i * IN_ROWS : (i + 1) * IN_ROWS] for i in range(2 * nets)]
    return [jnp.concatenate(halves[2 * i : 2 * i + 2], axis=1) for i in range(nets)]


def flatten_first(net, transposed, out, mask, units):
    blocks = [transposed[:, 0:LANES], transposed[:, LANES:HID]]
    parts = [part for block in blocks for part in three_parts(block)]
    spread = dot_nt(jnp.concatenate(parts, axis=0).astype(BF16), units[...])
    for half in range(2):
        high, middle, low = [
            spread[(3 * half + part) * IN_ROWS : (3 * half + part + 1) * IN_ROWS]
            for part in range(3)
        ]
        total = (high + (middle + low)) * mask[...]
        line = jnp.sum(total, axis=0, keepdims=True)
        for row in range(net.in_size):
            target = half * net.in_size + row
            out[target : target + 1, :] = line[:, row * LANES : (row + 1) * LANES]


def as_column(row):
    return jnp.transpose(jnp.broadcast_to(row, (LANES, HID)))


def flat_row(flat, start):
    return jnp.concatenate([flat[start : start + 1, :], flat[start + 1 : start + 2, :]], axis=1)


class Weights:
    shapes = (
        ((HID, IN_ROWS), BF16),
        ((HID, HID), BF16),
        ((HID, LANES), F32),
        ((16, HID), BF16),
    )
    back_shapes = (
        ((HID, HID), BF16),
        ((HID, LANES), F32),
        ((16, HID), BF16),
        ((HID, 16), BF16),
    )


def scratch_of(shapes):
    return [pltpu.VMEM(shape, dtype) for shape, dtype in shapes]


def unpack_first(net, first_t, bias1, refs, back=None):
    first_t = 0.5 * first_t
    row = iota((IN_ROWS, HID), 0)
    for part, value in enumerate(three_parts(0.5 * bias1)):
        first_t = jnp.where(row == ONES_ROW + part, value, first_t)
    refs[0][...] = jnp.transpose(first_t).astype(BF16)
    if back is not None and back[2] is not None:
        back[2][...] = first_t[16:32].astype(BF16)


def unpack_rest(net, flat, refs, back=None):
    first, second, bias2, third = refs
    left = flat[pl.ds(net.weight2, HID, stride=2), :]
    right = flat[pl.ds(net.weight2 + 1, HID, stride=2), :]
    second_value = 0.5 * jnp.concatenate([left, right], axis=1)
    second[...] = second_value.astype(BF16)
    bias2[...] = as_column(0.5 * flat_row(flat, net.bias2))
    left = flat[pl.ds(net.weight3, 8, stride=2), :]
    right = flat[pl.ds(net.weight3 + 1, 8, stride=2), :]
    third_value = jnp.concatenate([left, right], axis=1)
    third_value = jnp.where(iota((8, HID), 0) < net.out_size, third_value, 0.0)
    third_value = jnp.concatenate([third_value, jnp.zeros((8, HID), F32)], axis=0)
    third[...] = third_value.astype(BF16)
    if back is not None:
        second_t, third_column, unused, third_t = back
        second_t[...] = jnp.transpose(second_value).astype(BF16)
        third_low = 0.5 * third_value.astype(BF16).astype(F32)
        if third_column is not None:
            third_column[...] = as_column(third_low[0:1])
        if third_t is not None:
            third_t[...] = jnp.transpose(third_low).astype(BF16)


def unpack_nets(net, values, flat, mask, units, spread, refs, backs):
    biases = []
    for slot, (value, net_refs, back) in enumerate(zip(values, refs, backs)):
        load_flat(net, flat, value())
        spread_first(net, flat, mask, spread, slot)
        biases.append(flat_row(flat, net.bias1))
        unpack_rest(net, flat, net_refs, back)
    firsts = gather_first(spread, units, len(values))
    for first_t, bias1, net_refs, back in zip(firsts, biases, refs, backs):
        unpack_first(net, first_t, bias1, net_refs, back)


def load_flat(net, flat, value):
    flat[0 : net.rows, :] = value
    flat[net.rows : FLAT_ROWS, :] = jnp.zeros((FLAT_ROWS - net.rows, LANES), F32)


def span_of(net, ref, tail):
    where = pl.ds(net.rows * LANES, net.out_size) if tail else pl.ds(0, net.rows * LANES)
    return (where,) if len(ref.shape) == 1 else (slice(0, 1), where)


def body_of(net, ref):
    return ref[span_of(net, ref, False)].reshape(net.rows, LANES)


def tail_of(net, ref):
    return ref[span_of(net, ref, True)].reshape(1, net.out_size)


def tail_column(tail):
    size = tail.shape[1]
    eye = iota((8, size), 0) == iota((8, size), 1)
    return jnp.sum(jnp.where(eye, jnp.broadcast_to(tail, (8, size)), 0.0), axis=1, keepdims=True)


def start_inputs(inputs):
    inputs[...] = jnp.zeros_like(inputs)
    row = iota((8, inputs.shape[1]), 0) + 16
    inputs[16:24, :] = jnp.where((row >= ONES_ROW) & (row < ONES_ROW + 3), 1.0, 0.0)


def staggered(parts, lag):
    parts = list(parts)
    step = 0
    while any(part is not None for part in parts):
        for index, part in enumerate(parts):
            if part is not None and step >= index * lag:
                try:
                    next(part)
                except StopIteration:
                    parts[index] = None
        step += 1


def column_parts(width, size):
    return [slice(start, start + size) for start in range(0, width, size)]


def silu_low(half_pre):
    wave = jnp.tanh(half_pre)
    return (half_pre * wave + half_pre).astype(BF16)


def silu_and_slope(half_pre):
    wave = jnp.tanh(half_pre)
    above = 1.0 + wave
    hidden = half_pre * above
    return hidden.astype(BF16), above + hidden * (1.0 - wave)


def forward(refs, inputs):
    first, second, bias2, third = refs
    width = inputs.shape[1]
    pre = dot(first[...], inputs)
    yield
    hidden = silu_low(pre)
    yield
    pre = dot(second[...], hidden)
    yield
    hidden = silu_low(pre + wide(bias2[...], width))
    yield
    return dot(third[...], hidden)[0:8]


def forward_kept(refs, inputs, hidden1=None):
    first, second, bias2, third = refs
    width = inputs.shape[1]
    pre = dot(first[...], inputs)
    yield
    low1, slope1 = silu_and_slope(pre)
    if hidden1 is not None:
        hidden1[0:HID, :] = low1
    yield
    pre = dot(second[...], low1)
    yield
    low2, slope2 = silu_and_slope(pre + wide(bias2[...], width))
    yield
    return dot(third[...], low2)[0:8], slope1, low2, slope2


def write_gradient(net, sums, last_row, flat, mask, units):
    sum1, sum2, sum3 = sums
    flatten_first(net, sum1[...], flat, mask, units)
    bias1 = sum1[ONES_ROW : ONES_ROW + 1, :]
    bias2 = sum2[HID : HID + 1, :]
    weight2 = jnp.transpose(sum2[0:HID, :])
    for side in range(2):
        lanes = slice(side * LANES, (side + 1) * LANES)
        flat[net.bias1 + side : net.bias1 + side + 1, :] = bias1[:, lanes]
        flat[pl.ds(net.weight2 + side, HID, stride=2), :] = weight2[:, lanes]
        flat[net.bias2 + side : net.bias2 + side + 1, :] = bias2[:, lanes]
        for unit in range(net.out_size):
            row = net.weight3 + 2 * unit + side
            flat[row : row + 1, :] = sum3[unit : unit + 1, lanes]
    flat[net.rows : net.rows + 1, :] = last_row
    rest = FLAT_ROWS - net.rows - 1
    flat[net.rows + 1 : FLAT_ROWS, :] = jnp.zeros((rest, LANES), F32)


def split_halves(flat, core, keep, send):
    low = flat[0:HALF_ROWS, :]
    high = flat[HALF_ROWS:FLAT_ROWS, :]
    keep[...] = jnp.where(core == 0, low, high)
    send[...] = jnp.where(core == 0, high, low)


def join_halves(core, mine, other, flat):
    flat[0:HALF_ROWS, :] = jnp.where(core == 0, mine[...], other[...])
    flat[HALF_ROWS:FLAT_ROWS, :] = jnp.where(core == 0, other[...], mine[...])


def adamw_step(weight, gradient, moment_one, moment_two):
    moment_one = BETA_ONE * moment_one + (1.0 - BETA_ONE) * gradient
    moment_two = BETA_TWO * moment_two + (1.0 - BETA_TWO) * gradient * gradient
    corrected_one = moment_one / (1.0 - BETA_ONE**STEP)
    corrected_two = moment_two / (1.0 - BETA_TWO**STEP)
    weight = weight - LEARN_RATE * (
        corrected_one / (jnp.sqrt(corrected_two) + EPSILON) + WEIGHT_DECAY * weight
    )
    return (weight, moment_one, moment_two)


def polyak_mix(lagged, fresh):
    return POLYAK_RATE * fresh + (1.0 - POLYAK_RATE) * lagged


def clear(refs):
    for ref in refs:
        ref[...] = jnp.zeros_like(ref)


SUM_SHAPES = (((IN_ROWS, HID), F32), ((HID + 16, HID), F32), ((16, HID), F32))


def critic_part(refs, back, bias3, inputs, target, scale, hidden1, sums, tail_sums):
    second_t, third_column = back[0], back[1]
    width = inputs.shape[1]
    out, slope1, low2, slope2 = yield from forward_kept(refs, inputs, hidden1)
    error = out[0:1] + bias3 - target
    grad3 = (scale * error).astype(BF16).astype(F32)
    tail_sums[0:1, :] += grad3
    tail_sums[1:2, :] += error * error
    yield
    grad2 = (wide(third_column[...], width) * grad3 * slope2).astype(BF16)
    sums[2][...] += dot_nt(jnp.broadcast_to(grad3, (16, width)).astype(BF16), low2)
    yield
    grad_low1 = dot(second_t[...], grad2)
    yield
    grad1 = (grad_low1 * slope1).astype(BF16)
    sums[1][...] += dot_nt(hidden1[...], grad2)
    yield
    sums[0][...] += dot_nt(inputs, grad1)


def critic_last_row(tail_sums):
    totals = jnp.sum(tail_sums[...], axis=1, keepdims=True)
    lane = iota((1, LANES), 1)
    return jnp.where(lane == 0, totals[0:1], jnp.where(lane == 1, totals[1:2], 0.0))


def action_kernel(
    core_ref,
    next_states,
    smoothing,
    target_actor,
    next_action,
    mask_actor,
    units_actor,
    inputs,
    flat,
    spread,
    tails,
    *actor,
):
    step = pl.program_id(0)

    @pl.when(step == 0)
    def _():
        start_inputs(inputs)
        units_actor[...] = place_units(ACTOR)
        mask_actor[...] = place_mask(ACTOR)
        unpack_nets(
            ACTOR,
            [lambda: body_of(ACTOR, target_actor)],
            flat,
            mask_actor,
            units_actor,
            spread,
            [actor],
            [None],
        )
        tails[0:8, 0:1] = tail_column(tail_of(ACTOR, target_actor))

    inputs[0:SDIM, :] = next_states[...]

    def part(columns):
        out = yield from forward(actor, inputs[:, columns].astype(BF16))
        lagged_action = jnp.tanh(out + tails[0:8, 0:1])
        jitter = jnp.clip(NOISE_SCALE * smoothing[:, columns], -NOISE_CLIP, NOISE_CLIP)
        next_action[:, columns] = jnp.clip(lagged_action[0:ADIM] + jitter, -1.0, 1.0)

    staggered([part(columns) for columns in column_parts(TILE, ACTION_PART)], LAG)


def target_kernel(
    row_total,
    core_ref,
    states,
    actions,
    rewards,
    next_states,
    done_flags,
    next_action,
    own_lagged,
    far_lagged,
    own_critic,
    far_critic,
    target_out,
    keep,
    send,
    mask_critic,
    units_critic,
    *rest,
):
    next_critic, next_second_t, next_column, next_tail = rest[0:4], rest[4], rest[5], rest[6]
    inputs, hidden1, tail_sums, flat, spread, tails, next_inputs = rest[7:14]
    lag_one, lag_two, critic = rest[14:18], rest[18:22], rest[22:26]
    back = (rest[26], rest[27], None, None)
    sums = rest[28:31]
    core = core_ref[0]
    step = pl.program_id(0)
    width = inputs.shape[1]

    @pl.when(step == 0)
    def _():
        start_inputs(inputs)
        start_inputs(next_inputs)
        hidden1[HID : HID + 16, :] = jnp.ones((16, width), BF16)
        clear(sums)
        clear([tail_sums])
        units_critic[...] = place_units(CRITIC)
        mask_critic[...] = place_mask(CRITIC)

        def chosen(part, holder):
            return jnp.where(core == holder, part(CRITIC, own_critic), part(CRITIC, far_critic))

        unpack_nets(
            CRITIC,
            [
                lambda: body_of(CRITIC, own_lagged),
                lambda: body_of(CRITIC, far_lagged),
                lambda: chosen(body_of, 0),
                lambda: chosen(body_of, 1),
            ],
            flat,
            mask_critic,
            units_critic,
            spread,
            [lag_one, lag_two, critic, next_critic],
            [None, None, back, (next_second_t, next_column, None, None)],
        )
        tails[8:16, 0:1] = tail_column(tail_of(CRITIC, own_lagged))
        tails[16:24, 0:1] = tail_column(tail_of(CRITIC, far_lagged))
        tails[24:32, 0:1] = tail_column(chosen(tail_of, 0))
        next_tail[...] = jnp.broadcast_to(tail_column(chosen(tail_of, 1)), (8, LANES))

    next_inputs[0:SDIM, :] = next_states[...]
    next_inputs[ACTION_ROW : ACTION_ROW + ADIM, :] = next_action[...]
    inputs[0:SDIM, :] = states[...]
    inputs[ACTION_ROW : ACTION_ROW + ADIM, :] = actions[...]

    def part(columns):
        joined = next_inputs[:, columns].astype(BF16)
        out_one = yield from forward(lag_one, joined)
        yield
        out_two = yield from forward(lag_two, joined)
        value_one = out_one[0:1] + tails[8:9, 0:1]
        value_two = out_two[0:1] + tails[16:17, 0:1]
        keep_going = 1.0 - done_flags[:, columns].astype(F32)
        lagged = jnp.minimum(value_one, value_two)
        target = rewards[:, columns] + DISCOUNT * keep_going * lagged
        target_out[:, columns] = target

    def next_part(columns):
        return critic_part(
            critic,
            back,
            tails[24:25, 0:1],
            inputs[:, columns].astype(BF16),
            target_out[:, columns],
            2.0 / row_total,
            hidden1.at[:, columns],
            sums,
            tail_sums.at[:, columns],
        )

    staggered([part(columns) for columns in column_parts(width, TARGET_PART)], TARGET_LAG)
    staggered([next_part(columns) for columns in column_parts(width, CRITIC_PART)], CRITIC_LAG)

    @pl.when(step == pl.num_programs(0) - 1)
    def _():
        last = critic_last_row(tail_sums)
        write_gradient(CRITIC, sums, last, flat, mask_critic, units_critic)
        split_halves(flat, core, keep, send)


def critic_kernel(row_total, is_first, is_last, core_ref, *refs):
    states, actions, target = refs[0:3]
    critic, second_t, third_column, tail = refs[3:7], refs[7], refs[8], refs[9]
    refs = refs[10:]
    if is_last:
        mask, units = refs[0:2]
        refs = refs[2:]
    before = () if is_first else refs[0:4]
    refs = refs[len(before) :]
    if is_last:
        keep, send, inputs, hidden1 = refs[0:4]
        sums, tail_sums, flat = refs[4:7], refs[7], refs[8]
    else:
        sums, tail_sums, inputs, hidden1 = refs[0:3], refs[3], refs[4], refs[5]
    start_inputs(inputs)
    hidden1[HID : HID + 16, :] = jnp.ones((16, TILE), BF16)
    if is_first:
        clear([*sums, tail_sums])
    for after, value in zip([*sums, tail_sums], before):
        after[...] = value[...]
    inputs[0:SDIM, :] = states[...]
    inputs[ACTION_ROW : ACTION_ROW + ADIM, :] = actions[...]

    def part(columns):
        return critic_part(
            critic,
            (second_t, third_column),
            tail[0:1, 0:1],
            inputs[:, columns].astype(BF16),
            target[:, columns],
            2.0 / row_total,
            hidden1.at[:, columns],
            sums,
            tail_sums.at[:, columns],
        )

    staggered([part(columns) for columns in column_parts(TILE, CRITIC_PART)], CRITIC_LAG)
    if is_last:
        last = critic_last_row(tail_sums)
        write_gradient(CRITIC, sums, last, flat, mask, units)
        split_halves(flat, core_ref[0], keep, send)


def actor_kernel(
    row_total,
    core_ref,
    states,
    actor_weights,
    mine,
    other,
    own_critic,
    far_critic,
    own_first,
    far_first,
    own_second,
    far_second,
    mask_actor,
    units_actor,
    mask_critic,
    units_critic,
    keep,
    send,
    inputs,
    hidden1,
    tail_sums,
    flat,
    gradient,
    spread_actor,
    spread_critic,
    tails,
    *rest,
):
    actor, actor_back = rest[0:4], (rest[4], None, None, rest[5])
    judge, judge_back = rest[6:10], (rest[10], rest[11], rest[12], None)
    sums = rest[13:16]
    core = core_ref[0]
    step = pl.program_id(0)
    width = inputs.shape[1]

    @pl.when(step == 0)
    def _():
        start_inputs(inputs)
        hidden1[HID : HID + 16, :] = jnp.ones((16, width), BF16)
        clear(sums)
        clear([tail_sums])
        unpack_nets(
            ACTOR,
            [lambda: body_of(ACTOR, actor_weights)],
            flat,
            mask_actor,
            units_actor,
            spread_actor,
            [actor],
            [actor_back],
        )
        tails[0:8, 0:1] = tail_column(tail_of(ACTOR, actor_weights))
        join_halves(core, mine, other, gradient)

        def chosen(part, own, far):
            return jnp.where(core == 0, part(CRITIC, own), part(CRITIC, far))

        def fresh(part, grad):
            return adamw_step(
                chosen(part, own_critic, far_critic),
                grad,
                chosen(part, own_first, far_first),
                chosen(part, own_second, far_second),
            )[0]

        unpack_nets(
            CRITIC,
            [lambda: fresh(body_of, gradient[0 : CRITIC.rows, :])],
            flat,
            mask_critic,
            units_critic,
            spread_critic,
            [judge],
            [judge_back],
        )
        tail = fresh(tail_of, gradient[CRITIC.rows : CRITIC.rows + 1, 0:1])
        tails[8:16, 0:1] = tail_column(tail)

    inputs[0:SDIM, :] = states[...]
    judge_second_t, judge_column, judge_rows, unused = judge_back
    actor_second_t, unused, unused, actor_third_t = actor_back
    start = jnp.full((HID, LANES), -1.0 / row_total, F32).astype(BF16).astype(F32)
    start = judge_column[...] * start

    def part(columns):
        part_width = columns.stop - columns.start
        state_low = inputs[:, columns].astype(BF16)
        hidden = hidden1.at[:, columns]
        out, slope1, low2, slope2 = yield from forward_kept(actor, state_low, hidden)
        action = jnp.tanh(out + tails[0:8, 0:1])
        inputs[ACTION_ROW:IN_ROWS, columns] = action
        joined = inputs[:, columns].astype(BF16)
        yield
        out, judge_slope1, unused, judge_slope2 = yield from forward_kept(judge, joined)
        tail_sums[8:9, columns] += out[0:1] + tails[8:9, 0:1]
        grad2 = (wide(start, part_width) * judge_slope2).astype(BF16)
        yield
        grad_low1 = dot(judge_second_t[...], grad2)
        yield
        grad1 = (grad_low1 * judge_slope1).astype(BF16)
        yield
        grad_action = 2.0 * dot(judge_rows[...], grad1)[8:16]
        grad3 = (grad_action * (1.0 - action * action)).astype(BF16).astype(F32)
        tail_sums[0:8, columns] += grad3
        grad3_low = jnp.concatenate([grad3, jnp.zeros_like(grad3)], axis=0).astype(BF16)
        yield
        grad_low2 = dot(actor_third_t[...], grad3_low)
        yield
        grad2 = (grad_low2 * slope2).astype(BF16)
        sums[2][...] += dot_nt(grad3_low, low2)
        yield
        grad_low1 = dot(actor_second_t[...], grad2)
        yield
        grad1 = (grad_low1 * slope1).astype(BF16)
        sums[1][...] += dot_nt(hidden[...], grad2)
        yield
        sums[0][...] += dot_nt(state_low, grad1)

    staggered([part(columns) for columns in column_parts(width, ACTOR_PART)], ACTOR_LAG)

    @pl.when(step == pl.num_programs(0) - 1)
    def _():
        totals = jnp.sum(tail_sums[...], axis=1, keepdims=True)
        lane = iota((8, LANES), 1)
        biases = jnp.where(lane == iota((8, LANES), 0), totals[0:8], 0.0)
        last = jnp.sum(biases, axis=0, keepdims=True)
        last = jnp.where(iota((1, LANES), 1) == 8, -totals[8:9], last)
        write_gradient(ACTOR, sums, last, flat, mask_actor, units_actor)
        split_halves(flat, core, keep, send)


def step_kernel(net, loss_lane, core_ref, *refs):
    *halves, weights, first, second, lagged = refs[:-7]
    new_weights, new_first, new_second, new_lagged, loss, gradient, other_gradient = refs[-7:]
    core = core_ref[0]
    join_halves(core, halves[0], halves[1], gradient)
    if len(halves) > 2:
        join_halves(core, halves[2], halves[3], other_gradient)
        gradient[...] = jnp.where(core == 0, gradient[...], other_gradient[...])
    for part, tail, grad in (
        (body_of, False, gradient[0 : net.rows, :]),
        (tail_of, True, gradient[net.rows : net.rows + 1, 0 : net.out_size]),
    ):
        values = [part(net, source) for source in (weights, first, second)]
        fresh, moment_one, moment_two = adamw_step(values[0], grad, values[1], values[2])
        results = (fresh, moment_one, moment_two, polyak_mix(part(net, lagged), fresh))
        for out, result in zip((new_weights, new_first, new_second, new_lagged), results):
            shape = (1, result.size) if len(out.shape) == 2 else (result.size,)
            out[span_of(net, out, tail)] = result.reshape(shape)
    lane = iota((1, LANES), 1)
    row = gradient[net.rows : net.rows + 1, :]
    loss[0] = jnp.sum(jnp.where(lane == loss_lane, row, 0.0))


def twin_swap(value):
    return lax.ppermute(value, "twin", [(0, 1), (1, 0)])


def to_second(value):
    return lax.ppermute(value, "twin", [(0, 1)])


def chip_masks():
    return [1 << bit for bit in range((lax.axis_size("dp") - 1).bit_length())]


def partner(value, mask):
    pairs = [(source, source ^ mask) for source in range(lax.axis_size("dp"))]
    return lax.ppermute(value, "dp", pairs)


def in_hbm(value):
    return pltpu.with_memory_space_constraint(value, pltpu.HBM)


def whole(unused):
    return pl.BlockSpec(memory_space=pltpu.VMEM)


def on_device(
    states,
    actions,
    rewards,
    next_states,
    done_flags,
    smoothing,
    actor_weights,
    actor_first,
    actor_second,
    critic_weights,
    critic_first,
    critic_second,
    target_actor,
    target_critic,
):
    core = lax.axis_index("twin").astype(jnp.int32).reshape(1)
    local_rows = states.shape[1]
    tiles = local_rows // 2 // TILE
    row_total = local_rows * lax.axis_size("dp")
    rewards = rewards.reshape(1, local_rows)
    done_flags = done_flags.reshape(1, local_rows)
    far_lagged = twin_swap(target_critic)
    far_weights = twin_swap(critic_weights)
    far_first = twin_swap(critic_first)
    far_second = twin_swap(critic_second)
    far_lagged, far_weights, far_first, far_second = lax.optimization_barrier(
        (far_lagged, far_weights, far_first, far_second)
    )

    def mine(rows, tile=None, width=TILE):
        count = local_rows // 2 // width
        return pl.BlockSpec(
            (rows, width),
            lambda i, core_ref: (0, core_ref[0] * count + (i if tile is None else tile)),
        )

    def local(rows, tile=None, width=TILE):
        return pl.BlockSpec((rows, width), lambda i, core_ref: (0, i if tile is None else tile))

    def tile_scratch(width):
        return [
            pltpu.VMEM((IN_ROWS, width), F32),
            pltpu.VMEM((HID + 16, width), BF16),
            pltpu.VMEM((16, width), F32),
            flat,
        ]

    actor_flat = whole((ACTOR.size,))
    critic_flat = whole((1, CRITIC.size))
    half = whole((HALF_ROWS, LANES))
    half_shape = jax.ShapeDtypeStruct((HALF_ROWS, LANES), F32)
    tail_shapes = (((16, TILE), F32),)
    flat = pltpu.VMEM((FLAT_ROWS + 8, LANES), F32)

    def places(kind):
        width = LANES * kind.in_size
        mask = jax.ShapeDtypeStruct((IN_ROWS, width), F32)
        return [mask, jax.ShapeDtypeStruct((width, LANES), BF16)]

    def spread(kind, nets):
        return pltpu.VMEM((2 * IN_ROWS * nets, LANES * kind.in_size), BF16)

    place_specs = [whole(None)] * 2
    net = scratch_of(Weights.shapes)
    back = scratch_of(Weights.back_shapes)
    sums = scratch_of(SUM_SHAPES)
    tails = pltpu.VMEM((32, LANES), F32)
    params = pltpu.CompilerParams(vmem_limit_bytes=VMEM_BYTES)

    def call(
        kernel, steps, in_specs, out_specs, out_shape, scratch, name, flops, aliases=(), vmem=VMEM_BYTES
    ):
        return pl.pallas_call(
            kernel,
            grid_spec=pltpu.PrefetchScalarGridSpec(
                num_scalar_prefetch=1,
                grid=(steps,),
                in_specs=in_specs,
                out_specs=out_specs,
                scratch_shapes=scratch,
            ),
            out_shape=out_shape,
            input_output_aliases=dict(aliases),
            compiler_params=pltpu.CompilerParams(vmem_limit_bytes=vmem),
            cost_estimate=pl.CostEstimate(flops=flops, bytes_accessed=10**6, transcendentals=0),
            name=name,
        )

    unit_flops = 2 * HID * HID * TILE
    passed = Weights.shapes + Weights.back_shapes[0:2] + (((8, LANES), F32),)
    passed_specs = [whole(shape) for shape, dtype in passed]
    passed_shapes = [jax.ShapeDtypeStruct(shape, dtype) for shape, dtype in passed]
    next_action, *places_actor = call(
        action_kernel,
        tiles,
        [mine(SDIM), mine(ADIM), actor_flat],
        [local(ADIM)] + place_specs,
        [jax.ShapeDtypeStruct((ADIM, local_rows // 2), F32)] + places(ACTOR),
        [pltpu.VMEM((IN_ROWS, TILE), F32), flat, spread(ACTOR, 1), tails] + net,
        "next_action",
        2 * tiles * unit_flops,
    )(core, in_hbm(next_states), in_hbm(smoothing), target_actor)
    target, keep_one, send_one, *rest = call(
        lambda *refs: target_kernel(row_total, *refs),
        local_rows // 2 // TARGET_TILE,
        [mine(rows, None, TARGET_TILE) for rows in (SDIM, ADIM, 1, SDIM, 1)]
        + [local(ADIM, None, TARGET_TILE)]
        + [critic_flat] * 4,
        [local(1, None, TARGET_TILE), half, half] + place_specs + passed_specs,
        [jax.ShapeDtypeStruct((1, local_rows // 2), F32), half_shape, half_shape]
        + places(CRITIC)
        + passed_shapes,
        tile_scratch(TARGET_TILE)
        + [spread(CRITIC, 4), tails, pltpu.VMEM((IN_ROWS, TARGET_TILE), F32)]
        + net * 3
        + back[0:2]
        + sums,
        "target_and_first_critic",
        14 * tiles * unit_flops,
    )(
        core,
        in_hbm(states),
        in_hbm(actions),
        in_hbm(rewards),
        in_hbm(next_states),
        in_hbm(done_flags),
        next_action,
        target_critic,
        far_lagged,
        critic_weights,
        far_weights,
    )
    places_critic, critic_two = rest[0:2], rest[2:]

    carried = SUM_SHAPES + tail_shapes
    carried_specs = [whole(shape) for shape, dtype in carried]
    carried_shapes = [jax.ShapeDtypeStruct(shape, dtype) for shape, dtype in carried]

    def second_critic(tile, tied_target, state):
        is_first, is_last = tile == 0, tile == tiles - 1
        in_specs = [mine(SDIM, tile), mine(ADIM, tile), local(1, tile)] + passed_specs
        operands = [core, states, actions, tied_target, *critic_two]
        if is_last:
            in_specs = in_specs + place_specs
            operands = operands + places_critic
        scratch = tile_scratch(TILE)[0:2]
        out_specs, out_shape = carried_specs, carried_shapes
        aliases = []
        if not is_first:
            aliases = [(1 + len(in_specs) + i, i) for i in range(len(carried))]
            in_specs = in_specs + carried_specs
        if is_last:
            out_specs, out_shape, aliases = [half, half], [half_shape, half_shape], []
            scratch = scratch + sums + scratch_of(tail_shapes) + [flat]
        return call(
            lambda *refs: critic_kernel(row_total, is_first, is_last, *refs),
            1,
            in_specs,
            out_specs,
            out_shape,
            scratch,
            "second_critic",
            8 * unit_flops,
            aliases,
        )(*operands, *state)

    masks = chip_masks()
    state = ()
    one = keep_one + twin_swap(send_one)
    tile = 0
    for mask in masks:
        moved = partner(one, mask)
        if tile < tiles:
            one, tied_target = lax.optimization_barrier((one, target))
            state = second_critic(tile, tied_target, state)
            tile += 1
        one = one + moved
        one, state = lax.optimization_barrier((one, state))
    while tile < tiles:
        state = second_critic(tile, target, state)
        tile += 1
    keep_two, send_two = state
    one_other = twin_swap(one)
    two = keep_two + twin_swap(send_two)
    two_moved = partner(two, masks[-1])
    two, one, one_other = lax.optimization_barrier((two, one, one_other))
    keep_actor, send_actor = call(
        lambda *refs: actor_kernel(row_total, *refs),
        local_rows // 2 // ACTOR_TILE,
        [mine(SDIM, None, ACTOR_TILE), actor_flat, half, half] + [critic_flat] * 6 + place_specs * 2,
        [half, half],
        [half_shape, half_shape],
        tile_scratch(ACTOR_TILE)
        + [pltpu.VMEM((FLAT_ROWS, LANES), F32), spread(ACTOR, 1), spread(CRITIC, 1), tails]
        + net
        + [back[0], back[3]]
        + net
        + back[0:3]
        + sums,
        "actor",
        10 * tiles * unit_flops,
    )(
        core,
        states,
        actor_weights,
        one,
        one_other,
        critic_weights,
        far_weights,
        critic_first,
        far_first,
        critic_second,
        far_second,
        *places_actor,
        *places_critic,
    )
    actor_moved = twin_swap(send_actor)
    two = two + two_moved
    two, keep_actor, actor_moved = lax.optimization_barrier((two, keep_actor, actor_moved))
    actor = keep_actor + actor_moved
    for mask, other_mask in zip(masks, masks[-2:-1] + masks[:-2] + [None]):
        moved = partner(actor, mask)
        if other_mask is not None:
            two = two + partner(two, other_mask)
        actor = actor + moved
    actor_other = twin_swap(actor)
    two_other = to_second(two)

    def step(net, loss_lane, halves, sources, name):
        vector = pl.BlockSpec(memory_space=pltpu.VMEM)
        scalar = pl.BlockSpec(memory_space=pltpu.SMEM)
        return pl.pallas_call(
            lambda *refs: step_kernel(net, loss_lane, *refs),
            in_specs=[scalar] + [vector] * (len(halves) + len(sources)),
            out_specs=[vector] * len(sources) + [scalar],
            out_shape=[jax.ShapeDtypeStruct(source.shape, F32) for source in sources]
            + [jax.ShapeDtypeStruct((1,), F32)],
            scratch_shapes=[pltpu.VMEM((FLAT_ROWS, LANES), F32)] * 2,
            compiler_params=params,
            name=name,
        )(core, *halves, *sources)

    new_critic, new_critic_first, new_critic_second, new_target_critic, critic_loss = step(
        CRITIC,
        1,
        (one, one_other, two, two_other),
        (critic_weights, critic_first, critic_second, target_critic),
        "critic_step",
    )
    new_actor, new_actor_first, new_actor_second, new_target_actor, actor_loss = step(
        ACTOR,
        8,
        (actor, actor_other),
        (actor_weights, actor_first, actor_second, target_actor),
        "actor_step",
    )
    return (
        new_actor,
        new_actor_first,
        new_actor_second,
        new_critic,
        new_critic_first,
        new_critic_second,
        new_target_actor,
        new_target_critic,
        critic_loss,
        actor_loss.reshape(()),
    )


def solution(mesh):
    columns = P(None, "dp")
    critic = P("twin", None)
    return jax.shard_map(
        on_device,
        mesh=mesh,
        in_specs=(
            columns,
            columns,
            P("dp"),
            columns,
            P("dp"),
            columns,
            P(),
            P(),
            P(),
            critic,
            critic,
            critic,
            P(),
            critic,
        ),
        out_specs=(P(), P(), P(), critic, critic, critic, P(), critic, P("twin"), P()),
        check_vma=False,
    )
```

```python
import jax
import jax.numpy as jnp
from jax import lax
from jax.experimental import pallas as pl
from jax.experimental.pallas import tpu as pltpu
from jax.sharding import PartitionSpec as P

SDIM = 17
ADIM = 6
HID = 256
STEP = 10

DISCOUNT = 0.99
POLYAK_RATE = 0.005
LEARN_RATE = 0.05
BETA_ONE = 0.9
BETA_TWO = 0.999
EPSILON = 1e-08
WEIGHT_DECAY = 0.01
NOISE_SCALE = 0.2
NOISE_CLIP = 0.5

LANES = 128
TILE = 2048
ACTION_PART = 2048
LAG = 1
TARGET_TILE = 2048
TARGET_PART = 2048
TARGET_LAG = 1
CRITIC_PART = 1024
CRITIC_LAG = 3
FORWARD_PART = 2048
FORWARD_LAG = 1
ACTOR_PART = 1024
ACTOR_LAG = 3
ONES_ROW = 17
ACTION_ROW = 24
IN_ROWS = 32
FLAT_ROWS = 576
HALF_ROWS = FLAT_ROWS // 2
VMEM_BYTES = 24 * 2**20
SMALL_VMEM_BYTES = 2**21
FORWARD_VMEM = 8 * 2**20
ACTOR_VMEM = 16 * 2**20

F32 = jnp.float32
BF16 = jnp.bfloat16


class Net:
    def __init__(self, in_size, out_size):
        self.in_size = in_size
        self.out_size = out_size
        self.bias1 = 2 * in_size
        self.weight2 = self.bias1 + 2
        self.bias2 = self.weight2 + 2 * HID
        self.weight3 = self.bias2 + 2
        self.rows = self.weight3 + 2 * out_size
        self.size = self.rows * LANES + out_size


ACTOR = Net(SDIM, ADIM)
CRITIC = Net(SDIM + ADIM, 1)


def dot(a, b):
    return jnp.dot(a, b, preferred_element_type=F32)


def dot_nt(a, b):
    return lax.dot_general(a, b, (((1,), (1,)), ((), ())), preferred_element_type=F32)


def wide(column, width):
    return jnp.concatenate([column] * (width // LANES), axis=1)


def iota(shape, axis):
    return lax.broadcasted_iota(jnp.int32, shape, axis)


def rows_to_lanes(block):
    return jnp.concatenate([block[row : row + 1] for row in range(block.shape[0])], axis=1)


def place_mask(net):
    width = LANES * net.in_size
    position = iota((8, width), 1).astype(F32)
    phase = position - net.in_size * jnp.floor((position + 0.5) * (1.0 / net.in_size))
    blocks = []
    for start in range(0, IN_ROWS, 8):
        row = iota((8, width), 0) + start
        source = jnp.where(row < SDIM, row, jnp.where(row >= ACTION_ROW, row - ACTION_ROW + SDIM, -1))
        source = jnp.where(source < net.in_size, source, -1).astype(F32)
        blocks.append(jnp.where(phase == source, 1.0, 0.0))
    return jnp.concatenate(blocks, axis=0)


def place_units(net):
    shape = (LANES * net.in_size, LANES)
    gap = iota(shape, 0) - net.in_size * iota(shape, 1)
    return jnp.where(gap.astype(jnp.uint32) < net.in_size, 1.0, 0.0).astype(BF16)


def three_parts(value):
    high = value.astype(BF16).astype(F32)
    rest = value - high
    middle = rest.astype(BF16).astype(F32)
    return high, middle, rest - middle


def spread_first(net, flat, mask, spread, slot):
    for half in range(2):
        pieces = [
            jnp.broadcast_to(
                flat[half * net.in_size + row : half * net.in_size + row + 1, :],
                (IN_ROWS, LANES),
            )
            for row in range(net.in_size)
        ]
        start = (2 * slot + half) * IN_ROWS
        spread[start : start + IN_ROWS, :] = (
            jnp.concatenate(pieces, axis=1) * mask[...]
        ).astype(BF16)


def gather_first(spread, units, nets):
    gathered = dot(spread[0 : 2 * IN_ROWS * nets, :], units[...])
    halves = [gathered[i * IN_ROWS : (i + 1) * IN_ROWS] for i in range(2 * nets)]
    return [jnp.concatenate(halves[2 * i : 2 * i + 2], axis=1) for i in range(nets)]


def flatten_first(net, transposed, out, mask, units):
    blocks = [transposed[:, 0:LANES], transposed[:, LANES:HID]]
    parts = [part for block in blocks for part in three_parts(block)]
    spread = dot_nt(jnp.concatenate(parts, axis=0).astype(BF16), units[...])
    for half in range(2):
        high, middle, low = [
            spread[(3 * half + part) * IN_ROWS : (3 * half + part + 1) * IN_ROWS]
            for part in range(3)
        ]
        total = (high + (middle + low)) * mask[...]
        line = jnp.sum(total, axis=0, keepdims=True)
        for row in range(net.in_size):
            target = half * net.in_size + row
            out[target : target + 1, :] = line[:, row * LANES : (row + 1) * LANES]


def as_column(row):
    return jnp.transpose(jnp.broadcast_to(row, (LANES, HID)))


def flat_row(flat, start):
    return jnp.concatenate([flat[start : start + 1, :], flat[start + 1 : start + 2, :]], axis=1)


class Weights:
    shapes = (
        ((HID, IN_ROWS), BF16),
        ((HID, HID), BF16),
        ((HID, LANES), F32),
        ((16, HID), BF16),
    )
    back_shapes = (
        ((HID, HID), BF16),
        ((HID, LANES), F32),
        ((16, HID), BF16),
        ((HID, 16), BF16),
    )


def scratch_of(shapes):
    return [pltpu.VMEM(shape, dtype) for shape, dtype in shapes]


def unpack_first(net, first_t, bias1, refs, back=None):
    first_t = 0.5 * first_t
    row = iota((IN_ROWS, HID), 0)
    for part, value in enumerate(three_parts(0.5 * bias1)):
        first_t = jnp.where(row == ONES_ROW + part, value, first_t)
    refs[0][...] = jnp.transpose(first_t).astype(BF16)
    if back is not None and back[2] is not None:
        back[2][...] = first_t[16:32].astype(BF16)


def unpack_rest(net, flat, refs, back=None):
    first, second, bias2, third = refs
    left = flat[pl.ds(net.weight2, HID, stride=2), :]
    right = flat[pl.ds(net.weight2 + 1, HID, stride=2), :]
    second_value = 0.5 * jnp.concatenate([left, right], axis=1)
    second[...] = second_value.astype(BF16)
    bias2[...] = as_column(0.5 * flat_row(flat, net.bias2))
    left = flat[pl.ds(net.weight3, 8, stride=2), :]
    right = flat[pl.ds(net.weight3 + 1, 8, stride=2), :]
    third_value = jnp.concatenate([left, right], axis=1)
    third_value = jnp.where(iota((8, HID), 0) < net.out_size, third_value, 0.0)
    third_value = jnp.concatenate([third_value, jnp.zeros((8, HID), F32)], axis=0)
    third[...] = third_value.astype(BF16)
    if back is not None:
        second_t, third_column, unused, third_t = back
        second_t[...] = jnp.transpose(second_value).astype(BF16)
        third_low = 0.5 * third_value.astype(BF16).astype(F32)
        if third_column is not None:
            third_column[...] = as_column(third_low[0:1])
        if third_t is not None:
            third_t[...] = jnp.transpose(third_low).astype(BF16)


def unpack_nets(net, values, flat, mask, units, spread, refs, backs):
    biases = []
    for slot, (value, net_refs, back) in enumerate(zip(values, refs, backs)):
        load_flat(net, flat, value())
        spread_first(net, flat, mask, spread, slot)
        biases.append(flat_row(flat, net.bias1))
        unpack_rest(net, flat, net_refs, back)
    firsts = gather_first(spread, units, len(values))
    for first_t, bias1, net_refs, back in zip(firsts, biases, refs, backs):
        unpack_first(net, first_t, bias1, net_refs, back)


def load_flat(net, flat, value):
    flat[0 : net.rows, :] = value
    flat[net.rows : FLAT_ROWS, :] = jnp.zeros((FLAT_ROWS - net.rows, LANES), F32)


def span_of(net, ref, tail):
    where = pl.ds(net.rows * LANES, net.out_size) if tail else pl.ds(0, net.rows * LANES)
    return (where,) if len(ref.shape) == 1 else (slice(0, 1), where)


def body_of(net, ref):
    return ref[span_of(net, ref, False)].reshape(net.rows, LANES)


def tail_of(net, ref):
    return ref[span_of(net, ref, True)].reshape(1, net.out_size)


def tail_column(tail):
    size = tail.shape[1]
    eye = iota((8, size), 0) == iota((8, size), 1)
    return jnp.sum(jnp.where(eye, jnp.broadcast_to(tail, (8, size)), 0.0), axis=1, keepdims=True)


def start_inputs(inputs):
    inputs[...] = jnp.zeros_like(inputs)
    row = iota((8, inputs.shape[1]), 0) + 16
    inputs[16:24, :] = jnp.where((row >= ONES_ROW) & (row < ONES_ROW + 3), 1.0, 0.0)


def staggered(parts, lag):
    parts = list(parts)
    step = 0
    while any(part is not None for part in parts):
        for index, part in enumerate(parts):
            if part is not None and step >= index * lag:
                try:
                    next(part)
                except StopIteration:
                    parts[index] = None
        step += 1


def column_parts(width, size):
    return [slice(start, start + size) for start in range(0, width, size)]


def silu_low(half_pre):
    wave = jnp.tanh(half_pre)
    return (half_pre * wave + half_pre).astype(BF16)


def silu_and_slope(half_pre):
    wave = jnp.tanh(half_pre)
    above = 1.0 + wave
    hidden = half_pre * above
    return hidden.astype(BF16), above + hidden * (1.0 - wave)


def forward(refs, inputs):
    first, second, bias2, third = refs
    width = inputs.shape[1]
    pre = dot(first[...], inputs)
    yield
    hidden = silu_low(pre)
    yield
    pre = dot(second[...], hidden)
    yield
    hidden = silu_low(pre + wide(bias2[...], width))
    yield
    return dot(third[...], hidden)[0:8]


def forward_kept(refs, inputs, hidden1=None):
    first, second, bias2, third = refs
    width = inputs.shape[1]
    pre = dot(first[...], inputs)
    yield
    low1, slope1 = silu_and_slope(pre)
    if hidden1 is not None:
        hidden1[0:HID, :] = low1
    yield
    pre = dot(second[...], low1)
    yield
    low2, slope2 = silu_and_slope(pre + wide(bias2[...], width))
    yield
    return dot(third[...], low2)[0:8], slope1, low2, slope2


def write_gradient(net, sums, last_row, flat, mask, units):
    sum1, sum2, sum3 = sums
    flatten_first(net, sum1[...], flat, mask, units)
    bias1 = sum1[ONES_ROW : ONES_ROW + 1, :]
    bias2 = sum2[HID : HID + 1, :]
    weight2 = jnp.transpose(sum2[0:HID, :])
    for side in range(2):
        lanes = slice(side * LANES, (side + 1) * LANES)
        flat[net.bias1 + side : net.bias1 + side + 1, :] = bias1[:, lanes]
        flat[pl.ds(net.weight2 + side, HID, stride=2), :] = weight2[:, lanes]
        flat[net.bias2 + side : net.bias2 + side + 1, :] = bias2[:, lanes]
        for unit in range(net.out_size):
            row = net.weight3 + 2 * unit + side
            flat[row : row + 1, :] = sum3[unit : unit + 1, lanes]
    flat[net.rows : net.rows + 1, :] = last_row
    rest = FLAT_ROWS - net.rows - 1
    flat[net.rows + 1 : FLAT_ROWS, :] = jnp.zeros((rest, LANES), F32)


def split_halves(flat, core, keep, send):
    low = flat[0:HALF_ROWS, :]
    high = flat[HALF_ROWS:FLAT_ROWS, :]
    keep[...] = jnp.where(core == 0, low, high)
    send[...] = jnp.where(core == 0, high, low)


def join_halves(core, mine, other, flat):
    flat[0:HALF_ROWS, :] = jnp.where(core == 0, mine[...], other[...])
    flat[HALF_ROWS:FLAT_ROWS, :] = jnp.where(core == 0, other[...], mine[...])


def adamw_step(weight, gradient, moment_one, moment_two):
    moment_one = BETA_ONE * moment_one + (1.0 - BETA_ONE) * gradient
    moment_two = BETA_TWO * moment_two + (1.0 - BETA_TWO) * gradient * gradient
    corrected_one = moment_one / (1.0 - BETA_ONE**STEP)
    corrected_two = moment_two / (1.0 - BETA_TWO**STEP)
    weight = weight - LEARN_RATE * (
        corrected_one / (jnp.sqrt(corrected_two) + EPSILON) + WEIGHT_DECAY * weight
    )
    return (weight, moment_one, moment_two)


def polyak_mix(lagged, fresh):
    return POLYAK_RATE * fresh + (1.0 - POLYAK_RATE) * lagged


def clear(refs):
    for ref in refs:
        ref[...] = jnp.zeros_like(ref)


SUM_SHAPES = (((IN_ROWS, HID), F32), ((HID + 16, HID), F32), ((16, HID), F32))


def critic_part(refs, back, bias3, inputs, target, scale, hidden1, sums, tail_sums):
    second_t, third_column = back[0], back[1]
    width = inputs.shape[1]
    out, slope1, low2, slope2 = yield from forward_kept(refs, inputs, hidden1)
    error = out[0:1] + bias3 - target
    grad3 = (scale * error).astype(BF16).astype(F32)
    tail_sums[0:1, :] += grad3
    tail_sums[1:2, :] += error * error
    yield
    grad2 = (wide(third_column[...], width) * grad3 * slope2).astype(BF16)
    sums[2][...] += dot_nt(jnp.broadcast_to(grad3, (16, width)).astype(BF16), low2)
    yield
    grad_low1 = dot(second_t[...], grad2)
    yield
    grad1 = (grad_low1 * slope1).astype(BF16)
    sums[1][...] += dot_nt(hidden1[...], grad2)
    yield
    sums[0][...] += dot_nt(inputs, grad1)


def critic_last_row(tail_sums):
    totals = jnp.sum(tail_sums[...], axis=1, keepdims=True)
    lane = iota((1, LANES), 1)
    return jnp.where(lane == 0, totals[0:1], jnp.where(lane == 1, totals[1:2], 0.0))


def action_kernel(
    core_ref,
    next_states,
    smoothing,
    target_actor,
    next_action,
    mask_actor,
    units_actor,
    inputs,
    flat,
    spread,
    tails,
    *actor,
):
    step = pl.program_id(0)

    @pl.when(step == 0)
    def _():
        start_inputs(inputs)
        units_actor[...] = place_units(ACTOR)
        mask_actor[...] = place_mask(ACTOR)
        unpack_nets(
            ACTOR,
            [lambda: body_of(ACTOR, target_actor)],
            flat,
            mask_actor,
            units_actor,
            spread,
            [actor],
            [None],
        )
        tails[0:8, 0:1] = tail_column(tail_of(ACTOR, target_actor))

    inputs[0:SDIM, :] = next_states[...]

    def part(columns):
        out = yield from forward(actor, inputs[:, columns].astype(BF16))
        lagged_action = jnp.tanh(out + tails[0:8, 0:1])
        jitter = jnp.clip(NOISE_SCALE * smoothing[:, columns], -NOISE_CLIP, NOISE_CLIP)
        next_action[:, columns] = jnp.clip(lagged_action[0:ADIM] + jitter, -1.0, 1.0)

    staggered([part(columns) for columns in column_parts(TILE, ACTION_PART)], LAG)


def target_kernel(
    row_total,
    core_ref,
    states,
    actions,
    rewards,
    next_states,
    done_flags,
    next_action,
    own_lagged,
    far_lagged,
    own_critic,
    far_critic,
    actor_weights,
    mask_actor,
    units_actor,
    target_out,
    keep,
    send,
    mask_critic,
    units_critic,
    *rest,
):
    next_critic, next_second_t, next_column, next_tail = rest[0:4], rest[4], rest[5], rest[6]
    actor, actor_tail, actor_second_t, actor_third_t = rest[7:11], rest[11], rest[12], rest[13]
    rest = rest[14:]
    inputs, hidden1, tail_sums, flat, spread, spread_actor, tails, next_inputs = rest[0:8]
    lag_one, lag_two, critic = rest[8:12], rest[12:16], rest[16:20]
    back = (rest[20], rest[21], None, None)
    sums = rest[22:25]
    core = core_ref[0]
    step = pl.program_id(0)
    width = inputs.shape[1]

    @pl.when(step == 0)
    def _():
        start_inputs(inputs)
        start_inputs(next_inputs)
        hidden1[HID : HID + 16, :] = jnp.ones((16, width), BF16)
        clear(sums)
        clear([tail_sums])
        units_critic[...] = place_units(CRITIC)
        mask_critic[...] = place_mask(CRITIC)

        def chosen(part, holder):
            return jnp.where(core == holder, part(CRITIC, own_critic), part(CRITIC, far_critic))

        unpack_nets(
            CRITIC,
            [
                lambda: body_of(CRITIC, own_lagged),
                lambda: body_of(CRITIC, far_lagged),
                lambda: chosen(body_of, 0),
                lambda: chosen(body_of, 1),
            ],
            flat,
            mask_critic,
            units_critic,
            spread,
            [lag_one, lag_two, critic, next_critic],
            [None, None, back, (next_second_t, next_column, None, None)],
        )
        tails[8:16, 0:1] = tail_column(tail_of(CRITIC, own_lagged))
        tails[16:24, 0:1] = tail_column(tail_of(CRITIC, far_lagged))
        tails[24:32, 0:1] = tail_column(chosen(tail_of, 0))
        next_tail[...] = jnp.broadcast_to(tail_column(chosen(tail_of, 1)), (8, LANES))
        unpack_nets(
            ACTOR,
            [lambda: body_of(ACTOR, actor_weights)],
            flat,
            mask_actor,
            units_actor,
            spread_actor,
            [actor],
            [(actor_second_t, None, None, actor_third_t)],
        )
        tail = tail_column(tail_of(ACTOR, actor_weights))
        actor_tail[...] = jnp.broadcast_to(tail, (8, LANES))

    next_inputs[0:SDIM, :] = next_states[...]
    next_inputs[ACTION_ROW : ACTION_ROW + ADIM, :] = next_action[...]
    inputs[0:SDIM, :] = states[...]
    inputs[ACTION_ROW : ACTION_ROW + ADIM, :] = actions[...]

    def part(columns):
        joined = next_inputs[:, columns].astype(BF16)
        out_one = yield from forward(lag_one, joined)
        yield
        out_two = yield from forward(lag_two, joined)
        value_one = out_one[0:1] + tails[8:9, 0:1]
        value_two = out_two[0:1] + tails[16:17, 0:1]
        keep_going = 1.0 - done_flags[:, columns].astype(F32)
        lagged = jnp.minimum(value_one, value_two)
        target = rewards[:, columns] + DISCOUNT * keep_going * lagged
        target_out[:, columns] = target

    def next_part(columns):
        return critic_part(
            critic,
            back,
            tails[24:25, 0:1],
            inputs[:, columns].astype(BF16),
            target_out[:, columns],
            2.0 / row_total,
            hidden1.at[:, columns],
            sums,
            tail_sums.at[:, columns],
        )

    staggered([part(columns) for columns in column_parts(width, TARGET_PART)], TARGET_LAG)
    staggered([next_part(columns) for columns in column_parts(width, CRITIC_PART)], CRITIC_LAG)

    @pl.when(step == pl.num_programs(0) - 1)
    def _():
        last = critic_last_row(tail_sums)
        write_gradient(CRITIC, sums, last, flat, mask_critic, units_critic)
        split_halves(flat, core, keep, send)


def critic_kernel(row_total, start, width, is_first, is_last, core_ref, *refs):
    states, actions, target = refs[0:3]
    critic, second_t, third_column, tail = refs[3:7], refs[7], refs[8], refs[9]
    refs = refs[10:]
    if is_last:
        mask, units = refs[0:2]
        refs = refs[2:]
    before = ()
    if not is_first:
        before = refs[0:4]
        refs = refs[4:]
    if is_last:
        keep, send, inputs, hidden1 = refs[0:4]
        sums, tail_sums, flat = refs[4:7], refs[7], refs[8]
    else:
        sums, tail_sums, inputs, hidden1 = refs[0:3], refs[3], refs[4], refs[5]
    start_inputs(inputs)
    hidden1[HID : HID + 16, :] = jnp.ones((16, width), BF16)
    if is_first:
        clear([*sums, tail_sums])
    for after, value in zip([*sums, tail_sums], before):
        after[...] = value[...]
    first_column = pl.multiple_of(core_ref[0] * target.shape[1] + start, LANES)
    inputs[0:SDIM, :] = states[:, pl.ds(first_column, width)]
    inputs[ACTION_ROW : ACTION_ROW + ADIM, :] = actions[:, pl.ds(first_column, width)]

    def part(columns):
        return critic_part(
            critic,
            (second_t, third_column),
            tail[0:1, 0:1],
            inputs[:, columns].astype(BF16),
            target[:, start + columns.start : start + columns.stop],
            2.0 / row_total,
            hidden1.at[:, columns],
            sums,
            tail_sums.at[:, columns],
        )

    staggered([part(columns) for columns in column_parts(width, width // 2)], CRITIC_LAG)
    if is_last:
        last = critic_last_row(tail_sums)
        write_gradient(CRITIC, sums, last, flat, mask, units)
        split_halves(flat, core_ref[0], keep, send)


def forward_kernel(
    core_ref,
    states,
    first,
    second,
    bias2,
    third,
    tail,
    kept_low1,
    kept_slope1,
    kept_low2,
    kept_slope2,
    kept_action,
    inputs,
):
    step = pl.program_id(0)

    @pl.when(step == 0)
    def _():
        start_inputs(inputs)

    inputs[0:SDIM, :] = states[...]
    kept_low1[step, HID : HID + 16, :] = jnp.ones((16, TILE), BF16)

    def part(columns):
        out, slope1, low2, slope2 = yield from forward_kept(
            (first, second, bias2, third),
            inputs[:, columns].astype(BF16),
            kept_low1.at[step, :, columns],
        )
        kept_slope1[step, :, columns] = slope1
        kept_low2[step, :, columns] = low2
        kept_slope2[step, :, columns] = slope2
        kept_action[step, :, columns] = jnp.tanh(out + tail[0:8, 0:1])

    staggered([part(columns) for columns in column_parts(TILE, FORWARD_PART)], FORWARD_LAG)


def actor_kernel(
    row_total,
    core_ref,
    states,
    mine,
    other,
    own_critic,
    far_critic,
    own_first,
    far_first,
    own_second,
    far_second,
    mask_actor,
    units_actor,
    mask_critic,
    units_critic,
    actor_second_t,
    actor_third_t,
    kept_low1,
    kept_slope1,
    kept_low2,
    kept_slope2,
    kept_action,
    keep,
    send,
    inputs,
    tail_sums,
    flat,
    gradient,
    spread_critic,
    tails,
    *rest,
):
    judge, judge_back = rest[0:4], (rest[4], rest[5], rest[6], None)
    sums = rest[7:10]
    core = core_ref[0]
    step = pl.program_id(0)
    width = inputs.shape[1]

    @pl.when(step == 0)
    def _():
        start_inputs(inputs)
        clear(sums)
        clear([tail_sums])
        join_halves(core, mine, other, gradient)

        def chosen(part, own, far):
            return jnp.where(core == 0, part(CRITIC, own), part(CRITIC, far))

        def fresh(part, grad):
            return adamw_step(
                chosen(part, own_critic, far_critic),
                grad,
                chosen(part, own_first, far_first),
                chosen(part, own_second, far_second),
            )[0]

        unpack_nets(
            CRITIC,
            [lambda: fresh(body_of, gradient[0 : CRITIC.rows, :])],
            flat,
            mask_critic,
            units_critic,
            spread_critic,
            [judge],
            [judge_back],
        )
        tail = fresh(tail_of, gradient[CRITIC.rows : CRITIC.rows + 1, 0:1])
        tails[8:16, 0:1] = tail_column(tail)

    inputs[0:SDIM, :] = states[...]
    inputs[ACTION_ROW:IN_ROWS, :] = kept_action[step]
    judge_second_t, judge_column, judge_rows, unused = judge_back
    start = jnp.full((HID, LANES), -1.0 / row_total, F32).astype(BF16).astype(F32)
    start = judge_column[...] * start

    def part(columns):
        part_width = columns.stop - columns.start
        joined = inputs[:, columns].astype(BF16)
        action = kept_action[step, :, columns]
        out, judge_slope1, unused, judge_slope2 = yield from forward_kept(judge, joined)
        tail_sums[8:9, columns] += out[0:1] + tails[8:9, 0:1]
        grad2 = (wide(start, part_width) * judge_slope2).astype(BF16)
        yield
        grad_low1 = dot(judge_second_t[...], grad2)
        yield
        grad1 = (grad_low1 * judge_slope1).astype(BF16)
        yield
        grad_action = 2.0 * dot(judge_rows[...], grad1)[8:16]
        grad3 = (grad_action * (1.0 - action * action)).astype(BF16).astype(F32)
        tail_sums[0:8, columns] += grad3
        grad3_low = jnp.concatenate([grad3, jnp.zeros_like(grad3)], axis=0).astype(BF16)
        yield
        grad_low2 = dot(actor_third_t[...], grad3_low)
        yield
        grad2 = (grad_low2 * kept_slope2[step, :, columns]).astype(BF16)
        sums[2][...] += dot_nt(grad3_low, kept_low2[step, :, columns])
        yield
        grad_low1 = dot(actor_second_t[...], grad2)
        yield
        grad1 = (grad_low1 * kept_slope1[step, :, columns]).astype(BF16)
        sums[1][...] += dot_nt(kept_low1[step, :, columns], grad2)
        yield
        sums[0][...] += dot_nt(joined, grad1)

    staggered([part(columns) for columns in column_parts(width, ACTOR_PART)], ACTOR_LAG)

    @pl.when(step == pl.num_programs(0) - 1)
    def _():
        totals = jnp.sum(tail_sums[...], axis=1, keepdims=True)
        lane = iota((8, LANES), 1)
        biases = jnp.where(lane == iota((8, LANES), 0), totals[0:8], 0.0)
        last = jnp.sum(biases, axis=0, keepdims=True)
        last = jnp.where(iota((1, LANES), 1) == 8, -totals[8:9], last)
        write_gradient(ACTOR, sums, last, flat, mask_actor, units_actor)
        split_halves(flat, core, keep, send)


def step_kernel(net, loss_lane, core_ref, *refs):
    *halves, weights, first, second, lagged = refs[:-7]
    new_weights, new_first, new_second, new_lagged, loss, gradient, other_gradient = refs[-7:]
    core = core_ref[0]
    join_halves(core, halves[0], halves[1], gradient)
    if len(halves) > 2:
        join_halves(core, halves[2], halves[3], other_gradient)
        gradient[...] = jnp.where(core == 0, gradient[...], other_gradient[...])
    for part, tail, grad in (
        (body_of, False, gradient[0 : net.rows, :]),
        (tail_of, True, gradient[net.rows : net.rows + 1, 0 : net.out_size]),
    ):
        values = [part(net, source) for source in (weights, first, second)]
        fresh, moment_one, moment_two = adamw_step(values[0], grad, values[1], values[2])
        results = (fresh, moment_one, moment_two, polyak_mix(part(net, lagged), fresh))
        for out, result in zip((new_weights, new_first, new_second, new_lagged), results):
            shape = (1, result.size) if len(out.shape) == 2 else (result.size,)
            out[span_of(net, out, tail)] = result.reshape(shape)
    lane = iota((1, LANES), 1)
    row = gradient[net.rows : net.rows + 1, :]
    loss[0] = jnp.sum(jnp.where(lane == loss_lane, row, 0.0))


def twin_swap(value):
    return lax.ppermute(value, "twin", [(0, 1), (1, 0)])


def to_second(value):
    return lax.ppermute(value, "twin", [(0, 1)])


def chip_masks():
    return [1 << bit for bit in range((lax.axis_size("dp") - 1).bit_length())]


def partner(value, mask):
    pairs = [(source, source ^ mask) for source in range(lax.axis_size("dp"))]
    return lax.ppermute(value, "dp", pairs)


def plus_kernel(left, right, out):
    out[...] = left[...] + right[...]


def plus(left, right):
    vector = pl.BlockSpec(memory_space=pltpu.VMEM)
    return pl.pallas_call(
        plus_kernel,
        in_specs=[vector] * 2,
        out_specs=vector,
        out_shape=jax.ShapeDtypeStruct(left.shape, F32),
        compiler_params=pltpu.CompilerParams(vmem_limit_bytes=SMALL_VMEM_BYTES),
        name="plus",
    )(left, right)


def in_hbm(value):
    return pltpu.with_memory_space_constraint(value, pltpu.HBM)


def whole(unused):
    return pl.BlockSpec(memory_space=pltpu.VMEM)


def on_device(
    states,
    actions,
    rewards,
    next_states,
    done_flags,
    smoothing,
    actor_weights,
    actor_first,
    actor_second,
    critic_weights,
    critic_first,
    critic_second,
    target_actor,
    target_critic,
):
    core = lax.axis_index("twin").astype(jnp.int32).reshape(1)
    local_rows = states.shape[1]
    tiles = local_rows // 2 // TILE
    row_total = local_rows * lax.axis_size("dp")
    rewards = rewards.reshape(1, local_rows)
    done_flags = done_flags.reshape(1, local_rows)
    far_lagged = twin_swap(target_critic)
    far_weights = twin_swap(critic_weights)
    far_first = twin_swap(critic_first)
    far_second = twin_swap(critic_second)
    far_lagged, far_weights, far_first, far_second = lax.optimization_barrier(
        (far_lagged, far_weights, far_first, far_second)
    )

    def mine(rows, tile=None, width=TILE):
        count = local_rows // 2 // width
        return pl.BlockSpec(
            (rows, width),
            lambda i, core_ref: (0, core_ref[0] * count + (i if tile is None else tile)),
        )

    def local(rows, tile=None, width=TILE):
        return pl.BlockSpec((rows, width), lambda i, core_ref: (0, i if tile is None else tile))

    def tile_scratch(width):
        return [
            pltpu.VMEM((IN_ROWS, width), F32),
            pltpu.VMEM((HID + 16, width), BF16),
            pltpu.VMEM((16, width), F32),
            flat,
        ]

    actor_flat = whole((ACTOR.size,))
    critic_flat = whole((1, CRITIC.size))
    half = whole((HALF_ROWS, LANES))
    half_shape = jax.ShapeDtypeStruct((HALF_ROWS, LANES), F32)
    tail_shapes = (((16, TILE), F32),)
    flat = pltpu.VMEM((FLAT_ROWS + 8, LANES), F32)

    def places(kind):
        width = LANES * kind.in_size
        mask = jax.ShapeDtypeStruct((IN_ROWS, width), F32)
        return [mask, jax.ShapeDtypeStruct((width, LANES), BF16)]

    def spread(kind, nets):
        return pltpu.VMEM((2 * IN_ROWS * nets, LANES * kind.in_size), BF16)

    place_specs = [whole(None)] * 2
    net = scratch_of(Weights.shapes)
    back = scratch_of(Weights.back_shapes)
    sums = scratch_of(SUM_SHAPES)
    tails = pltpu.VMEM((32, LANES), F32)
    params = pltpu.CompilerParams(vmem_limit_bytes=VMEM_BYTES)

    def call(
        kernel, steps, in_specs, out_specs, out_shape, scratch, name, flops, aliases=(), vmem=VMEM_BYTES
    ):
        return pl.pallas_call(
            kernel,
            grid_spec=pltpu.PrefetchScalarGridSpec(
                num_scalar_prefetch=1,
                grid=(steps,),
                in_specs=in_specs,
                out_specs=out_specs,
                scratch_shapes=scratch,
            ),
            out_shape=out_shape,
            input_output_aliases=dict(aliases),
            compiler_params=pltpu.CompilerParams(vmem_limit_bytes=vmem),
            cost_estimate=pl.CostEstimate(flops=flops, bytes_accessed=10**6, transcendentals=0),
            name=name,
        )

    unit_flops = 2 * HID * HID * TILE
    passed = Weights.shapes + Weights.back_shapes[0:2] + (((8, LANES), F32),)
    passed_specs = [whole(shape) for shape, dtype in passed]
    passed_shapes = [jax.ShapeDtypeStruct(shape, dtype) for shape, dtype in passed]
    next_action, *places_actor = call(
        action_kernel,
        tiles,
        [mine(SDIM), mine(ADIM), actor_flat],
        [local(ADIM)] + place_specs,
        [jax.ShapeDtypeStruct((ADIM, local_rows // 2), F32)] + places(ACTOR),
        [pltpu.VMEM((IN_ROWS, TILE), F32), flat, spread(ACTOR, 1), tails] + net,
        "next_action",
        2 * tiles * unit_flops,
    )(core, in_hbm(next_states), in_hbm(smoothing), target_actor)
    actor_passed = Weights.shapes + (((8, LANES), F32), Weights.back_shapes[0], Weights.back_shapes[3])
    actor_shapes = [jax.ShapeDtypeStruct(shape, dtype) for shape, dtype in actor_passed]
    target, keep_one, send_one, *rest = call(
        lambda *refs: target_kernel(row_total, *refs),
        local_rows // 2 // TARGET_TILE,
        [mine(rows, None, TARGET_TILE) for rows in (SDIM, ADIM, 1, SDIM, 1)]
        + [local(ADIM, None, TARGET_TILE)]
        + [critic_flat] * 4
        + [actor_flat]
        + place_specs,
        [local(1, None, TARGET_TILE), half, half]
        + place_specs
        + passed_specs
        + [whole(None)] * len(actor_shapes),
        [jax.ShapeDtypeStruct((1, local_rows // 2), F32), half_shape, half_shape]
        + places(CRITIC)
        + passed_shapes
        + actor_shapes,
        tile_scratch(TARGET_TILE)
        + [spread(CRITIC, 4), spread(ACTOR, 1), tails, pltpu.VMEM((IN_ROWS, TARGET_TILE), F32)]
        + net * 3
        + back[0:2]
        + sums,
        "target_and_first_critic",
        14 * tiles * unit_flops,
    )(
        core,
        in_hbm(states),
        in_hbm(actions),
        in_hbm(rewards),
        in_hbm(next_states),
        in_hbm(done_flags),
        next_action,
        target_critic,
        far_lagged,
        critic_weights,
        far_weights,
        actor_weights,
        *places_actor,
    )
    places_critic, critic_two, actor_net = rest[0:2], rest[2 : 2 + len(passed)], rest[2 + len(passed) :]
    kept_shapes = [
        pltpu.VMEM((tiles, rows, TILE), dtype)
        for rows, dtype in ((HID + 16, BF16), (HID, F32), (HID, BF16), (HID, F32), (8, F32))
    ]
    kept_specs = [whole(None)] * len(kept_shapes)

    columns = local_rows // 2
    step_columns = columns // 3 // 512 * 512
    pieces = [(columns - 2 * step_columns, 0)]
    pieces = pieces + [(step_columns, columns - i * step_columns) for i in (2, 1)]
    tail_shapes = (((16, pieces[0][0]), F32),)
    carried = SUM_SHAPES + tail_shapes
    carried_specs = [whole(shape) for shape, dtype in carried]
    carried_shapes = [jax.ShapeDtypeStruct(shape, dtype) for shape, dtype in carried]

    def second_critic(piece, tied_target, state):
        is_first, is_last = piece == 0, piece == len(pieces) - 1
        width, start = pieces[piece]
        operands = [core, states, actions, tied_target, *critic_two]
        scratch = tile_scratch(width)[0:2]
        out_shape = carried_shapes
        if is_last:
            operands = operands + places_critic
            out_shape = [half_shape, half_shape]
            scratch = scratch + sums + scratch_of(tail_shapes) + [flat]
        aliases = []
        if not is_first and not is_last:
            aliases = [(len(operands) + i, i) for i in range(len(state))]
        operands = operands + list(state)
        return call(
            lambda *refs: critic_kernel(row_total, start, width, is_first, is_last, *refs),
            1,
            [whole(None)] * (len(operands) - 1),
            [whole(None)] * len(out_shape),
            out_shape,
            scratch,
            "second_critic",
            8 * unit_flops,
            aliases,
        )(*operands)

    def actor_forward(tied_tail):
        return call(
            forward_kernel,
            tiles,
            [mine(SDIM)] + [whole(None)] * 5,
            kept_specs,
            kept_shapes,
            [pltpu.VMEM((IN_ROWS, TILE), F32)],
            "actor_forward",
            12 * unit_flops,
            vmem=FORWARD_VMEM,
        )(core, states, *actor_net[0:4], tied_tail)

    masks = chip_masks()
    state = ()
    one = keep_one + twin_swap(send_one)
    piece = 0
    for mask in masks:
        moved = partner(one, mask)
        if mask == masks[-1]:
            one, tied_tail = lax.optimization_barrier((one, actor_net[4]))
            kept = actor_forward(tied_tail)
            *kept, last = kept
            one, last = lax.optimization_barrier((plus(one, moved), last))
            kept = [*kept, last]
        elif piece < len(pieces):
            one, tied_target = lax.optimization_barrier((one, target))
            state = second_critic(piece, tied_target, state)
            piece += 1
            one, state = lax.optimization_barrier((one + moved, state))
        else:
            one = one + moved
    while piece < len(pieces):
        state = second_critic(piece, target, state)
        piece += 1
    keep_two, send_two = state
    one_other = twin_swap(one)
    two = plus(keep_two, twin_swap(send_two))
    two_moved = partner(two, masks[-1])
    two, one, one_other = lax.optimization_barrier((two, one, one_other))
    keep_actor, send_actor = call(
        lambda *refs: actor_kernel(row_total, *refs),
        tiles,
        [mine(SDIM), half, half]
        + [critic_flat] * 6
        + place_specs * 2
        + [whole(None)] * 2
        + kept_specs,
        [half, half],
        [half_shape, half_shape],
        [tile_scratch(TILE)[i] for i in (0, 2, 3)]
        + [pltpu.VMEM((FLAT_ROWS, LANES), F32), spread(CRITIC, 1), tails]
        + net
        + back[0:3]
        + sums,
        "actor",
        8 * tiles * unit_flops,
        vmem=ACTOR_VMEM,
    )(
        core,
        states,
        one,
        one_other,
        critic_weights,
        far_weights,
        critic_first,
        far_first,
        critic_second,
        far_second,
        *places_actor,
        *places_critic,
        *actor_net[5:7],
        *[pltpu.with_memory_space_constraint(value, pltpu.VMEM) for value in kept],
    )
    actor_moved = twin_swap(send_actor)
    two = two + two_moved
    two, keep_actor, actor_moved = lax.optimization_barrier((two, keep_actor, actor_moved))
    actor = keep_actor + actor_moved
    for mask, other_mask in zip(masks, masks[-2:-1] + masks[:-2] + [None]):
        moved = partner(actor, mask)
        if other_mask is not None:
            two = two + partner(two, other_mask)
        actor = actor + moved
    actor_other = twin_swap(actor)
    two_other = to_second(two)

    def step(net, loss_lane, halves, sources, name):
        vector = pl.BlockSpec(memory_space=pltpu.VMEM)
        scalar = pl.BlockSpec(memory_space=pltpu.SMEM)
        return pl.pallas_call(
            lambda *refs: step_kernel(net, loss_lane, *refs),
            in_specs=[scalar] + [vector] * (len(halves) + len(sources)),
            out_specs=[vector] * len(sources) + [scalar],
            out_shape=[jax.ShapeDtypeStruct(source.shape, F32) for source in sources]
            + [jax.ShapeDtypeStruct((1,), F32)],
            scratch_shapes=[pltpu.VMEM((FLAT_ROWS, LANES), F32)] * 2,
            compiler_params=params,
            name=name,
        )(core, *halves, *sources)

    new_critic, new_critic_first, new_critic_second, new_target_critic, critic_loss = step(
        CRITIC,
        1,
        (one, one_other, two, two_other),
        (critic_weights, critic_first, critic_second, target_critic),
        "critic_step",
    )
    new_actor, new_actor_first, new_actor_second, new_target_actor, actor_loss = step(
        ACTOR,
        8,
        (actor, actor_other),
        (actor_weights, actor_first, actor_second, target_actor),
        "actor_step",
    )
    return (
        new_actor,
        new_actor_first,
        new_actor_second,
        new_critic,
        new_critic_first,
        new_critic_second,
        new_target_actor,
        new_target_critic,
        critic_loss,
        actor_loss.reshape(()),
    )


def solution(mesh):
    columns = P(None, "dp")
    critic = P("twin", None)
    return jax.shard_map(
        on_device,
        mesh=mesh,
        in_specs=(
            columns,
            columns,
            P("dp"),
            columns,
            P("dp"),
            columns,
            P(),
            P(),
            P(),
            critic,
            critic,
            critic,
            P(),
            critic,
        ),
        out_specs=(P(), P(), P(), critic, critic, critic, P(), critic, P("twin"), P()),
        check_vma=False,
    )
```

```python
import jax
import jax.numpy as jnp
from jax import lax
from jax.experimental import pallas as pl
from jax.experimental.pallas import tpu as pltpu
from jax.sharding import PartitionSpec as P

SDIM = 17
ADIM = 6
HID = 256
STEP = 10

DISCOUNT = 0.99
POLYAK_RATE = 0.005
LEARN_RATE = 0.05
BETA_ONE = 0.9
BETA_TWO = 0.999
EPSILON = 1e-08
WEIGHT_DECAY = 0.01
NOISE_SCALE = 0.2
NOISE_CLIP = 0.5

LANES = 128
TILE = 2048
ACTION_PART = 2048
LAG = 1
TARGET_TILE = 2048
TARGET_PART = 2048
TARGET_LAG = 1
CRITIC_PART = 1024
CRITIC_LAG = 3
FORWARD_PART = 2048
FORWARD_LAG = 1
ACTOR_PART = 1024
ACTOR_LAG = 3
ONES_ROW = 17
ACTION_ROW = 24
IN_ROWS = 32
FLAT_ROWS = 576
HALF_ROWS = FLAT_ROWS // 2
VMEM_BYTES = 24 * 2**20
SMALL_VMEM_BYTES = 2**21
FORWARD_VMEM = 8 * 2**20
ACTOR_VMEM = 16 * 2**20

F32 = jnp.float32
BF16 = jnp.bfloat16


class Net:
    def __init__(self, in_size, out_size):
        self.in_size = in_size
        self.out_size = out_size
        self.bias1 = 2 * in_size
        self.weight2 = self.bias1 + 2
        self.bias2 = self.weight2 + 2 * HID
        self.weight3 = self.bias2 + 2
        self.rows = self.weight3 + 2 * out_size
        self.size = self.rows * LANES + out_size


ACTOR = Net(SDIM, ADIM)
CRITIC = Net(SDIM + ADIM, 1)


def dot(a, b):
    return jnp.dot(a, b, preferred_element_type=F32)


def dot_nt(a, b):
    return lax.dot_general(a, b, (((1,), (1,)), ((), ())), preferred_element_type=F32)


def wide(column, width):
    return jnp.concatenate([column] * (width // LANES), axis=1)


def iota(shape, axis):
    return lax.broadcasted_iota(jnp.int32, shape, axis)


def rows_to_lanes(block):
    return jnp.concatenate([block[row : row + 1] for row in range(block.shape[0])], axis=1)


def place_mask(net):
    width = LANES * net.in_size
    position = iota((8, width), 1).astype(F32)
    phase = position - net.in_size * jnp.floor((position + 0.5) * (1.0 / net.in_size))
    blocks = []
    for start in range(0, IN_ROWS, 8):
        row = iota((8, width), 0) + start
        source = jnp.where(row < SDIM, row, jnp.where(row >= ACTION_ROW, row - ACTION_ROW + SDIM, -1))
        source = jnp.where(source < net.in_size, source, -1).astype(F32)
        blocks.append(jnp.where(phase == source, 1.0, 0.0))
    return jnp.concatenate(blocks, axis=0)


def place_units(net):
    shape = (LANES * net.in_size, LANES)
    gap = iota(shape, 0) - net.in_size * iota(shape, 1)
    return jnp.where(gap.astype(jnp.uint32) < net.in_size, 1.0, 0.0).astype(BF16)


def three_parts(value):
    high = value.astype(BF16).astype(F32)
    rest = value - high
    middle = rest.astype(BF16).astype(F32)
    return high, middle, rest - middle


def spread_first(net, flat, mask, spread, slot):
    for half in range(2):
        pieces = [
            jnp.broadcast_to(
                flat[half * net.in_size + row : half * net.in_size + row + 1, :],
                (IN_ROWS, LANES),
            )
            for row in range(net.in_size)
        ]
        start = (2 * slot + half) * IN_ROWS
        spread[start : start + IN_ROWS, :] = (
            jnp.concatenate(pieces, axis=1) * mask[...]
        ).astype(BF16)


def gather_first(spread, units, nets):
    gathered = dot(spread[0 : 2 * IN_ROWS * nets, :], units[...])
    halves = [gathered[i * IN_ROWS : (i + 1) * IN_ROWS] for i in range(2 * nets)]
    return [jnp.concatenate(halves[2 * i : 2 * i + 2], axis=1) for i in range(nets)]


def flatten_first(net, transposed, out, mask, units):
    blocks = [transposed[:, 0:LANES], transposed[:, LANES:HID]]
    parts = [part for block in blocks for part in three_parts(block)]
    spread = dot_nt(jnp.concatenate(parts, axis=0).astype(BF16), units[...])
    for half in range(2):
        high, middle, low = [
            spread[(3 * half + part) * IN_ROWS : (3 * half + part + 1) * IN_ROWS]
            for part in range(3)
        ]
        total = (high + (middle + low)) * mask[...]
        line = jnp.sum(total, axis=0, keepdims=True)
        for row in range(net.in_size):
            target = half * net.in_size + row
            out[target : target + 1, :] = line[:, row * LANES : (row + 1) * LANES]


def as_column(row):
    return jnp.transpose(jnp.broadcast_to(row, (LANES, HID)))


def flat_row(flat, start):
    return jnp.concatenate([flat[start : start + 1, :], flat[start + 1 : start + 2, :]], axis=1)


class Weights:
    shapes = (
        ((HID, IN_ROWS), BF16),
        ((HID, HID), BF16),
        ((HID, LANES), F32),
        ((16, HID), BF16),
    )
    back_shapes = (
        ((HID, HID), BF16),
        ((HID, LANES), F32),
        ((16, HID), BF16),
        ((HID, 16), BF16),
    )


def scratch_of(shapes):
    return [pltpu.VMEM(shape, dtype) for shape, dtype in shapes]


def unpack_first(net, first_t, bias1, refs, back=None):
    first_t = 0.5 * first_t
    row = iota((IN_ROWS, HID), 0)
    for part, value in enumerate(three_parts(0.5 * bias1)):
        first_t = jnp.where(row == ONES_ROW + part, value, first_t)
    refs[0][...] = jnp.transpose(first_t).astype(BF16)
    if back is not None and back[2] is not None:
        back[2][...] = first_t[16:32].astype(BF16)


def unpack_rest(net, flat, refs, back=None):
    first, second, bias2, third = refs
    left = flat[pl.ds(net.weight2, HID, stride=2), :]
    right = flat[pl.ds(net.weight2 + 1, HID, stride=2), :]
    second_value = 0.5 * jnp.concatenate([left, right], axis=1)
    second[...] = second_value.astype(BF16)
    bias2[...] = as_column(0.5 * flat_row(flat, net.bias2))
    left = flat[pl.ds(net.weight3, 8, stride=2), :]
    right = flat[pl.ds(net.weight3 + 1, 8, stride=2), :]
    third_value = jnp.concatenate([left, right], axis=1)
    third_value = jnp.where(iota((8, HID), 0) < net.out_size, third_value, 0.0)
    third_value = jnp.concatenate([third_value, jnp.zeros((8, HID), F32)], axis=0)
    third[...] = third_value.astype(BF16)
    if back is not None:
        second_t, third_column, unused, third_t = back
        second_t[...] = jnp.transpose(second_value).astype(BF16)
        third_low = 0.5 * third_value.astype(BF16).astype(F32)
        if third_column is not None:
            third_column[...] = as_column(third_low[0:1])
        if third_t is not None:
            third_t[...] = jnp.transpose(third_low).astype(BF16)


def unpack_nets(net, values, flat, mask, units, spread, refs, backs):
    biases = []
    for slot, (value, net_refs, back) in enumerate(zip(values, refs, backs)):
        load_flat(net, flat, value())
        spread_first(net, flat, mask, spread, slot)
        biases.append(flat_row(flat, net.bias1))
        unpack_rest(net, flat, net_refs, back)
    firsts = gather_first(spread, units, len(values))
    for first_t, bias1, net_refs, back in zip(firsts, biases, refs, backs):
        unpack_first(net, first_t, bias1, net_refs, back)


def load_flat(net, flat, value):
    flat[0 : net.rows, :] = value
    flat[net.rows : FLAT_ROWS, :] = jnp.zeros((FLAT_ROWS - net.rows, LANES), F32)


def span_of(net, ref, tail):
    where = pl.ds(net.rows * LANES, net.out_size) if tail else pl.ds(0, net.rows * LANES)
    return (where,) if len(ref.shape) == 1 else (slice(0, 1), where)


def body_of(net, ref):
    return ref[span_of(net, ref, False)].reshape(net.rows, LANES)


def tail_of(net, ref):
    return ref[span_of(net, ref, True)].reshape(1, net.out_size)


def tail_column(tail):
    size = tail.shape[1]
    eye = iota((8, size), 0) == iota((8, size), 1)
    return jnp.sum(jnp.where(eye, jnp.broadcast_to(tail, (8, size)), 0.0), axis=1, keepdims=True)


def start_inputs(inputs):
    inputs[...] = jnp.zeros_like(inputs)
    row = iota((8, inputs.shape[1]), 0) + 16
    inputs[16:24, :] = jnp.where((row >= ONES_ROW) & (row < ONES_ROW + 3), 1.0, 0.0)


def staggered(parts, lag):
    parts = list(parts)
    step = 0
    while any(part is not None for part in parts):
        for index, part in enumerate(parts):
            if part is not None and step >= index * lag:
                try:
                    next(part)
                except StopIteration:
                    parts[index] = None
        step += 1


def column_parts(width, size):
    return [slice(start, start + size) for start in range(0, width, size)]


def silu_low(half_pre):
    wave = jnp.tanh(half_pre)
    return (half_pre * wave + half_pre).astype(BF16)


def silu_and_slope(half_pre):
    wave = jnp.tanh(half_pre)
    above = 1.0 + wave
    hidden = half_pre * above
    return hidden.astype(BF16), above + hidden * (1.0 - wave)


def forward(refs, inputs):
    first, second, bias2, third = refs
    width = inputs.shape[1]
    pre = dot(first[...], inputs)
    yield
    hidden = silu_low(pre)
    yield
    pre = dot(second[...], hidden)
    yield
    hidden = silu_low(pre + wide(bias2[...], width))
    yield
    return dot(third[...], hidden)[0:8]


def forward_kept(refs, inputs, hidden1=None):
    first, second, bias2, third = refs
    width = inputs.shape[1]
    pre = dot(first[...], inputs)
    yield
    low1, slope1 = silu_and_slope(pre)
    if hidden1 is not None:
        hidden1[0:HID, :] = low1
    yield
    pre = dot(second[...], low1)
    yield
    low2, slope2 = silu_and_slope(pre + wide(bias2[...], width))
    yield
    return dot(third[...], low2)[0:8], slope1, low2, slope2


def write_gradient(net, sums, last_row, flat, mask, units):
    sum1, sum2, sum3 = sums
    flatten_first(net, sum1[...], flat, mask, units)
    bias1 = sum1[ONES_ROW : ONES_ROW + 1, :]
    bias2 = sum2[HID : HID + 1, :]
    weight2 = jnp.transpose(sum2[0:HID, :])
    for side in range(2):
        lanes = slice(side * LANES, (side + 1) * LANES)
        flat[net.bias1 + side : net.bias1 + side + 1, :] = bias1[:, lanes]
        flat[pl.ds(net.weight2 + side, HID, stride=2), :] = weight2[:, lanes]
        flat[net.bias2 + side : net.bias2 + side + 1, :] = bias2[:, lanes]
        for unit in range(net.out_size):
            row = net.weight3 + 2 * unit + side
            flat[row : row + 1, :] = sum3[unit : unit + 1, lanes]
    flat[net.rows : net.rows + 1, :] = last_row
    rest = FLAT_ROWS - net.rows - 1
    flat[net.rows + 1 : FLAT_ROWS, :] = jnp.zeros((rest, LANES), F32)


def split_halves(flat, core, keep, send):
    low = flat[0:HALF_ROWS, :]
    high = flat[HALF_ROWS:FLAT_ROWS, :]
    keep[...] = jnp.where(core == 0, low, high)
    send[...] = jnp.where(core == 0, high, low)


def join_halves(core, mine, other, flat):
    flat[0:HALF_ROWS, :] = jnp.where(core == 0, mine[...], other[...])
    flat[HALF_ROWS:FLAT_ROWS, :] = jnp.where(core == 0, other[...], mine[...])


def adamw_step(weight, gradient, moment_one, moment_two):
    moment_one = BETA_ONE * moment_one + (1.0 - BETA_ONE) * gradient
    moment_two = BETA_TWO * moment_two + (1.0 - BETA_TWO) * gradient * gradient
    corrected_one = moment_one / (1.0 - BETA_ONE**STEP)
    corrected_two = moment_two / (1.0 - BETA_TWO**STEP)
    weight = weight - LEARN_RATE * (
        corrected_one / (jnp.sqrt(corrected_two) + EPSILON) + WEIGHT_DECAY * weight
    )
    return (weight, moment_one, moment_two)


def polyak_mix(lagged, fresh):
    return POLYAK_RATE * fresh + (1.0 - POLYAK_RATE) * lagged


def clear(refs):
    for ref in refs:
        ref[...] = jnp.zeros_like(ref)


SUM_SHAPES = (((IN_ROWS, HID), F32), ((HID + 16, HID), F32), ((16, HID), F32))


def critic_part(refs, back, bias3, inputs, target, scale, hidden1, sums, tail_sums):
    second_t, third_column = back[0], back[1]
    width = inputs.shape[1]
    out, slope1, low2, slope2 = yield from forward_kept(refs, inputs, hidden1)
    error = out[0:1] + bias3 - target
    grad3 = (scale * error).astype(BF16).astype(F32)
    tail_sums[0:1, :] += grad3
    tail_sums[1:2, :] += error * error
    yield
    grad2 = (wide(third_column[...], width) * grad3 * slope2).astype(BF16)
    sums[2][...] += dot_nt(jnp.broadcast_to(grad3, (16, width)).astype(BF16), low2)
    yield
    grad_low1 = dot(second_t[...], grad2)
    yield
    grad1 = (grad_low1 * slope1).astype(BF16)
    sums[1][...] += dot_nt(hidden1[...], grad2)
    yield
    sums[0][...] += dot_nt(inputs, grad1)


def critic_last_row(tail_sums):
    totals = jnp.sum(tail_sums[...], axis=1, keepdims=True)
    lane = iota((1, LANES), 1)
    return jnp.where(lane == 0, totals[0:1], jnp.where(lane == 1, totals[1:2], 0.0))


def action_kernel(
    core_ref,
    next_states,
    smoothing,
    target_actor,
    next_action,
    mask_actor,
    units_actor,
    inputs,
    flat,
    spread,
    tails,
    *actor,
):
    step = pl.program_id(0)

    @pl.when(step == 0)
    def _():
        start_inputs(inputs)
        units_actor[...] = place_units(ACTOR)
        mask_actor[...] = place_mask(ACTOR)
        unpack_nets(
            ACTOR,
            [lambda: body_of(ACTOR, target_actor)],
            flat,
            mask_actor,
            units_actor,
            spread,
            [actor],
            [None],
        )
        tails[0:8, 0:1] = tail_column(tail_of(ACTOR, target_actor))

    inputs[0:SDIM, :] = next_states[...]

    def part(columns):
        out = yield from forward(actor, inputs[:, columns].astype(BF16))
        lagged_action = jnp.tanh(out + tails[0:8, 0:1])
        jitter = jnp.clip(NOISE_SCALE * smoothing[:, columns], -NOISE_CLIP, NOISE_CLIP)
        next_action[:, columns] = jnp.clip(lagged_action[0:ADIM] + jitter, -1.0, 1.0)

    staggered([part(columns) for columns in column_parts(TILE, ACTION_PART)], LAG)


def target_kernel(
    row_total,
    core_ref,
    states,
    actions,
    rewards,
    next_states,
    done_flags,
    next_action,
    own_lagged,
    far_lagged,
    own_critic,
    far_critic,
    actor_weights,
    mask_actor,
    units_actor,
    target_out,
    keep,
    send,
    mask_critic,
    units_critic,
    *rest,
):
    next_critic, next_second_t, next_column, next_tail = rest[0:4], rest[4], rest[5], rest[6]
    actor, actor_tail, actor_second_t, actor_third_t = rest[7:11], rest[11], rest[12], rest[13]
    rest = rest[14:]
    inputs, hidden1, tail_sums, flat, spread, spread_actor, tails, next_inputs = rest[0:8]
    lag_one, lag_two, critic = rest[8:12], rest[12:16], rest[16:20]
    back = (rest[20], rest[21], None, None)
    sums = rest[22:25]
    core = core_ref[0]
    step = pl.program_id(0)
    width = inputs.shape[1]

    @pl.when(step == 0)
    def _():
        start_inputs(inputs)
        start_inputs(next_inputs)
        hidden1[HID : HID + 16, :] = jnp.ones((16, width), BF16)
        clear(sums)
        clear([tail_sums])
        units_critic[...] = place_units(CRITIC)
        mask_critic[...] = place_mask(CRITIC)

        def chosen(part, holder):
            return jnp.where(core == holder, part(CRITIC, own_critic), part(CRITIC, far_critic))

        unpack_nets(
            CRITIC,
            [
                lambda: body_of(CRITIC, own_lagged),
                lambda: body_of(CRITIC, far_lagged),
                lambda: chosen(body_of, 0),
                lambda: chosen(body_of, 1),
            ],
            flat,
            mask_critic,
            units_critic,
            spread,
            [lag_one, lag_two, critic, next_critic],
            [None, None, back, (next_second_t, next_column, None, None)],
        )
        tails[8:16, 0:1] = tail_column(tail_of(CRITIC, own_lagged))
        tails[16:24, 0:1] = tail_column(tail_of(CRITIC, far_lagged))
        tails[24:32, 0:1] = tail_column(chosen(tail_of, 0))
        next_tail[...] = jnp.broadcast_to(tail_column(chosen(tail_of, 1)), (8, LANES))
        unpack_nets(
            ACTOR,
            [lambda: body_of(ACTOR, actor_weights)],
            flat,
            mask_actor,
            units_actor,
            spread_actor,
            [actor],
            [(actor_second_t, None, None, actor_third_t)],
        )
        tail = tail_column(tail_of(ACTOR, actor_weights))
        actor_tail[...] = jnp.broadcast_to(tail, (8, LANES))

    next_inputs[0:SDIM, :] = next_states[...]
    next_inputs[ACTION_ROW : ACTION_ROW + ADIM, :] = next_action[...]
    inputs[0:SDIM, :] = states[...]
    inputs[ACTION_ROW : ACTION_ROW + ADIM, :] = actions[...]

    def part(columns):
        joined = next_inputs[:, columns].astype(BF16)
        out_one = yield from forward(lag_one, joined)
        yield
        out_two = yield from forward(lag_two, joined)
        value_one = out_one[0:1] + tails[8:9, 0:1]
        value_two = out_two[0:1] + tails[16:17, 0:1]
        keep_going = 1.0 - done_flags[:, columns].astype(F32)
        lagged = jnp.minimum(value_one, value_two)
        target = rewards[:, columns] + DISCOUNT * keep_going * lagged
        target_out[:, columns] = target

    def next_part(columns):
        return critic_part(
            critic,
            back,
            tails[24:25, 0:1],
            inputs[:, columns].astype(BF16),
            target_out[:, columns],
            2.0 / row_total,
            hidden1.at[:, columns],
            sums,
            tail_sums.at[:, columns],
        )

    staggered([part(columns) for columns in column_parts(width, TARGET_PART)], TARGET_LAG)
    staggered([next_part(columns) for columns in column_parts(width, CRITIC_PART)], CRITIC_LAG)

    @pl.when(step == pl.num_programs(0) - 1)
    def _():
        last = critic_last_row(tail_sums)
        write_gradient(CRITIC, sums, last, flat, mask_critic, units_critic)
        split_halves(flat, core, keep, send)


def critic_kernel(row_total, start, width, is_first, is_last, core_ref, *refs):
    states, actions, target = refs[0:3]
    critic, second_t, third_column, tail = refs[3:7], refs[7], refs[8], refs[9]
    refs = refs[10:]
    if is_last:
        mask, units = refs[0:2]
        refs = refs[2:]
    before = ()
    if not is_first:
        before = refs[0:4]
        refs = refs[4:]
    if is_last:
        keep, send, inputs, hidden1 = refs[0:4]
        sums, tail_sums, flat = refs[4:7], refs[7], refs[8]
    else:
        sums, tail_sums, inputs, hidden1 = refs[0:3], refs[3], refs[4], refs[5]
    start_inputs(inputs)
    hidden1[HID : HID + 16, :] = jnp.ones((16, width), BF16)
    if is_first:
        clear([*sums, tail_sums])
    for after, value in zip([*sums, tail_sums], before):
        after[...] = value[...]
    first_column = pl.multiple_of(core_ref[0] * target.shape[1] + start, LANES)
    inputs[0:SDIM, :] = states[:, pl.ds(first_column, width)]
    inputs[ACTION_ROW : ACTION_ROW + ADIM, :] = actions[:, pl.ds(first_column, width)]

    def part(columns):
        return critic_part(
            critic,
            (second_t, third_column),
            tail[0:1, 0:1],
            inputs[:, columns].astype(BF16),
            target[:, start + columns.start : start + columns.stop],
            2.0 / row_total,
            hidden1.at[:, columns],
            sums,
            tail_sums.at[:, columns],
        )

    staggered([part(columns) for columns in column_parts(width, width // 2)], CRITIC_LAG)
    if is_last:
        last = critic_last_row(tail_sums)
        write_gradient(CRITIC, sums, last, flat, mask, units)
        split_halves(flat, core_ref[0], keep, send)


def forward_kernel(
    core_ref,
    states,
    first,
    second,
    bias2,
    third,
    tail,
    kept_low1,
    kept_slope1,
    kept_low2,
    kept_slope2,
    kept_action,
    inputs,
):
    step = pl.program_id(0)

    @pl.when(step == 0)
    def _():
        start_inputs(inputs)

    inputs[0:SDIM, :] = states[...]
    kept_low1[step, HID : HID + 16, :] = jnp.ones((16, TILE), BF16)

    def part(columns):
        out, slope1, low2, slope2 = yield from forward_kept(
            (first, second, bias2, third),
            inputs[:, columns].astype(BF16),
            kept_low1.at[step, :, columns],
        )
        kept_slope1[step, :, columns] = slope1
        kept_low2[step, :, columns] = low2
        kept_slope2[step, :, columns] = slope2
        kept_action[step, :, columns] = jnp.tanh(out + tail[0:8, 0:1])

    staggered([part(columns) for columns in column_parts(TILE, FORWARD_PART)], FORWARD_LAG)


def actor_kernel(
    row_total,
    core_ref,
    states,
    mine,
    other,
    own_critic,
    far_critic,
    own_first,
    far_first,
    own_second,
    far_second,
    mask_actor,
    units_actor,
    mask_critic,
    units_critic,
    actor_second_t,
    actor_third_t,
    kept_low1,
    kept_slope1,
    kept_low2,
    kept_slope2,
    kept_action,
    keep,
    send,
    inputs,
    tail_sums,
    flat,
    gradient,
    spread_critic,
    tails,
    *rest,
):
    judge, judge_back = rest[0:4], (rest[4], rest[5], rest[6], None)
    sums = rest[7:10]
    core = core_ref[0]
    step = pl.program_id(0)
    width = inputs.shape[1]

    @pl.when(step == 0)
    def _():
        start_inputs(inputs)
        clear(sums)
        clear([tail_sums])
        join_halves(core, mine, other, gradient)

        def chosen(part, own, far):
            return jnp.where(core == 0, part(CRITIC, own), part(CRITIC, far))

        def fresh(part, grad):
            return adamw_step(
                chosen(part, own_critic, far_critic),
                grad,
                chosen(part, own_first, far_first),
                chosen(part, own_second, far_second),
            )[0]

        unpack_nets(
            CRITIC,
            [lambda: fresh(body_of, gradient[0 : CRITIC.rows, :])],
            flat,
            mask_critic,
            units_critic,
            spread_critic,
            [judge],
            [judge_back],
        )
        tail = fresh(tail_of, gradient[CRITIC.rows : CRITIC.rows + 1, 0:1])
        tails[8:16, 0:1] = tail_column(tail)

    inputs[0:SDIM, :] = states[...]
    inputs[ACTION_ROW:IN_ROWS, :] = kept_action[step]
    judge_second_t, judge_column, judge_rows, unused = judge_back
    start = jnp.full((HID, LANES), -1.0 / row_total, F32).astype(BF16).astype(F32)
    start = judge_column[...] * start

    def part(columns):
        part_width = columns.stop - columns.start
        joined = inputs[:, columns].astype(BF16)
        action = kept_action[step, :, columns]
        out, judge_slope1, unused, judge_slope2 = yield from forward_kept(judge, joined)
        tail_sums[8:9, columns] += out[0:1] + tails[8:9, 0:1]
        grad2 = (wide(start, part_width) * judge_slope2).astype(BF16)
        yield
        grad_low1 = dot(judge_second_t[...], grad2)
        yield
        grad1 = (grad_low1 * judge_slope1).astype(BF16)
        yield
        grad_action = 2.0 * dot(judge_rows[...], grad1)[8:16]
        grad3 = (grad_action * (1.0 - action * action)).astype(BF16).astype(F32)
        tail_sums[0:8, columns] += grad3
        grad3_low = jnp.concatenate([grad3, jnp.zeros_like(grad3)], axis=0).astype(BF16)
        yield
        grad_low2 = dot(actor_third_t[...], grad3_low)
        yield
        grad2 = (grad_low2 * kept_slope2[step, :, columns]).astype(BF16)
        sums[2][...] += dot_nt(grad3_low, kept_low2[step, :, columns])
        yield
        grad_low1 = dot(actor_second_t[...], grad2)
        yield
        grad1 = (grad_low1 * kept_slope1[step, :, columns]).astype(BF16)
        sums[1][...] += dot_nt(kept_low1[step, :, columns], grad2)
        yield
        sums[0][...] += dot_nt(joined, grad1)

    staggered([part(columns) for columns in column_parts(width, ACTOR_PART)], ACTOR_LAG)

    @pl.when(step == pl.num_programs(0) - 1)
    def _():
        totals = jnp.sum(tail_sums[...], axis=1, keepdims=True)
        lane = iota((8, LANES), 1)
        biases = jnp.where(lane == iota((8, LANES), 0), totals[0:8], 0.0)
        last = jnp.sum(biases, axis=0, keepdims=True)
        last = jnp.where(iota((1, LANES), 1) == 8, -totals[8:9], last)
        write_gradient(ACTOR, sums, last, flat, mask_actor, units_actor)
        split_halves(flat, core, keep, send)


def step_kernel(net, loss_lane, core_ref, *refs):
    *halves, weights, first, second, lagged = refs[:-7]
    new_weights, new_first, new_second, new_lagged, loss, gradient, other_gradient = refs[-7:]
    core = core_ref[0]
    join_halves(core, halves[0], halves[1], gradient)
    if len(halves) > 2:
        join_halves(core, halves[2], halves[3], other_gradient)
        gradient[...] = jnp.where(core == 0, gradient[...], other_gradient[...])
    for part, tail, grad in (
        (body_of, False, gradient[0 : net.rows, :]),
        (tail_of, True, gradient[net.rows : net.rows + 1, 0 : net.out_size]),
    ):
        values = [part(net, source) for source in (weights, first, second)]
        fresh, moment_one, moment_two = adamw_step(values[0], grad, values[1], values[2])
        results = (fresh, moment_one, moment_two, polyak_mix(part(net, lagged), fresh))
        for out, result in zip((new_weights, new_first, new_second, new_lagged), results):
            shape = (1, result.size) if len(out.shape) == 2 else (result.size,)
            out[span_of(net, out, tail)] = result.reshape(shape)
    lane = iota((1, LANES), 1)
    row = gradient[net.rows : net.rows + 1, :]
    loss[0] = jnp.sum(jnp.where(lane == loss_lane, row, 0.0))


def twin_swap(value):
    return lax.ppermute(value, "twin", [(0, 1), (1, 0)])


def to_second(value):
    return lax.ppermute(value, "twin", [(0, 1)])


def chip_masks():
    return [1 << bit for bit in range((lax.axis_size("dp") - 1).bit_length())]


def partner(value, mask):
    pairs = [(source, source ^ mask) for source in range(lax.axis_size("dp"))]
    return lax.ppermute(value, "dp", pairs)


def partner_by_core(value, masks):
    pairs = [
        (2 * source + core, 2 * (source ^ masks[core]) + core)
        for source in range(lax.axis_size("dp"))
        for core in range(2)
    ]
    return lax.ppermute(value, ("dp", "twin"), pairs)


def plus_kernel(left, right, out):
    out[...] = left[...] + right[...]


def plus(left, right):
    vector = pl.BlockSpec(memory_space=pltpu.VMEM)
    return pl.pallas_call(
        plus_kernel,
        in_specs=[vector] * 2,
        out_specs=vector,
        out_shape=jax.ShapeDtypeStruct(left.shape, F32),
        compiler_params=pltpu.CompilerParams(vmem_limit_bytes=SMALL_VMEM_BYTES),
        name="plus",
    )(left, right)


def in_hbm(value):
    return pltpu.with_memory_space_constraint(value, pltpu.HBM)


def whole(unused):
    return pl.BlockSpec(memory_space=pltpu.VMEM)


def on_device(
    states,
    actions,
    rewards,
    next_states,
    done_flags,
    smoothing,
    actor_weights,
    actor_first,
    actor_second,
    critic_weights,
    critic_first,
    critic_second,
    target_actor,
    target_critic,
):
    core = lax.axis_index("twin").astype(jnp.int32).reshape(1)
    local_rows = states.shape[1]
    tiles = local_rows // 2 // TILE
    row_total = local_rows * lax.axis_size("dp")
    rewards = rewards.reshape(1, local_rows)
    done_flags = done_flags.reshape(1, local_rows)
    far_lagged = twin_swap(target_critic)
    far_weights = twin_swap(critic_weights)
    far_first = twin_swap(critic_first)
    far_second = twin_swap(critic_second)
    far_lagged, far_weights, far_first, far_second = lax.optimization_barrier(
        (far_lagged, far_weights, far_first, far_second)
    )

    def mine(rows, tile=None, width=TILE):
        count = local_rows // 2 // width
        return pl.BlockSpec(
            (rows, width),
            lambda i, core_ref: (0, core_ref[0] * count + (i if tile is None else tile)),
        )

    def local(rows, tile=None, width=TILE):
        return pl.BlockSpec((rows, width), lambda i, core_ref: (0, i if tile is None else tile))

    def tile_scratch(width):
        return [
            pltpu.VMEM((IN_ROWS, width), F32),
            pltpu.VMEM((HID + 16, width), BF16),
            pltpu.VMEM((16, width), F32),
            flat,
        ]

    actor_flat = whole((ACTOR.size,))
    critic_flat = whole((1, CRITIC.size))
    half = whole((HALF_ROWS, LANES))
    half_shape = jax.ShapeDtypeStruct((HALF_ROWS, LANES), F32)
    tail_shapes = (((16, TILE), F32),)
    flat = pltpu.VMEM((FLAT_ROWS + 8, LANES), F32)

    def places(kind):
        width = LANES * kind.in_size
        mask = jax.ShapeDtypeStruct((IN_ROWS, width), F32)
        return [mask, jax.ShapeDtypeStruct((width, LANES), BF16)]

    def spread(kind, nets):
        return pltpu.VMEM((2 * IN_ROWS * nets, LANES * kind.in_size), BF16)

    place_specs = [whole(None)] * 2
    net = scratch_of(Weights.shapes)
    back = scratch_of(Weights.back_shapes)
    sums = scratch_of(SUM_SHAPES)
    tails = pltpu.VMEM((32, LANES), F32)
    params = pltpu.CompilerParams(vmem_limit_bytes=VMEM_BYTES)

    def call(
        kernel, steps, in_specs, out_specs, out_shape, scratch, name, flops, aliases=(), vmem=VMEM_BYTES
    ):
        return pl.pallas_call(
            kernel,
            grid_spec=pltpu.PrefetchScalarGridSpec(
                num_scalar_prefetch=1,
                grid=(steps,),
                in_specs=in_specs,
                out_specs=out_specs,
                scratch_shapes=scratch,
            ),
            out_shape=out_shape,
            input_output_aliases=dict(aliases),
            compiler_params=pltpu.CompilerParams(vmem_limit_bytes=vmem),
            cost_estimate=pl.CostEstimate(flops=flops, bytes_accessed=10**6, transcendentals=0),
            name=name,
        )

    unit_flops = 2 * HID * HID * TILE
    passed = Weights.shapes + Weights.back_shapes[0:2] + (((8, LANES), F32),)
    passed_specs = [whole(shape) for shape, dtype in passed]
    passed_shapes = [jax.ShapeDtypeStruct(shape, dtype) for shape, dtype in passed]
    next_action, *places_actor = call(
        action_kernel,
        tiles,
        [mine(SDIM), mine(ADIM), actor_flat],
        [local(ADIM)] + place_specs,
        [jax.ShapeDtypeStruct((ADIM, local_rows // 2), F32)] + places(ACTOR),
        [pltpu.VMEM((IN_ROWS, TILE), F32), flat, spread(ACTOR, 1), tails] + net,
        "next_action",
        2 * tiles * unit_flops,
    )(core, in_hbm(next_states), in_hbm(smoothing), target_actor)
    actor_passed = Weights.shapes + (((8, LANES), F32), Weights.back_shapes[0], Weights.back_shapes[3])
    actor_shapes = [jax.ShapeDtypeStruct(shape, dtype) for shape, dtype in actor_passed]
    target, keep_one, send_one, *rest = call(
        lambda *refs: target_kernel(row_total, *refs),
        local_rows // 2 // TARGET_TILE,
        [mine(rows, None, TARGET_TILE) for rows in (SDIM, ADIM, 1, SDIM, 1)]
        + [local(ADIM, None, TARGET_TILE)]
        + [critic_flat] * 4
        + [actor_flat]
        + place_specs,
        [local(1, None, TARGET_TILE), half, half]
        + place_specs
        + passed_specs
        + [whole(None)] * len(actor_shapes),
        [jax.ShapeDtypeStruct((1, local_rows // 2), F32), half_shape, half_shape]
        + places(CRITIC)
        + passed_shapes
        + actor_shapes,
        tile_scratch(TARGET_TILE)
        + [spread(CRITIC, 4), spread(ACTOR, 1), tails, pltpu.VMEM((IN_ROWS, TARGET_TILE), F32)]
        + net * 3
        + back[0:2]
        + sums,
        "target_and_first_critic",
        14 * tiles * unit_flops,
    )(
        core,
        in_hbm(states),
        in_hbm(actions),
        in_hbm(rewards),
        in_hbm(next_states),
        in_hbm(done_flags),
        next_action,
        target_critic,
        far_lagged,
        critic_weights,
        far_weights,
        actor_weights,
        *places_actor,
    )
    places_critic, critic_two, actor_net = rest[0:2], rest[2 : 2 + len(passed)], rest[2 + len(passed) :]
    kept_shapes = [
        pltpu.VMEM((tiles, rows, TILE), dtype)
        for rows, dtype in ((HID + 16, BF16), (HID, F32), (HID, BF16), (HID, F32), (8, F32))
    ]
    kept_specs = [whole(None)] * len(kept_shapes)

    columns = local_rows // 2
    step_columns = columns // 3 // 512 * 512
    pieces = [(columns - 2 * step_columns, 0)]
    pieces = pieces + [(step_columns, columns - i * step_columns) for i in (2, 1)]
    tail_shapes = (((16, pieces[0][0]), F32),)
    carried = SUM_SHAPES + tail_shapes
    carried_specs = [whole(shape) for shape, dtype in carried]
    carried_shapes = [jax.ShapeDtypeStruct(shape, dtype) for shape, dtype in carried]

    def second_critic(piece, tied_target, state):
        is_first, is_last = piece == 0, piece == len(pieces) - 1
        width, start = pieces[piece]
        operands = [core, states, actions, tied_target, *critic_two]
        scratch = tile_scratch(width)[0:2]
        out_shape = carried_shapes
        if is_last:
            operands = operands + places_critic
            out_shape = [half_shape, half_shape]
            scratch = scratch + sums + scratch_of(tail_shapes) + [flat]
        aliases = []
        if not is_first and not is_last:
            aliases = [(len(operands) + i, i) for i in range(len(state))]
        operands = operands + list(state)
        return call(
            lambda *refs: critic_kernel(row_total, start, width, is_first, is_last, *refs),
            1,
            [whole(None)] * (len(operands) - 1),
            [whole(None)] * len(out_shape),
            out_shape,
            scratch,
            "second_critic",
            8 * unit_flops,
            aliases,
        )(*operands)

    def actor_forward(tied_tail):
        return call(
            forward_kernel,
            tiles,
            [mine(SDIM)] + [whole(None)] * 5,
            kept_specs,
            kept_shapes,
            [pltpu.VMEM((IN_ROWS, TILE), F32)],
            "actor_forward",
            12 * unit_flops,
            vmem=FORWARD_VMEM,
        )(core, states, *actor_net[0:4], tied_tail)

    masks = chip_masks()
    state = ()
    one = keep_one + twin_swap(send_one)
    piece = 0
    for mask, other in zip(masks, masks[len(masks) // 2 :] + masks[: len(masks) // 2]):
        moved = partner_by_core(one, (mask, other))
        if mask == masks[-1]:
            one, tied_tail = lax.optimization_barrier((one, actor_net[4]))
            kept = actor_forward(tied_tail)
            *kept, last = kept
            one, last = lax.optimization_barrier((plus(one, moved), last))
            kept = [*kept, last]
        elif piece < len(pieces):
            one, tied_target = lax.optimization_barrier((one, target))
            state = second_critic(piece, tied_target, state)
            piece += 1
            one, state = lax.optimization_barrier((one + moved, state))
        else:
            one = one + moved
    while piece < len(pieces):
        state = second_critic(piece, target, state)
        piece += 1
    keep_two, send_two = state
    one_other = twin_swap(one)
    two = plus(keep_two, twin_swap(send_two))
    two_moved = partner(two, masks[-1])
    two, one, one_other = lax.optimization_barrier((two, one, one_other))
    keep_actor, send_actor = call(
        lambda *refs: actor_kernel(row_total, *refs),
        tiles,
        [mine(SDIM), half, half]
        + [critic_flat] * 6
        + place_specs * 2
        + [whole(None)] * 2
        + kept_specs,
        [half, half],
        [half_shape, half_shape],
        [tile_scratch(TILE)[i] for i in (0, 2, 3)]
        + [pltpu.VMEM((FLAT_ROWS, LANES), F32), spread(CRITIC, 1), tails]
        + net
        + back[0:3]
        + sums,
        "actor",
        8 * tiles * unit_flops,
        vmem=ACTOR_VMEM,
    )(
        core,
        states,
        one,
        one_other,
        critic_weights,
        far_weights,
        critic_first,
        far_first,
        critic_second,
        far_second,
        *places_actor,
        *places_critic,
        *actor_net[5:7],
        *[pltpu.with_memory_space_constraint(value, pltpu.VMEM) for value in kept],
    )
    actor_moved = twin_swap(send_actor)
    two = two + two_moved
    two, keep_actor, actor_moved = lax.optimization_barrier((two, keep_actor, actor_moved))
    actor = keep_actor + actor_moved
    turned = masks[len(masks) // 2 :] + masks[: len(masks) // 2]
    later = masks[:-1]
    for index, pair in enumerate(zip(masks, turned)):
        moved = partner_by_core(actor, pair)
        if index < len(later):
            two = two + partner(two, later[index - 1])
        actor = actor + moved
    actor_other = twin_swap(actor)
    two_other = to_second(two)

    def step(net, loss_lane, halves, sources, name):
        vector = pl.BlockSpec(memory_space=pltpu.VMEM)
        scalar = pl.BlockSpec(memory_space=pltpu.SMEM)
        return pl.pallas_call(
            lambda *refs: step_kernel(net, loss_lane, *refs),
            in_specs=[scalar] + [vector] * (len(halves) + len(sources)),
            out_specs=[vector] * len(sources) + [scalar],
            out_shape=[jax.ShapeDtypeStruct(source.shape, F32) for source in sources]
            + [jax.ShapeDtypeStruct((1,), F32)],
            scratch_shapes=[pltpu.VMEM((FLAT_ROWS, LANES), F32)] * 2,
            compiler_params=params,
            name=name,
        )(core, *halves, *sources)

    new_critic, new_critic_first, new_critic_second, new_target_critic, critic_loss = step(
        CRITIC,
        1,
        (one, one_other, two, two_other),
        (critic_weights, critic_first, critic_second, target_critic),
        "critic_step",
    )
    new_actor, new_actor_first, new_actor_second, new_target_actor, actor_loss = step(
        ACTOR,
        8,
        (actor, actor_other),
        (actor_weights, actor_first, actor_second, target_actor),
        "actor_step",
    )
    return (
        new_actor,
        new_actor_first,
        new_actor_second,
        new_critic,
        new_critic_first,
        new_critic_second,
        new_target_actor,
        new_target_critic,
        critic_loss,
        actor_loss.reshape(()),
    )


def solution(mesh):
    columns = P(None, "dp")
    critic = P("twin", None)
    return jax.shard_map(
        on_device,
        mesh=mesh,
        in_specs=(
            columns,
            columns,
            P("dp"),
            columns,
            P("dp"),
            columns,
            P(),
            P(),
            P(),
            critic,
            critic,
            critic,
            P(),
            critic,
        ),
        out_specs=(P(), P(), P(), critic, critic, critic, P(), critic, P("twin"), P()),
        check_vma=False,
    )
```

```python
import jax
import jax.numpy as jnp
from jax import lax
from jax.experimental import pallas as pl
from jax.experimental.pallas import tpu as pltpu
from jax.sharding import PartitionSpec as P

SDIM = 17
ADIM = 6
HID = 256
STEP = 10

DISCOUNT = 0.99
POLYAK_RATE = 0.005
LEARN_RATE = 0.05
BETA_ONE = 0.9
BETA_TWO = 0.999
EPSILON = 1e-08
WEIGHT_DECAY = 0.01
NOISE_SCALE = 0.2
NOISE_CLIP = 0.5

LANES = 128
TILE = 2048
ACTION_PART = 2048
LAG = 1
TARGET_TILE = 2048
TARGET_PART = 2048
TARGET_LAG = 1
CRITIC_PART = 1024
CRITIC_LAG = 3
FORWARD_PART = 2048
FORWARD_LAG = 1
ACTOR_PART = 1024
ACTOR_LAG = 3
ONES_ROW = 17
ACTION_ROW = 24
IN_ROWS = 32
FLAT_ROWS = 576
HALF_ROWS = FLAT_ROWS // 2
VMEM_BYTES = 24 * 2**20
SMALL_VMEM_BYTES = 2**21
FORWARD_VMEM = 8 * 2**20
ACTOR_VMEM = 16 * 2**20

F32 = jnp.float32
BF16 = jnp.bfloat16


class Net:
    def __init__(self, in_size, out_size):
        self.in_size = in_size
        self.out_size = out_size
        self.bias1 = 2 * in_size
        self.weight2 = self.bias1 + 2
        self.bias2 = self.weight2 + 2 * HID
        self.weight3 = self.bias2 + 2
        self.rows = self.weight3 + 2 * out_size
        self.size = self.rows * LANES + out_size


ACTOR = Net(SDIM, ADIM)
CRITIC = Net(SDIM + ADIM, 1)


def dot(a, b):
    return jnp.dot(a, b, preferred_element_type=F32)


def dot_nt(a, b):
    return lax.dot_general(a, b, (((1,), (1,)), ((), ())), preferred_element_type=F32)


def wide(column, width):
    return jnp.concatenate([column] * (width // LANES), axis=1)


def iota(shape, axis):
    return lax.broadcasted_iota(jnp.int32, shape, axis)


def rows_to_lanes(block):
    return jnp.concatenate([block[row : row + 1] for row in range(block.shape[0])], axis=1)


def place_mask(net):
    width = LANES * net.in_size
    position = iota((8, width), 1).astype(F32)
    phase = position - net.in_size * jnp.floor((position + 0.5) * (1.0 / net.in_size))
    blocks = []
    for start in range(0, IN_ROWS, 8):
        row = iota((8, width), 0) + start
        source = jnp.where(row < SDIM, row, jnp.where(row >= ACTION_ROW, row - ACTION_ROW + SDIM, -1))
        source = jnp.where(source < net.in_size, source, -1).astype(F32)
        blocks.append(jnp.where(phase == source, 1.0, 0.0))
    return jnp.concatenate(blocks, axis=0)


def place_units(net):
    shape = (LANES * net.in_size, LANES)
    gap = iota(shape, 0) - net.in_size * iota(shape, 1)
    return jnp.where(gap.astype(jnp.uint32) < net.in_size, 1.0, 0.0).astype(BF16)


def three_parts(value):
    high = value.astype(BF16).astype(F32)
    rest = value - high
    middle = rest.astype(BF16).astype(F32)
    return high, middle, rest - middle


def spread_first(net, flat, mask, spread, slot):
    for half in range(2):
        pieces = [
            jnp.broadcast_to(
                flat[half * net.in_size + row : half * net.in_size + row + 1, :],
                (IN_ROWS, LANES),
            )
            for row in range(net.in_size)
        ]
        start = (2 * slot + half) * IN_ROWS
        spread[start : start + IN_ROWS, :] = (
            jnp.concatenate(pieces, axis=1) * mask[...]
        ).astype(BF16)


def gather_first(spread, units, nets):
    gathered = dot(spread[0 : 2 * IN_ROWS * nets, :], units[...])
    halves = [gathered[i * IN_ROWS : (i + 1) * IN_ROWS] for i in range(2 * nets)]
    return [jnp.concatenate(halves[2 * i : 2 * i + 2], axis=1) for i in range(nets)]


def flatten_first(net, transposed, out, mask, units):
    blocks = [transposed[:, 0:LANES], transposed[:, LANES:HID]]
    parts = [part for block in blocks for part in three_parts(block)]
    spread = dot_nt(jnp.concatenate(parts, axis=0).astype(BF16), units[...])
    for half in range(2):
        high, middle, low = [
            spread[(3 * half + part) * IN_ROWS : (3 * half + part + 1) * IN_ROWS]
            for part in range(3)
        ]
        total = (high + (middle + low)) * mask[...]
        line = jnp.sum(total, axis=0, keepdims=True)
        for row in range(net.in_size):
            target = half * net.in_size + row
            out[target : target + 1, :] = line[:, row * LANES : (row + 1) * LANES]


def as_column(row):
    return jnp.transpose(jnp.broadcast_to(row, (LANES, HID)))


def flat_row(flat, start):
    return jnp.concatenate([flat[start : start + 1, :], flat[start + 1 : start + 2, :]], axis=1)


class Weights:
    shapes = (
        ((HID, IN_ROWS), BF16),
        ((HID, HID), BF16),
        ((HID, LANES), F32),
        ((16, HID), BF16),
    )
    back_shapes = (
        ((HID, HID), BF16),
        ((HID, LANES), F32),
        ((16, HID), BF16),
        ((HID, 16), BF16),
    )


def scratch_of(shapes):
    return [pltpu.VMEM(shape, dtype) for shape, dtype in shapes]


def unpack_first(net, first_t, bias1, refs, back=None):
    first_t = 0.5 * first_t
    row = iota((IN_ROWS, HID), 0)
    for part, value in enumerate(three_parts(0.5 * bias1)):
        first_t = jnp.where(row == ONES_ROW + part, value, first_t)
    refs[0][...] = jnp.transpose(first_t).astype(BF16)
    if back is not None and back[2] is not None:
        back[2][...] = first_t[16:32].astype(BF16)


def unpack_rest(net, flat, refs, back=None):
    first, second, bias2, third = refs
    left = flat[pl.ds(net.weight2, HID, stride=2), :]
    right = flat[pl.ds(net.weight2 + 1, HID, stride=2), :]
    second_value = 0.5 * jnp.concatenate([left, right], axis=1)
    second[...] = second_value.astype(BF16)
    bias2[...] = as_column(0.5 * flat_row(flat, net.bias2))
    left = flat[pl.ds(net.weight3, 8, stride=2), :]
    right = flat[pl.ds(net.weight3 + 1, 8, stride=2), :]
    third_value = jnp.concatenate([left, right], axis=1)
    third_value = jnp.where(iota((8, HID), 0) < net.out_size, third_value, 0.0)
    third_value = jnp.concatenate([third_value, jnp.zeros((8, HID), F32)], axis=0)
    third[...] = third_value.astype(BF16)
    if back is not None:
        second_t, third_column, unused, third_t = back
        second_t[...] = jnp.transpose(second_value).astype(BF16)
        third_low = 0.5 * third_value.astype(BF16).astype(F32)
        if third_column is not None:
            third_column[...] = as_column(third_low[0:1])
        if third_t is not None:
            third_t[...] = jnp.transpose(third_low).astype(BF16)


def unpack_nets(net, values, flat, mask, units, spread, refs, backs):
    biases = []
    for slot, (value, net_refs, back) in enumerate(zip(values, refs, backs)):
        load_flat(net, flat, value())
        spread_first(net, flat, mask, spread, slot)
        biases.append(flat_row(flat, net.bias1))
        unpack_rest(net, flat, net_refs, back)
    firsts = gather_first(spread, units, len(values))
    for first_t, bias1, net_refs, back in zip(firsts, biases, refs, backs):
        unpack_first(net, first_t, bias1, net_refs, back)


def load_flat(net, flat, value):
    flat[0 : net.rows, :] = value
    flat[net.rows : FLAT_ROWS, :] = jnp.zeros((FLAT_ROWS - net.rows, LANES), F32)


def span_of(net, ref, tail):
    where = pl.ds(net.rows * LANES, net.out_size) if tail else pl.ds(0, net.rows * LANES)
    return (where,) if len(ref.shape) == 1 else (slice(0, 1), where)


def body_of(net, ref):
    return ref[span_of(net, ref, False)].reshape(net.rows, LANES)


def tail_of(net, ref):
    return ref[span_of(net, ref, True)].reshape(1, net.out_size)


def tail_column(tail):
    size = tail.shape[1]
    eye = iota((8, size), 0) == iota((8, size), 1)
    return jnp.sum(jnp.where(eye, jnp.broadcast_to(tail, (8, size)), 0.0), axis=1, keepdims=True)


def start_inputs(inputs):
    inputs[...] = jnp.zeros_like(inputs)
    row = iota((8, inputs.shape[1]), 0) + 16
    inputs[16:24, :] = jnp.where((row >= ONES_ROW) & (row < ONES_ROW + 3), 1.0, 0.0)


def staggered(parts, lag):
    parts = list(parts)
    step = 0
    while any(part is not None for part in parts):
        for index, part in enumerate(parts):
            if part is not None and step >= index * lag:
                try:
                    next(part)
                except StopIteration:
                    parts[index] = None
        step += 1


def column_parts(width, size):
    return [slice(start, start + size) for start in range(0, width, size)]


def silu_low(half_pre):
    wave = jnp.tanh(half_pre)
    return (half_pre * wave + half_pre).astype(BF16)


def silu_and_slope(half_pre):
    wave = jnp.tanh(half_pre)
    above = 1.0 + wave
    hidden = half_pre * above
    return hidden.astype(BF16), above + hidden * (1.0 - wave)


def forward(refs, inputs):
    first, second, bias2, third = refs
    width = inputs.shape[1]
    pre = dot(first[...], inputs)
    yield
    hidden = silu_low(pre)
    yield
    pre = dot(second[...], hidden)
    yield
    hidden = silu_low(pre + wide(bias2[...], width))
    yield
    return dot(third[...], hidden)[0:8]


def forward_kept(refs, inputs, hidden1=None):
    first, second, bias2, third = refs
    width = inputs.shape[1]
    pre = dot(first[...], inputs)
    yield
    low1, slope1 = silu_and_slope(pre)
    if hidden1 is not None:
        hidden1[0:HID, :] = low1
    yield
    pre = dot(second[...], low1)
    yield
    low2, slope2 = silu_and_slope(pre + wide(bias2[...], width))
    yield
    return dot(third[...], low2)[0:8], slope1, low2, slope2


def write_gradient(net, sums, last_row, flat, mask, units):
    sum1, sum2, sum3 = sums
    flatten_first(net, sum1[...], flat, mask, units)
    bias1 = sum1[ONES_ROW : ONES_ROW + 1, :]
    bias2 = sum2[HID : HID + 1, :]
    weight2 = jnp.transpose(sum2[0:HID, :])
    for side in range(2):
        lanes = slice(side * LANES, (side + 1) * LANES)
        flat[net.bias1 + side : net.bias1 + side + 1, :] = bias1[:, lanes]
        flat[pl.ds(net.weight2 + side, HID, stride=2), :] = weight2[:, lanes]
        flat[net.bias2 + side : net.bias2 + side + 1, :] = bias2[:, lanes]
        for unit in range(net.out_size):
            row = net.weight3 + 2 * unit + side
            flat[row : row + 1, :] = sum3[unit : unit + 1, lanes]
    flat[net.rows : net.rows + 1, :] = last_row
    rest = FLAT_ROWS - net.rows - 1
    flat[net.rows + 1 : FLAT_ROWS, :] = jnp.zeros((rest, LANES), F32)


def split_halves(flat, core, keep, send):
    low = flat[0:HALF_ROWS, :]
    high = flat[HALF_ROWS:FLAT_ROWS, :]
    keep[...] = jnp.where(core == 0, low, high)
    send[...] = jnp.where(core == 0, high, low)


def join_halves(core, mine, other, flat):
    flat[0:HALF_ROWS, :] = jnp.where(core == 0, mine[...], other[...])
    flat[HALF_ROWS:FLAT_ROWS, :] = jnp.where(core == 0, other[...], mine[...])


def adamw_step(weight, gradient, moment_one, moment_two):
    moment_one = BETA_ONE * moment_one + (1.0 - BETA_ONE) * gradient
    moment_two = BETA_TWO * moment_two + (1.0 - BETA_TWO) * gradient * gradient
    corrected_one = moment_one / (1.0 - BETA_ONE**STEP)
    corrected_two = moment_two / (1.0 - BETA_TWO**STEP)
    weight = weight - LEARN_RATE * (
        corrected_one / (jnp.sqrt(corrected_two) + EPSILON) + WEIGHT_DECAY * weight
    )
    return (weight, moment_one, moment_two)


def polyak_mix(lagged, fresh):
    return POLYAK_RATE * fresh + (1.0 - POLYAK_RATE) * lagged


def clear(refs):
    for ref in refs:
        ref[...] = jnp.zeros_like(ref)


SUM_SHAPES = (((IN_ROWS, HID), F32), ((HID + 16, HID), F32), ((16, HID), F32))


def critic_part(refs, back, bias3, inputs, target, scale, hidden1, sums, tail_sums):
    second_t, third_column = back[0], back[1]
    width = inputs.shape[1]
    out, slope1, low2, slope2 = yield from forward_kept(refs, inputs, hidden1)
    error = out[0:1] + bias3 - target
    grad3 = (scale * error).astype(BF16).astype(F32)
    tail_sums[0:1, :] += grad3
    tail_sums[1:2, :] += error * error
    yield
    grad2 = (wide(third_column[...], width) * grad3 * slope2).astype(BF16)
    sums[2][...] += dot_nt(jnp.broadcast_to(grad3, (16, width)).astype(BF16), low2)
    yield
    grad_low1 = dot(second_t[...], grad2)
    yield
    grad1 = (grad_low1 * slope1).astype(BF16)
    sums[1][...] += dot_nt(hidden1[...], grad2)
    yield
    sums[0][...] += dot_nt(inputs, grad1)


def critic_last_row(tail_sums):
    totals = jnp.sum(tail_sums[...], axis=1, keepdims=True)
    lane = iota((1, LANES), 1)
    return jnp.where(lane == 0, totals[0:1], jnp.where(lane == 1, totals[1:2], 0.0))


def action_kernel(
    core_ref,
    next_states,
    smoothing,
    target_actor,
    joined,
    mask_actor,
    units_actor,
    inputs,
    flat,
    spread,
    tails,
    *actor,
):
    step = pl.program_id(0)

    @pl.when(step == 0)
    def _():
        start_inputs(inputs)
        units_actor[...] = place_units(ACTOR)
        mask_actor[...] = place_mask(ACTOR)
        unpack_nets(
            ACTOR,
            [lambda: body_of(ACTOR, target_actor)],
            flat,
            mask_actor,
            units_actor,
            spread,
            [actor],
            [None],
        )
        tails[0:8, 0:1] = tail_column(tail_of(ACTOR, target_actor))

    inputs[0:SDIM, :] = next_states[...]

    def part(columns):
        out = yield from forward(actor, inputs[:, columns].astype(BF16))
        lagged_action = jnp.tanh(out + tails[0:8, 0:1])
        jitter = jnp.clip(NOISE_SCALE * smoothing[:, columns], -NOISE_CLIP, NOISE_CLIP)
        next_action = jnp.clip(lagged_action[0:ADIM] + jitter, -1.0, 1.0)
        inputs[ACTION_ROW : ACTION_ROW + ADIM, columns] = next_action
        joined[:, columns] = inputs[:, columns].astype(BF16)

    staggered([part(columns) for columns in column_parts(TILE, ACTION_PART)], LAG)


def target_kernel(
    row_total,
    core_ref,
    states,
    actions,
    rewards,
    done_flags,
    next_joined,
    own_lagged,
    far_lagged,
    own_critic,
    far_critic,
    actor_weights,
    mask_actor,
    units_actor,
    target_out,
    keep,
    send,
    mask_critic,
    units_critic,
    *rest,
):
    next_critic, next_second_t, next_column, next_tail = rest[0:4], rest[4], rest[5], rest[6]
    actor, actor_tail, actor_second_t, actor_third_t = rest[7:11], rest[11], rest[12], rest[13]
    rest = rest[14:]
    inputs, hidden1, tail_sums, flat, spread, spread_actor, tails = rest[0:7]
    lag_one, lag_two, critic = rest[7:11], rest[11:15], rest[15:19]
    back = (rest[19], rest[20], None, None)
    sums = rest[21:24]
    core = core_ref[0]
    step = pl.program_id(0)
    width = inputs.shape[1]

    @pl.when(step == 0)
    def _():
        start_inputs(inputs)
        hidden1[HID : HID + 16, :] = jnp.ones((16, width), BF16)
        clear(sums)
        clear([tail_sums])
        units_critic[...] = place_units(CRITIC)
        mask_critic[...] = place_mask(CRITIC)

        def chosen(part, holder):
            return jnp.where(core == holder, part(CRITIC, own_critic), part(CRITIC, far_critic))

        unpack_nets(
            CRITIC,
            [
                lambda: body_of(CRITIC, own_lagged),
                lambda: body_of(CRITIC, far_lagged),
                lambda: chosen(body_of, 0),
                lambda: chosen(body_of, 1),
            ],
            flat,
            mask_critic,
            units_critic,
            spread,
            [lag_one, lag_two, critic, next_critic],
            [None, None, back, (next_second_t, next_column, None, None)],
        )
        tails[8:16, 0:1] = tail_column(tail_of(CRITIC, own_lagged))
        tails[16:24, 0:1] = tail_column(tail_of(CRITIC, far_lagged))
        tails[24:32, 0:1] = tail_column(chosen(tail_of, 0))
        next_tail[...] = jnp.broadcast_to(tail_column(chosen(tail_of, 1)), (8, LANES))
        unpack_nets(
            ACTOR,
            [lambda: body_of(ACTOR, actor_weights)],
            flat,
            mask_actor,
            units_actor,
            spread_actor,
            [actor],
            [(actor_second_t, None, None, actor_third_t)],
        )
        tail = tail_column(tail_of(ACTOR, actor_weights))
        actor_tail[...] = jnp.broadcast_to(tail, (8, LANES))

    own = core * target_out.shape[1] + step * width

    def span(start, columns):
        start = pl.multiple_of(start + columns.start, LANES)
        return pl.ds(start, columns.stop - columns.start)

    tile = span(own, slice(0, width))
    inputs[0:SDIM, :] = states[:, tile]
    inputs[ACTION_ROW : ACTION_ROW + ADIM, :] = actions[:, tile]

    def part(columns):
        joined = next_joined[:, span(step * width, columns)]
        out_one = yield from forward(lag_one, joined)
        yield
        out_two = yield from forward(lag_two, joined)
        value_one = out_one[0:1] + tails[8:9, 0:1]
        value_two = out_two[0:1] + tails[16:17, 0:1]
        keep_going = 1.0 - done_flags[:, span(own, columns)].astype(F32)
        lagged = jnp.minimum(value_one, value_two)
        target = rewards[:, span(own, columns)] + DISCOUNT * keep_going * lagged
        target_out[:, span(step * width, columns)] = target

    def next_part(columns):
        return critic_part(
            critic,
            back,
            tails[24:25, 0:1],
            inputs[:, columns].astype(BF16),
            target_out[:, span(step * width, columns)],
            2.0 / row_total,
            hidden1.at[:, columns],
            sums,
            tail_sums.at[:, columns],
        )

    staggered([part(columns) for columns in column_parts(width, TARGET_PART)], TARGET_LAG)
    staggered([next_part(columns) for columns in column_parts(width, CRITIC_PART)], CRITIC_LAG)

    @pl.when(step == pl.num_programs(0) - 1)
    def _():
        last = critic_last_row(tail_sums)
        write_gradient(CRITIC, sums, last, flat, mask_critic, units_critic)
        split_halves(flat, core, keep, send)


def critic_kernel(row_total, start, width, is_first, is_last, core_ref, *refs):
    states, actions, target = refs[0:3]
    critic, second_t, third_column, tail = refs[3:7], refs[7], refs[8], refs[9]
    refs = refs[10:]
    if is_last:
        mask, units = refs[0:2]
        refs = refs[2:]
    before = ()
    if not is_first:
        before = refs[0:4]
        refs = refs[4:]
    if is_last:
        keep, send, inputs, hidden1 = refs[0:4]
        sums, tail_sums, flat = refs[4:7], refs[7], refs[8]
    else:
        sums, tail_sums, inputs, hidden1 = refs[0:3], refs[3], refs[4], refs[5]
    start_inputs(inputs)
    hidden1[HID : HID + 16, :] = jnp.ones((16, width), BF16)
    if is_first:
        clear([*sums, tail_sums])
    for after, value in zip([*sums, tail_sums], before):
        after[...] = value[...]
    first_column = pl.multiple_of(core_ref[0] * target.shape[1] + start, LANES)
    inputs[0:SDIM, :] = states[:, pl.ds(first_column, width)]
    inputs[ACTION_ROW : ACTION_ROW + ADIM, :] = actions[:, pl.ds(first_column, width)]

    def part(columns):
        return critic_part(
            critic,
            (second_t, third_column),
            tail[0:1, 0:1],
            inputs[:, columns].astype(BF16),
            target[:, start + columns.start : start + columns.stop],
            2.0 / row_total,
            hidden1.at[:, columns],
            sums,
            tail_sums.at[:, columns],
        )

    staggered([part(columns) for columns in column_parts(width, width // 2)], CRITIC_LAG)
    if is_last:
        last = critic_last_row(tail_sums)
        write_gradient(CRITIC, sums, last, flat, mask, units)
        split_halves(flat, core_ref[0], keep, send)


def forward_kernel(
    core_ref,
    states,
    first,
    second,
    bias2,
    third,
    tail,
    kept_low1,
    kept_slope1,
    kept_low2,
    kept_slope2,
    kept_action,
    inputs,
):
    step = pl.program_id(0)

    @pl.when(step == 0)
    def _():
        start_inputs(inputs)

    columns = TILE * pl.num_programs(0)
    first_column = pl.multiple_of(core_ref[0] * columns + step * TILE, LANES)
    inputs[0:SDIM, :] = states[:, pl.ds(first_column, TILE)]
    kept_low1[step, HID : HID + 16, :] = jnp.ones((16, TILE), BF16)

    def part(columns):
        out, slope1, low2, slope2 = yield from forward_kept(
            (first, second, bias2, third),
            inputs[:, columns].astype(BF16),
            kept_low1.at[step, :, columns],
        )
        kept_slope1[step, :, columns] = slope1
        kept_low2[step, :, columns] = low2
        kept_slope2[step, :, columns] = slope2
        kept_action[step, :, columns] = jnp.tanh(out + tail[0:8, 0:1])

    staggered([part(columns) for columns in column_parts(TILE, FORWARD_PART)], FORWARD_LAG)


def actor_kernel(
    row_total,
    core_ref,
    states,
    mine,
    other,
    own_critic,
    far_critic,
    own_first,
    far_first,
    own_second,
    far_second,
    mask_actor,
    units_actor,
    mask_critic,
    units_critic,
    actor_second_t,
    actor_third_t,
    kept_low1,
    kept_slope1,
    kept_low2,
    kept_slope2,
    kept_action,
    keep,
    send,
    inputs,
    tail_sums,
    flat,
    gradient,
    spread_critic,
    tails,
    *rest,
):
    judge, judge_back = rest[0:4], (rest[4], rest[5], rest[6], None)
    sums = rest[7:10]
    core = core_ref[0]
    step = pl.program_id(0)
    width = inputs.shape[1]

    @pl.when(step == 0)
    def _():
        start_inputs(inputs)
        clear(sums)
        clear([tail_sums])
        join_halves(core, mine, other, gradient)

        def chosen(part, own, far):
            return jnp.where(core == 0, part(CRITIC, own), part(CRITIC, far))

        def fresh(part, grad):
            return adamw_step(
                chosen(part, own_critic, far_critic),
                grad,
                chosen(part, own_first, far_first),
                chosen(part, own_second, far_second),
            )[0]

        unpack_nets(
            CRITIC,
            [lambda: fresh(body_of, gradient[0 : CRITIC.rows, :])],
            flat,
            mask_critic,
            units_critic,
            spread_critic,
            [judge],
            [judge_back],
        )
        tail = fresh(tail_of, gradient[CRITIC.rows : CRITIC.rows + 1, 0:1])
        tails[8:16, 0:1] = tail_column(tail)

    columns = width * pl.num_programs(0)
    first_column = pl.multiple_of(core * columns + step * width, LANES)
    inputs[0:SDIM, :] = states[:, pl.ds(first_column, width)]
    inputs[ACTION_ROW:IN_ROWS, :] = kept_action[step]
    judge_second_t, judge_column, judge_rows, unused = judge_back
    start = jnp.full((HID, LANES), -1.0 / row_total, F32).astype(BF16).astype(F32)
    start = judge_column[...] * start

    def part(columns):
        part_width = columns.stop - columns.start
        joined = inputs[:, columns].astype(BF16)
        action = kept_action[step, :, columns]
        out, judge_slope1, unused, judge_slope2 = yield from forward_kept(judge, joined)
        tail_sums[8:9, columns] += out[0:1] + tails[8:9, 0:1]
        grad2 = (wide(start, part_width) * judge_slope2).astype(BF16)
        yield
        grad_low1 = dot(judge_second_t[...], grad2)
        yield
        grad1 = (grad_low1 * judge_slope1).astype(BF16)
        yield
        grad_action = 2.0 * dot(judge_rows[...], grad1)[8:16]
        grad3 = (grad_action * (1.0 - action * action)).astype(BF16).astype(F32)
        tail_sums[0:8, columns] += grad3
        grad3_low = jnp.concatenate([grad3, jnp.zeros_like(grad3)], axis=0).astype(BF16)
        yield
        grad_low2 = dot(actor_third_t[...], grad3_low)
        yield
        grad2 = (grad_low2 * kept_slope2[step, :, columns]).astype(BF16)
        sums[2][...] += dot_nt(grad3_low, kept_low2[step, :, columns])
        yield
        grad_low1 = dot(actor_second_t[...], grad2)
        yield
        grad1 = (grad_low1 * kept_slope1[step, :, columns]).astype(BF16)
        sums[1][...] += dot_nt(kept_low1[step, :, columns], grad2)
        yield
        sums[0][...] += dot_nt(joined, grad1)

    staggered([part(columns) for columns in column_parts(width, ACTOR_PART)], ACTOR_LAG)

    @pl.when(step == pl.num_programs(0) - 1)
    def _():
        totals = jnp.sum(tail_sums[...], axis=1, keepdims=True)
        lane = iota((8, LANES), 1)
        biases = jnp.where(lane == iota((8, LANES), 0), totals[0:8], 0.0)
        last = jnp.sum(biases, axis=0, keepdims=True)
        last = jnp.where(iota((1, LANES), 1) == 8, -totals[8:9], last)
        write_gradient(ACTOR, sums, last, flat, mask_actor, units_actor)
        split_halves(flat, core, keep, send)


def step_kernel(net, loss_lane, core_ref, *refs):
    *halves, weights, first, second, lagged = refs[:-7]
    new_weights, new_first, new_second, new_lagged, loss, gradient, other_gradient = refs[-7:]
    core = core_ref[0]
    join_halves(core, halves[0], halves[1], gradient)
    if len(halves) > 2:
        join_halves(core, halves[2], halves[3], other_gradient)
        gradient[...] = jnp.where(core == 0, gradient[...], other_gradient[...])
    for part, tail, grad in (
        (body_of, False, gradient[0 : net.rows, :]),
        (tail_of, True, gradient[net.rows : net.rows + 1, 0 : net.out_size]),
    ):
        values = [part(net, source) for source in (weights, first, second)]
        fresh, moment_one, moment_two = adamw_step(values[0], grad, values[1], values[2])
        results = (fresh, moment_one, moment_two, polyak_mix(part(net, lagged), fresh))
        for out, result in zip((new_weights, new_first, new_second, new_lagged), results):
            shape = (1, result.size) if len(out.shape) == 2 else (result.size,)
            out[span_of(net, out, tail)] = result.reshape(shape)
    lane = iota((1, LANES), 1)
    row = gradient[net.rows : net.rows + 1, :]
    loss[0] = jnp.sum(jnp.where(lane == loss_lane, row, 0.0))


def twin_swap(value):
    return lax.ppermute(value, "twin", [(0, 1), (1, 0)])


def to_second(value):
    return lax.ppermute(value, "twin", [(0, 1)])


def chip_masks():
    return [1 << bit for bit in range((lax.axis_size("dp") - 1).bit_length())]


def partner(value, mask):
    pairs = [(source, source ^ mask) for source in range(lax.axis_size("dp"))]
    return lax.ppermute(value, "dp", pairs)


def partner_by_core(value, masks):
    pairs = [
        (2 * source + core, 2 * (source ^ masks[core]) + core)
        for source in range(lax.axis_size("dp"))
        for core in range(2)
    ]
    return lax.ppermute(value, ("dp", "twin"), pairs)


def plus_kernel(left, right, out):
    out[...] = left[...] + right[...]


def plus(left, right):
    vector = pl.BlockSpec(memory_space=pltpu.VMEM)
    return pl.pallas_call(
        plus_kernel,
        in_specs=[vector] * 2,
        out_specs=vector,
        out_shape=jax.ShapeDtypeStruct(left.shape, F32),
        compiler_params=pltpu.CompilerParams(vmem_limit_bytes=SMALL_VMEM_BYTES),
        name="plus",
    )(left, right)


def in_hbm(value):
    return pltpu.with_memory_space_constraint(value, pltpu.HBM)


def whole(unused):
    return pl.BlockSpec(memory_space=pltpu.VMEM)


def on_device(
    states,
    actions,
    rewards,
    next_states,
    done_flags,
    smoothing,
    actor_weights,
    actor_first,
    actor_second,
    critic_weights,
    critic_first,
    critic_second,
    target_actor,
    target_critic,
):
    core = lax.axis_index("twin").astype(jnp.int32).reshape(1)
    local_rows = states.shape[1]
    tiles = local_rows // 2 // TILE
    row_total = local_rows * lax.axis_size("dp")
    rewards = rewards.reshape(1, local_rows)
    done_flags = done_flags.reshape(1, local_rows)
    far_lagged = twin_swap(target_critic)
    far_weights = twin_swap(critic_weights)
    far_first = twin_swap(critic_first)
    far_second = twin_swap(critic_second)
    far_lagged, far_weights, far_first, far_second = lax.optimization_barrier(
        (far_lagged, far_weights, far_first, far_second)
    )

    def mine(rows, tile=None, width=TILE):
        count = local_rows // 2 // width
        return pl.BlockSpec(
            (rows, width),
            lambda i, core_ref: (0, core_ref[0] * count + (i if tile is None else tile)),
        )

    def local(rows, tile=None, width=TILE):
        return pl.BlockSpec((rows, width), lambda i, core_ref: (0, i if tile is None else tile))

    def tile_scratch(width):
        return [
            pltpu.VMEM((IN_ROWS, width), F32),
            pltpu.VMEM((HID + 16, width), BF16),
            pltpu.VMEM((16, width), F32),
            flat,
        ]

    actor_flat = whole((ACTOR.size,))
    critic_flat = whole((1, CRITIC.size))
    half = whole((HALF_ROWS, LANES))
    half_shape = jax.ShapeDtypeStruct((HALF_ROWS, LANES), F32)
    tail_shapes = (((16, TILE), F32),)
    flat = pltpu.VMEM((FLAT_ROWS + 8, LANES), F32)

    def places(kind):
        width = LANES * kind.in_size
        mask = jax.ShapeDtypeStruct((IN_ROWS, width), F32)
        return [mask, jax.ShapeDtypeStruct((width, LANES), BF16)]

    def spread(kind, nets):
        return pltpu.VMEM((2 * IN_ROWS * nets, LANES * kind.in_size), BF16)

    place_specs = [whole(None)] * 2
    net = scratch_of(Weights.shapes)
    back = scratch_of(Weights.back_shapes)
    sums = scratch_of(SUM_SHAPES)
    tails = pltpu.VMEM((32, LANES), F32)
    params = pltpu.CompilerParams(vmem_limit_bytes=VMEM_BYTES)

    def call(
        kernel, steps, in_specs, out_specs, out_shape, scratch, name, flops, aliases=(), vmem=VMEM_BYTES
    ):
        return pl.pallas_call(
            kernel,
            grid_spec=pltpu.PrefetchScalarGridSpec(
                num_scalar_prefetch=1,
                grid=(steps,),
                in_specs=in_specs,
                out_specs=out_specs,
                scratch_shapes=scratch,
            ),
            out_shape=out_shape,
            input_output_aliases=dict(aliases),
            compiler_params=pltpu.CompilerParams(vmem_limit_bytes=vmem),
            cost_estimate=pl.CostEstimate(flops=flops, bytes_accessed=10**6, transcendentals=0),
            name=name,
        )

    unit_flops = 2 * HID * HID * TILE
    passed = Weights.shapes + Weights.back_shapes[0:2] + (((8, LANES), F32),)
    passed_specs = [whole(shape) for shape, dtype in passed]
    passed_shapes = [jax.ShapeDtypeStruct(shape, dtype) for shape, dtype in passed]
    next_joined, *places_actor = call(
        action_kernel,
        tiles,
        [mine(SDIM), mine(ADIM), actor_flat],
        [local(IN_ROWS)] + place_specs,
        [jax.ShapeDtypeStruct((IN_ROWS, local_rows // 2), BF16)] + places(ACTOR),
        [pltpu.VMEM((IN_ROWS, TILE), F32), flat, spread(ACTOR, 1), tails] + net,
        "next_action",
        2 * tiles * unit_flops,
    )(core, in_hbm(next_states), in_hbm(smoothing), target_actor)
    actor_passed = Weights.shapes + (((8, LANES), F32), Weights.back_shapes[0], Weights.back_shapes[3])
    actor_shapes = [jax.ShapeDtypeStruct(shape, dtype) for shape, dtype in actor_passed]
    target, keep_one, send_one, *rest = call(
        lambda *refs: target_kernel(row_total, *refs),
        local_rows // 2 // TARGET_TILE,
        [whole(None)] * 5
        + [critic_flat] * 4
        + [actor_flat]
        + place_specs,
        [whole(None), half, half]
        + place_specs
        + passed_specs
        + [whole(None)] * len(actor_shapes),
        [jax.ShapeDtypeStruct((1, local_rows // 2), F32), half_shape, half_shape]
        + places(CRITIC)
        + passed_shapes
        + actor_shapes,
        tile_scratch(TARGET_TILE)
        + [spread(CRITIC, 4), spread(ACTOR, 1), tails]
        + net * 3
        + back[0:2]
        + sums,
        "target_and_first_critic",
        14 * tiles * unit_flops,
    )(
        core,
        states,
        actions,
        rewards,
        done_flags,
        next_joined,
        target_critic,
        far_lagged,
        critic_weights,
        far_weights,
        actor_weights,
        *places_actor,
    )
    places_critic, critic_two, actor_net = rest[0:2], rest[2 : 2 + len(passed)], rest[2 + len(passed) :]
    kept_shapes = [
        pltpu.VMEM((tiles, rows, TILE), dtype)
        for rows, dtype in ((HID + 16, BF16), (HID, F32), (HID, BF16), (HID, F32), (8, F32))
    ]
    kept_specs = [whole(None)] * len(kept_shapes)

    columns = local_rows // 2
    step_columns = columns // 3 // 512 * 512
    pieces = [(columns - 2 * step_columns, 0)]
    pieces = pieces + [(step_columns, columns - i * step_columns) for i in (2, 1)]
    tail_shapes = (((16, pieces[0][0]), F32),)
    carried = SUM_SHAPES + tail_shapes
    carried_specs = [whole(shape) for shape, dtype in carried]
    carried_shapes = [jax.ShapeDtypeStruct(shape, dtype) for shape, dtype in carried]

    def second_critic(piece, tied_target, state):
        is_first, is_last = piece == 0, piece == len(pieces) - 1
        width, start = pieces[piece]
        operands = [core, states, actions, tied_target, *critic_two]
        scratch = tile_scratch(width)[0:2]
        out_shape = carried_shapes
        if is_last:
            operands = operands + places_critic
            out_shape = [half_shape, half_shape]
            scratch = scratch + sums + scratch_of(tail_shapes) + [flat]
        aliases = []
        if not is_first and not is_last:
            aliases = [(len(operands) + i, i) for i in range(len(state))]
        operands = operands + list(state)
        return call(
            lambda *refs: critic_kernel(row_total, start, width, is_first, is_last, *refs),
            1,
            [whole(None)] * (len(operands) - 1),
            [whole(None)] * len(out_shape),
            out_shape,
            scratch,
            "second_critic",
            8 * unit_flops,
            aliases,
        )(*operands)

    def actor_forward(tied_tail):
        return call(
            forward_kernel,
            tiles,
            [whole(None)] * 6,
            kept_specs,
            kept_shapes,
            [pltpu.VMEM((IN_ROWS, TILE), F32)],
            "actor_forward",
            12 * unit_flops,
            vmem=FORWARD_VMEM,
        )(core, states, *actor_net[0:4], tied_tail)

    masks = chip_masks()
    state = ()
    one = keep_one + twin_swap(send_one)
    piece = 0
    for mask, other in zip(masks, masks[len(masks) // 2 :] + masks[: len(masks) // 2]):
        moved = partner_by_core(one, (mask, other))
        if mask == masks[-1]:
            one, tied_tail = lax.optimization_barrier((one, actor_net[4]))
            kept = actor_forward(tied_tail)
            *kept, last = kept
            one, last = lax.optimization_barrier((plus(one, moved), last))
            kept = [*kept, last]
        elif piece < len(pieces):
            one, tied_target = lax.optimization_barrier((one, target))
            state = second_critic(piece, tied_target, state)
            piece += 1
            one, state = lax.optimization_barrier((one + moved, state))
        else:
            one = one + moved
    while piece < len(pieces):
        state = second_critic(piece, target, state)
        piece += 1
    keep_two, send_two = state
    one_other = twin_swap(one)
    two = plus(keep_two, twin_swap(send_two))
    two_moved = partner(two, masks[-1])
    two, one, one_other = lax.optimization_barrier((two, one, one_other))
    keep_actor, send_actor = call(
        lambda *refs: actor_kernel(row_total, *refs),
        tiles,
        [whole(None), half, half]
        + [critic_flat] * 6
        + place_specs * 2
        + [whole(None)] * 2
        + kept_specs,
        [half, half],
        [half_shape, half_shape],
        [tile_scratch(TILE)[i] for i in (0, 2, 3)]
        + [pltpu.VMEM((FLAT_ROWS, LANES), F32), spread(CRITIC, 1), tails]
        + net
        + back[0:3]
        + sums,
        "actor",
        8 * tiles * unit_flops,
        vmem=ACTOR_VMEM,
    )(
        core,
        states,
        one,
        one_other,
        critic_weights,
        far_weights,
        critic_first,
        far_first,
        critic_second,
        far_second,
        *places_actor,
        *places_critic,
        *actor_net[5:7],
        *[pltpu.with_memory_space_constraint(value, pltpu.VMEM) for value in kept],
    )
    actor_moved = twin_swap(send_actor)
    two = two + two_moved
    two, keep_actor, actor_moved = lax.optimization_barrier((two, keep_actor, actor_moved))
    actor = keep_actor + actor_moved
    turned = masks[len(masks) // 2 :] + masks[: len(masks) // 2]
    later = masks[:-1]
    for index, pair in enumerate(zip(masks, turned)):
        moved = partner_by_core(actor, pair)
        if index < len(later):
            two = two + partner(two, later[index - 1])
        actor = actor + moved
    actor_other = twin_swap(actor)
    two_other = to_second(two)

    def step(net, loss_lane, halves, sources, name):
        vector = pl.BlockSpec(memory_space=pltpu.VMEM)
        scalar = pl.BlockSpec(memory_space=pltpu.SMEM)
        return pl.pallas_call(
            lambda *refs: step_kernel(net, loss_lane, *refs),
            in_specs=[scalar] + [vector] * (len(halves) + len(sources)),
            out_specs=[vector] * len(sources) + [scalar],
            out_shape=[jax.ShapeDtypeStruct(source.shape, F32) for source in sources]
            + [jax.ShapeDtypeStruct((1,), F32)],
            scratch_shapes=[pltpu.VMEM((FLAT_ROWS, LANES), F32)] * 2,
            compiler_params=params,
            name=name,
        )(core, *halves, *sources)

    new_critic, new_critic_first, new_critic_second, new_target_critic, critic_loss = step(
        CRITIC,
        1,
        (one, one_other, two, two_other),
        (critic_weights, critic_first, critic_second, target_critic),
        "critic_step",
    )
    new_actor, new_actor_first, new_actor_second, new_target_actor, actor_loss = step(
        ACTOR,
        8,
        (actor, actor_other),
        (actor_weights, actor_first, actor_second, target_actor),
        "actor_step",
    )
    return (
        new_actor,
        new_actor_first,
        new_actor_second,
        new_critic,
        new_critic_first,
        new_critic_second,
        new_target_actor,
        new_target_critic,
        critic_loss,
        actor_loss.reshape(()),
    )


def solution(mesh):
    columns = P(None, "dp")
    critic = P("twin", None)
    return jax.shard_map(
        on_device,
        mesh=mesh,
        in_specs=(
            columns,
            columns,
            P("dp"),
            columns,
            P("dp"),
            columns,
            P(),
            P(),
            P(),
            critic,
            critic,
            critic,
            P(),
            critic,
        ),
        out_specs=(P(), P(), P(), critic, critic, critic, P(), critic, P("twin"), P()),
        check_vma=False,
    )
```

```python
import jax
import jax.numpy as jnp
from jax import lax
from jax.experimental import pallas as pl
from jax.experimental.pallas import tpu as pltpu
from jax.sharding import PartitionSpec as P

SDIM = 17
ADIM = 6
HID = 256
STEP = 10

DISCOUNT = 0.99
POLYAK_RATE = 0.005
LEARN_RATE = 0.05
BETA_ONE = 0.9
BETA_TWO = 0.999
EPSILON = 1e-08
WEIGHT_DECAY = 0.01
NOISE_SCALE = 0.2
NOISE_CLIP = 0.5

LANES = 128
TILE = 2048
ACTION_PART = 2048
LAG = 1
TARGET_TILE = 2048
TARGET_PART = 2048
TARGET_LAG = 1
CRITIC_PART = 1024
CRITIC_LAG = 3
FORWARD_PART = 2048
FORWARD_LAG = 1
ACTOR_PART = 1024
ACTOR_LAG = 3
ONES_ROW = 17
ACTION_ROW = 24
IN_ROWS = 32
FLAT_ROWS = 576
HALF_ROWS = FLAT_ROWS // 2
VMEM_BYTES = 24 * 2**20
SMALL_VMEM_BYTES = 2**21
STEP_VMEM = 10 * 2**20
FORWARD_VMEM = 8 * 2**20
ACTOR_VMEM = 16 * 2**20

F32 = jnp.float32
BF16 = jnp.bfloat16


class Net:
    def __init__(self, in_size, out_size):
        self.in_size = in_size
        self.out_size = out_size
        self.bias1 = 2 * in_size
        self.weight2 = self.bias1 + 2
        self.bias2 = self.weight2 + 2 * HID
        self.weight3 = self.bias2 + 2
        self.rows = self.weight3 + 2 * out_size
        self.size = self.rows * LANES + out_size


ACTOR = Net(SDIM, ADIM)
CRITIC = Net(SDIM + ADIM, 1)


def dot(a, b):
    return jnp.dot(a, b, preferred_element_type=F32)


def dot_nt(a, b):
    return lax.dot_general(a, b, (((1,), (1,)), ((), ())), preferred_element_type=F32)


def wide(column, width):
    return jnp.concatenate([column] * (width // LANES), axis=1)


def iota(shape, axis):
    return lax.broadcasted_iota(jnp.int32, shape, axis)


def rows_to_lanes(block):
    return jnp.concatenate([block[row : row + 1] for row in range(block.shape[0])], axis=1)


def place_mask(net):
    width = LANES * net.in_size
    position = iota((8, width), 1).astype(F32)
    phase = position - net.in_size * jnp.floor((position + 0.5) * (1.0 / net.in_size))
    blocks = []
    for start in range(0, IN_ROWS, 8):
        row = iota((8, width), 0) + start
        source = jnp.where(row < SDIM, row, jnp.where(row >= ACTION_ROW, row - ACTION_ROW + SDIM, -1))
        source = jnp.where(source < net.in_size, source, -1).astype(F32)
        blocks.append(jnp.where(phase == source, 1.0, 0.0))
    return jnp.concatenate(blocks, axis=0)


def place_units(net):
    shape = (LANES * net.in_size, LANES)
    gap = iota(shape, 0) - net.in_size * iota(shape, 1)
    return jnp.where(gap.astype(jnp.uint32) < net.in_size, 1.0, 0.0).astype(BF16)


def three_parts(value):
    high = value.astype(BF16).astype(F32)
    rest = value - high
    middle = rest.astype(BF16).astype(F32)
    return high, middle, rest - middle


def spread_first(net, flat, mask, spread, slot):
    for half in range(2):
        pieces = [
            jnp.broadcast_to(
                flat[half * net.in_size + row : half * net.in_size + row + 1, :],
                (IN_ROWS, LANES),
            )
            for row in range(net.in_size)
        ]
        start = (2 * slot + half) * IN_ROWS
        spread[start : start + IN_ROWS, :] = (
            jnp.concatenate(pieces, axis=1) * mask[...]
        ).astype(BF16)


def gather_first(spread, units, nets):
    gathered = dot(spread[0 : 2 * IN_ROWS * nets, :], units[...])
    halves = [gathered[i * IN_ROWS : (i + 1) * IN_ROWS] for i in range(2 * nets)]
    return [jnp.concatenate(halves[2 * i : 2 * i + 2], axis=1) for i in range(nets)]


def flatten_first(net, transposed, out, mask, units):
    blocks = [transposed[:, 0:LANES], transposed[:, LANES:HID]]
    parts = [part for block in blocks for part in three_parts(block)]
    spread = dot_nt(jnp.concatenate(parts, axis=0).astype(BF16), units[...])
    for half in range(2):
        high, middle, low = [
            spread[(3 * half + part) * IN_ROWS : (3 * half + part + 1) * IN_ROWS]
            for part in range(3)
        ]
        total = (high + (middle + low)) * mask[...]
        line = jnp.sum(total, axis=0, keepdims=True)
        for row in range(net.in_size):
            target = half * net.in_size + row
            out[target : target + 1, :] = line[:, row * LANES : (row + 1) * LANES]


def as_column(row):
    return jnp.transpose(jnp.broadcast_to(row, (LANES, HID)))


def flat_row(flat, start):
    return jnp.concatenate([flat[start : start + 1, :], flat[start + 1 : start + 2, :]], axis=1)


class Weights:
    shapes = (
        ((HID, IN_ROWS), BF16),
        ((HID, HID), BF16),
        ((HID, LANES), F32),
        ((16, HID), BF16),
    )
    back_shapes = (
        ((HID, HID), BF16),
        ((HID, LANES), F32),
        ((16, HID), BF16),
        ((HID, 16), BF16),
    )


def scratch_of(shapes):
    return [pltpu.VMEM(shape, dtype) for shape, dtype in shapes]


def unpack_first(net, first_t, bias1, refs, back=None):
    first_t = 0.5 * first_t
    row = iota((IN_ROWS, HID), 0)
    for part, value in enumerate(three_parts(0.5 * bias1)):
        first_t = jnp.where(row == ONES_ROW + part, value, first_t)
    refs[0][...] = jnp.transpose(first_t).astype(BF16)
    if back is not None and back[2] is not None:
        back[2][...] = first_t[16:32].astype(BF16)


def unpack_rest(net, flat, refs, back=None):
    first, second, bias2, third = refs
    left = flat[pl.ds(net.weight2, HID, stride=2), :]
    right = flat[pl.ds(net.weight2 + 1, HID, stride=2), :]
    second_value = 0.5 * jnp.concatenate([left, right], axis=1)
    second[...] = second_value.astype(BF16)
    bias2[...] = as_column(0.5 * flat_row(flat, net.bias2))
    left = flat[pl.ds(net.weight3, 8, stride=2), :]
    right = flat[pl.ds(net.weight3 + 1, 8, stride=2), :]
    third_value = jnp.concatenate([left, right], axis=1)
    third_value = jnp.where(iota((8, HID), 0) < net.out_size, third_value, 0.0)
    third_value = jnp.concatenate([third_value, jnp.zeros((8, HID), F32)], axis=0)
    third[...] = third_value.astype(BF16)
    if back is not None:
        second_t, third_column, unused, third_t = back
        second_t[...] = jnp.transpose(second_value).astype(BF16)
        third_low = 0.5 * third_value.astype(BF16).astype(F32)
        if third_column is not None:
            third_column[...] = as_column(third_low[0:1])
        if third_t is not None:
            third_t[...] = jnp.transpose(third_low).astype(BF16)


def unpack_nets(net, values, flat, mask, units, spread, refs, backs):
    biases = []
    for slot, (value, net_refs, back) in enumerate(zip(values, refs, backs)):
        load_flat(net, flat, value())
        spread_first(net, flat, mask, spread, slot)
        biases.append(flat_row(flat, net.bias1))
        unpack_rest(net, flat, net_refs, back)
    firsts = gather_first(spread, units, len(values))
    for first_t, bias1, net_refs, back in zip(firsts, biases, refs, backs):
        unpack_first(net, first_t, bias1, net_refs, back)


def load_flat(net, flat, value):
    flat[0 : net.rows, :] = value
    flat[net.rows : FLAT_ROWS, :] = jnp.zeros((FLAT_ROWS - net.rows, LANES), F32)


def span_of(net, ref, tail):
    where = pl.ds(net.rows * LANES, net.out_size) if tail else pl.ds(0, net.rows * LANES)
    return (where,) if len(ref.shape) == 1 else (slice(0, 1), where)


def body_of(net, ref):
    return ref[span_of(net, ref, False)].reshape(net.rows, LANES)


def tail_of(net, ref):
    return ref[span_of(net, ref, True)].reshape(1, net.out_size)


def tail_column(tail):
    size = tail.shape[1]
    eye = iota((8, size), 0) == iota((8, size), 1)
    return jnp.sum(jnp.where(eye, jnp.broadcast_to(tail, (8, size)), 0.0), axis=1, keepdims=True)


def start_inputs(inputs):
    inputs[...] = jnp.zeros_like(inputs)
    row = iota((8, inputs.shape[1]), 0) + 16
    inputs[16:24, :] = jnp.where((row >= ONES_ROW) & (row < ONES_ROW + 3), 1.0, 0.0)


def staggered(parts, lag):
    parts = list(parts)
    step = 0
    while any(part is not None for part in parts):
        for index, part in enumerate(parts):
            if part is not None and step >= index * lag:
                try:
                    next(part)
                except StopIteration:
                    parts[index] = None
        step += 1


def column_parts(width, size):
    return [slice(start, start + size) for start in range(0, width, size)]


def silu_low(half_pre):
    wave = jnp.tanh(half_pre)
    return (half_pre * wave + half_pre).astype(BF16)


def silu_and_slope(half_pre):
    wave = jnp.tanh(half_pre)
    above = 1.0 + wave
    hidden = half_pre * above
    return hidden.astype(BF16), above + hidden * (1.0 - wave)


def forward(refs, inputs):
    first, second, bias2, third = refs
    width = inputs.shape[1]
    pre = dot(first[...], inputs)
    yield
    hidden = silu_low(pre)
    yield
    pre = dot(second[...], hidden)
    yield
    hidden = silu_low(pre + wide(bias2[...], width))
    yield
    return dot(third[...], hidden)[0:8]


def forward_kept(refs, inputs, hidden1=None):
    first, second, bias2, third = refs
    width = inputs.shape[1]
    pre = dot(first[...], inputs)
    yield
    low1, slope1 = silu_and_slope(pre)
    if hidden1 is not None:
        hidden1[0:HID, :] = low1
    yield
    pre = dot(second[...], low1)
    yield
    low2, slope2 = silu_and_slope(pre + wide(bias2[...], width))
    yield
    return dot(third[...], low2)[0:8], slope1, low2, slope2


def write_gradient(net, sums, last_row, flat, mask, units):
    sum1, sum2, sum3 = sums
    flatten_first(net, sum1[...], flat, mask, units)
    bias1 = sum1[ONES_ROW : ONES_ROW + 1, :]
    bias2 = sum2[HID : HID + 1, :]
    weight2 = jnp.transpose(sum2[0:HID, :])
    for side in range(2):
        lanes = slice(side * LANES, (side + 1) * LANES)
        flat[net.bias1 + side : net.bias1 + side + 1, :] = bias1[:, lanes]
        flat[pl.ds(net.weight2 + side, HID, stride=2), :] = weight2[:, lanes]
        flat[net.bias2 + side : net.bias2 + side + 1, :] = bias2[:, lanes]
        for unit in range(net.out_size):
            row = net.weight3 + 2 * unit + side
            flat[row : row + 1, :] = sum3[unit : unit + 1, lanes]
    flat[net.rows : net.rows + 1, :] = last_row
    rest = FLAT_ROWS - net.rows - 1
    flat[net.rows + 1 : FLAT_ROWS, :] = jnp.zeros((rest, LANES), F32)


def split_halves(flat, core, keep, send):
    low = flat[0:HALF_ROWS, :]
    high = flat[HALF_ROWS:FLAT_ROWS, :]
    keep[...] = jnp.where(core == 0, low, high)
    send[...] = jnp.where(core == 0, high, low)


def join_halves(core, mine, other, flat):
    flat[0:HALF_ROWS, :] = jnp.where(core == 0, mine[...], other[...])
    flat[HALF_ROWS:FLAT_ROWS, :] = jnp.where(core == 0, other[...], mine[...])


def adamw_step(weight, gradient, moment_one, moment_two):
    moment_one = BETA_ONE * moment_one + (1.0 - BETA_ONE) * gradient
    moment_two = BETA_TWO * moment_two + (1.0 - BETA_TWO) * gradient * gradient
    corrected_one = moment_one / (1.0 - BETA_ONE**STEP)
    corrected_two = moment_two / (1.0 - BETA_TWO**STEP)
    weight = weight - LEARN_RATE * (
        corrected_one / (jnp.sqrt(corrected_two) + EPSILON) + WEIGHT_DECAY * weight
    )
    return (weight, moment_one, moment_two)


def polyak_mix(lagged, fresh):
    return POLYAK_RATE * fresh + (1.0 - POLYAK_RATE) * lagged


def clear(refs):
    for ref in refs:
        ref[...] = jnp.zeros_like(ref)


SUM_SHAPES = (((IN_ROWS, HID), F32), ((HID + 16, HID), F32), ((16, HID), F32))


def critic_part(refs, back, bias3, inputs, target, scale, hidden1, sums, tail_sums):
    second_t, third_column = back[0], back[1]
    width = inputs.shape[1]
    out, slope1, low2, slope2 = yield from forward_kept(refs, inputs, hidden1)
    error = out[0:1] + bias3 - target
    grad3 = (scale * error).astype(BF16).astype(F32)
    tail_sums[0:1, :] += grad3
    tail_sums[1:2, :] += error * error
    yield
    grad2 = (wide(third_column[...], width) * grad3 * slope2).astype(BF16)
    sums[2][...] += dot_nt(jnp.broadcast_to(grad3, (16, width)).astype(BF16), low2)
    yield
    grad_low1 = dot(second_t[...], grad2)
    yield
    grad1 = (grad_low1 * slope1).astype(BF16)
    sums[1][...] += dot_nt(hidden1[...], grad2)
    yield
    sums[0][...] += dot_nt(inputs, grad1)


def critic_last_row(tail_sums):
    totals = jnp.sum(tail_sums[...], axis=1, keepdims=True)
    lane = iota((1, LANES), 1)
    return jnp.where(lane == 0, totals[0:1], jnp.where(lane == 1, totals[1:2], 0.0))


def action_kernel(
    core_ref,
    next_states,
    smoothing,
    target_actor,
    joined,
    mask_actor,
    units_actor,
    inputs,
    flat,
    spread,
    tails,
    *actor,
):
    step = pl.program_id(0)

    @pl.when(step == 0)
    def _():
        start_inputs(inputs)
        units_actor[...] = place_units(ACTOR)
        mask_actor[...] = place_mask(ACTOR)
        unpack_nets(
            ACTOR,
            [lambda: body_of(ACTOR, target_actor)],
            flat,
            mask_actor,
            units_actor,
            spread,
            [actor],
            [None],
        )
        tails[0:8, 0:1] = tail_column(tail_of(ACTOR, target_actor))

    inputs[0:SDIM, :] = next_states[...]

    def part(columns):
        out = yield from forward(actor, inputs[:, columns].astype(BF16))
        lagged_action = jnp.tanh(out + tails[0:8, 0:1])
        jitter = jnp.clip(NOISE_SCALE * smoothing[:, columns], -NOISE_CLIP, NOISE_CLIP)
        next_action = jnp.clip(lagged_action[0:ADIM] + jitter, -1.0, 1.0)
        inputs[ACTION_ROW : ACTION_ROW + ADIM, columns] = next_action
        joined[:, columns] = inputs[:, columns].astype(BF16)

    staggered([part(columns) for columns in column_parts(TILE, ACTION_PART)], LAG)


def target_kernel(
    row_total,
    core_ref,
    states,
    actions,
    rewards,
    done_flags,
    next_joined,
    own_lagged,
    far_lagged,
    own_critic,
    far_critic,
    actor_weights,
    mask_actor,
    units_actor,
    target_out,
    keep,
    send,
    mask_critic,
    units_critic,
    *rest,
):
    next_critic, next_second_t, next_column, next_tail = rest[0:4], rest[4], rest[5], rest[6]
    actor, actor_tail, actor_second_t, actor_third_t = rest[7:11], rest[11], rest[12], rest[13]
    rest = rest[14:]
    inputs, hidden1, tail_sums, flat, spread, spread_actor, tails = rest[0:7]
    lag_one, lag_two, critic = rest[7:11], rest[11:15], rest[15:19]
    back = (rest[19], rest[20], None, None)
    sums = rest[21:24]
    core = core_ref[0]
    step = pl.program_id(0)
    width = inputs.shape[1]

    @pl.when(step == 0)
    def _():
        start_inputs(inputs)
        hidden1[HID : HID + 16, :] = jnp.ones((16, width), BF16)
        clear(sums)
        clear([tail_sums])
        units_critic[...] = place_units(CRITIC)
        mask_critic[...] = place_mask(CRITIC)

        def chosen(part, holder):
            return jnp.where(core == holder, part(CRITIC, own_critic), part(CRITIC, far_critic))

        unpack_nets(
            CRITIC,
            [
                lambda: body_of(CRITIC, own_lagged),
                lambda: body_of(CRITIC, far_lagged),
                lambda: chosen(body_of, 0),
                lambda: chosen(body_of, 1),
            ],
            flat,
            mask_critic,
            units_critic,
            spread,
            [lag_one, lag_two, critic, next_critic],
            [None, None, back, (next_second_t, next_column, None, None)],
        )
        tails[8:16, 0:1] = tail_column(tail_of(CRITIC, own_lagged))
        tails[16:24, 0:1] = tail_column(tail_of(CRITIC, far_lagged))
        tails[24:32, 0:1] = tail_column(chosen(tail_of, 0))
        next_tail[...] = jnp.broadcast_to(tail_column(chosen(tail_of, 1)), (8, LANES))
        unpack_nets(
            ACTOR,
            [lambda: body_of(ACTOR, actor_weights)],
            flat,
            mask_actor,
            units_actor,
            spread_actor,
            [actor],
            [(actor_second_t, None, None, actor_third_t)],
        )
        tail = tail_column(tail_of(ACTOR, actor_weights))
        actor_tail[...] = jnp.broadcast_to(tail, (8, LANES))

    own = core * target_out.shape[1] + step * width

    def span(start, columns):
        start = pl.multiple_of(start + columns.start, LANES)
        return pl.ds(start, columns.stop - columns.start)

    tile = span(own, slice(0, width))
    inputs[0:SDIM, :] = states[:, tile]
    inputs[ACTION_ROW : ACTION_ROW + ADIM, :] = actions[:, tile]

    def part(columns):
        joined = next_joined[:, span(step * width, columns)]
        out_one = yield from forward(lag_one, joined)
        yield
        out_two = yield from forward(lag_two, joined)
        value_one = out_one[0:1] + tails[8:9, 0:1]
        value_two = out_two[0:1] + tails[16:17, 0:1]
        keep_going = 1.0 - done_flags[:, span(own, columns)].astype(F32)
        lagged = jnp.minimum(value_one, value_two)
        target = rewards[:, span(own, columns)] + DISCOUNT * keep_going * lagged
        target_out[:, span(step * width, columns)] = target

    def next_part(columns):
        return critic_part(
            critic,
            back,
            tails[24:25, 0:1],
            inputs[:, columns].astype(BF16),
            target_out[:, span(step * width, columns)],
            2.0 / row_total,
            hidden1.at[:, columns],
            sums,
            tail_sums.at[:, columns],
        )

    staggered([part(columns) for columns in column_parts(width, TARGET_PART)], TARGET_LAG)
    staggered([next_part(columns) for columns in column_parts(width, CRITIC_PART)], CRITIC_LAG)

    @pl.when(step == pl.num_programs(0) - 1)
    def _():
        last = critic_last_row(tail_sums)
        write_gradient(CRITIC, sums, last, flat, mask_critic, units_critic)
        split_halves(flat, core, keep, send)


def critic_kernel(row_total, start, width, is_first, is_last, core_ref, *refs):
    states, actions, target = refs[0:3]
    critic, second_t, third_column, tail = refs[3:7], refs[7], refs[8], refs[9]
    refs = refs[10:]
    if is_last:
        mask, units = refs[0:2]
        refs = refs[2:]
    before = ()
    if not is_first:
        before = refs[0:4]
        refs = refs[4:]
    if is_last:
        keep, send, inputs, hidden1 = refs[0:4]
        sums, tail_sums, flat = refs[4:7], refs[7], refs[8]
    else:
        sums, tail_sums, inputs, hidden1 = refs[0:3], refs[3], refs[4], refs[5]
    start_inputs(inputs)
    hidden1[HID : HID + 16, :] = jnp.ones((16, width), BF16)
    if is_first:
        clear([*sums, tail_sums])
    for after, value in zip([*sums, tail_sums], before):
        after[...] = value[...]
    first_column = pl.multiple_of(core_ref[0] * target.shape[1] + start, LANES)
    inputs[0:SDIM, :] = states[:, pl.ds(first_column, width)]
    inputs[ACTION_ROW : ACTION_ROW + ADIM, :] = actions[:, pl.ds(first_column, width)]

    def part(columns):
        return critic_part(
            critic,
            (second_t, third_column),
            tail[0:1, 0:1],
            inputs[:, columns].astype(BF16),
            target[:, start + columns.start : start + columns.stop],
            2.0 / row_total,
            hidden1.at[:, columns],
            sums,
            tail_sums.at[:, columns],
        )

    staggered([part(columns) for columns in column_parts(width, width // 2)], CRITIC_LAG)
    if is_last:
        last = critic_last_row(tail_sums)
        write_gradient(CRITIC, sums, last, flat, mask, units)
        split_halves(flat, core_ref[0], keep, send)


def forward_kernel(
    core_ref,
    states,
    first,
    second,
    bias2,
    third,
    tail,
    kept_low1,
    kept_slope1,
    kept_low2,
    kept_slope2,
    kept_action,
    inputs,
):
    step = pl.program_id(0)

    @pl.when(step == 0)
    def _():
        start_inputs(inputs)

    columns = TILE * pl.num_programs(0)
    first_column = pl.multiple_of(core_ref[0] * columns + step * TILE, LANES)
    inputs[0:SDIM, :] = states[:, pl.ds(first_column, TILE)]
    kept_low1[step, HID : HID + 16, :] = jnp.ones((16, TILE), BF16)

    def part(columns):
        out, slope1, low2, slope2 = yield from forward_kept(
            (first, second, bias2, third),
            inputs[:, columns].astype(BF16),
            kept_low1.at[step, :, columns],
        )
        kept_slope1[step, :, columns] = slope1
        kept_low2[step, :, columns] = low2
        kept_slope2[step, :, columns] = slope2
        kept_action[step, :, columns] = jnp.tanh(out + tail[0:8, 0:1])

    staggered([part(columns) for columns in column_parts(TILE, FORWARD_PART)], FORWARD_LAG)


def actor_kernel(
    row_total,
    core_ref,
    states,
    mine,
    other,
    own_critic,
    far_critic,
    own_first,
    far_first,
    own_second,
    far_second,
    mask_actor,
    units_actor,
    mask_critic,
    units_critic,
    actor_second_t,
    actor_third_t,
    kept_low1,
    kept_slope1,
    kept_low2,
    kept_slope2,
    kept_action,
    keep,
    send,
    inputs,
    tail_sums,
    flat,
    gradient,
    spread_critic,
    tails,
    *rest,
):
    judge, judge_back = rest[0:4], (rest[4], rest[5], rest[6], None)
    sums = rest[7:10]
    core = core_ref[0]
    step = pl.program_id(0)
    width = inputs.shape[1]

    @pl.when(step == 0)
    def _():
        start_inputs(inputs)
        clear(sums)
        clear([tail_sums])
        join_halves(core, mine, other, gradient)

        def chosen(part, own, far):
            return jnp.where(core == 0, part(CRITIC, own), part(CRITIC, far))

        def fresh(part, grad):
            return adamw_step(
                chosen(part, own_critic, far_critic),
                grad,
                chosen(part, own_first, far_first),
                chosen(part, own_second, far_second),
            )[0]

        unpack_nets(
            CRITIC,
            [lambda: fresh(body_of, gradient[0 : CRITIC.rows, :])],
            flat,
            mask_critic,
            units_critic,
            spread_critic,
            [judge],
            [judge_back],
        )
        tail = fresh(tail_of, gradient[CRITIC.rows : CRITIC.rows + 1, 0:1])
        tails[8:16, 0:1] = tail_column(tail)

    columns = width * pl.num_programs(0)
    first_column = pl.multiple_of(core * columns + step * width, LANES)
    inputs[0:SDIM, :] = states[:, pl.ds(first_column, width)]
    inputs[ACTION_ROW:IN_ROWS, :] = kept_action[step]
    judge_second_t, judge_column, judge_rows, unused = judge_back
    start = jnp.full((HID, LANES), -1.0 / row_total, F32).astype(BF16).astype(F32)
    start = judge_column[...] * start

    def part(columns):
        part_width = columns.stop - columns.start
        joined = inputs[:, columns].astype(BF16)
        action = kept_action[step, :, columns]
        out, judge_slope1, unused, judge_slope2 = yield from forward_kept(judge, joined)
        tail_sums[8:9, columns] += out[0:1] + tails[8:9, 0:1]
        grad2 = (wide(start, part_width) * judge_slope2).astype(BF16)
        yield
        grad_low1 = dot(judge_second_t[...], grad2)
        yield
        grad1 = (grad_low1 * judge_slope1).astype(BF16)
        yield
        grad_action = 2.0 * dot(judge_rows[...], grad1)[8:16]
        grad3 = (grad_action * (1.0 - action * action)).astype(BF16).astype(F32)
        tail_sums[0:8, columns] += grad3
        grad3_low = jnp.concatenate([grad3, jnp.zeros_like(grad3)], axis=0).astype(BF16)
        yield
        grad_low2 = dot(actor_third_t[...], grad3_low)
        yield
        grad2 = (grad_low2 * kept_slope2[step, :, columns]).astype(BF16)
        sums[2][...] += dot_nt(grad3_low, kept_low2[step, :, columns])
        yield
        grad_low1 = dot(actor_second_t[...], grad2)
        yield
        grad1 = (grad_low1 * kept_slope1[step, :, columns]).astype(BF16)
        sums[1][...] += dot_nt(kept_low1[step, :, columns], grad2)
        yield
        sums[0][...] += dot_nt(joined, grad1)

    staggered([part(columns) for columns in column_parts(width, ACTOR_PART)], ACTOR_LAG)

    @pl.when(step == pl.num_programs(0) - 1)
    def _():
        totals = jnp.sum(tail_sums[...], axis=1, keepdims=True)
        lane = iota((8, LANES), 1)
        biases = jnp.where(lane == iota((8, LANES), 0), totals[0:8], 0.0)
        last = jnp.sum(biases, axis=0, keepdims=True)
        last = jnp.where(iota((1, LANES), 1) == 8, -totals[8:9], last)
        write_gradient(ACTOR, sums, last, flat, mask_actor, units_actor)
        split_halves(flat, core, keep, send)


def step_kernel(net, loss_lane, core_ref, *refs):
    *halves, weights, first, second, lagged = refs[:-7]
    new_weights, new_first, new_second, new_lagged, loss, gradient, other_gradient = refs[-7:]
    core = core_ref[0]
    join_halves(core, halves[0], halves[1], gradient)
    if len(halves) > 2:
        join_halves(core, halves[2], halves[3], other_gradient)
        gradient[...] = jnp.where(core == 0, gradient[...], other_gradient[...])
    for part, tail, grad in (
        (body_of, False, gradient[0 : net.rows, :]),
        (tail_of, True, gradient[net.rows : net.rows + 1, 0 : net.out_size]),
    ):
        values = [part(net, source) for source in (weights, first, second)]
        fresh, moment_one, moment_two = adamw_step(values[0], grad, values[1], values[2])
        results = (fresh, moment_one, moment_two, polyak_mix(part(net, lagged), fresh))
        for out, result in zip((new_weights, new_first, new_second, new_lagged), results):
            shape = (1, result.size) if len(out.shape) == 2 else (result.size,)
            out[span_of(net, out, tail)] = result.reshape(shape)
    lane = iota((1, LANES), 1)
    row = gradient[net.rows : net.rows + 1, :]
    loss[0] = jnp.sum(jnp.where(lane == loss_lane, row, 0.0))


def twin_swap(value):
    return lax.ppermute(value, "twin", [(0, 1), (1, 0)])


def to_second(value):
    return lax.ppermute(value, "twin", [(0, 1)])


def chip_masks():
    return [1 << bit for bit in range((lax.axis_size("dp") - 1).bit_length())]


def partner(value, mask):
    pairs = [(source, source ^ mask) for source in range(lax.axis_size("dp"))]
    return lax.ppermute(value, "dp", pairs)


def partner_by_core(value, masks):
    pairs = [
        (2 * source + core, 2 * (source ^ masks[core]) + core)
        for source in range(lax.axis_size("dp"))
        for core in range(2)
    ]
    return lax.ppermute(value, ("dp", "twin"), pairs)


def plus_kernel(left, right, out):
    out[...] = left[...] + right[...]


def plus(left, right):
    vector = pl.BlockSpec(memory_space=pltpu.VMEM)
    return pl.pallas_call(
        plus_kernel,
        in_specs=[vector] * 2,
        out_specs=vector,
        out_shape=jax.ShapeDtypeStruct(left.shape, F32),
        compiler_params=pltpu.CompilerParams(vmem_limit_bytes=SMALL_VMEM_BYTES),
        name="plus",
    )(left, right)


def in_hbm(value):
    return pltpu.with_memory_space_constraint(value, pltpu.HBM)


def whole(unused):
    return pl.BlockSpec(memory_space=pltpu.VMEM)


def on_device(
    states,
    actions,
    rewards,
    next_states,
    done_flags,
    smoothing,
    actor_weights,
    actor_first,
    actor_second,
    critic_weights,
    critic_first,
    critic_second,
    target_actor,
    target_critic,
):
    core = lax.axis_index("twin").astype(jnp.int32).reshape(1)
    local_rows = states.shape[1]
    tiles = local_rows // 2 // TILE
    row_total = local_rows * lax.axis_size("dp")
    rewards = rewards.reshape(1, local_rows)
    done_flags = done_flags.reshape(1, local_rows)
    far_lagged = twin_swap(target_critic)
    far_weights = twin_swap(critic_weights)
    far_first = twin_swap(critic_first)
    far_second = twin_swap(critic_second)
    far_lagged, far_weights, far_first, far_second = lax.optimization_barrier(
        (far_lagged, far_weights, far_first, far_second)
    )

    def mine(rows, tile=None, width=TILE):
        count = local_rows // 2 // width
        return pl.BlockSpec(
            (rows, width),
            lambda i, core_ref: (0, core_ref[0] * count + (i if tile is None else tile)),
        )

    def local(rows, tile=None, width=TILE):
        return pl.BlockSpec((rows, width), lambda i, core_ref: (0, i if tile is None else tile))

    def tile_scratch(width):
        return [
            pltpu.VMEM((IN_ROWS, width), F32),
            pltpu.VMEM((HID + 16, width), BF16),
            pltpu.VMEM((16, width), F32),
            flat,
        ]

    actor_flat = whole((ACTOR.size,))
    critic_flat = whole((1, CRITIC.size))
    half = whole((HALF_ROWS, LANES))
    half_shape = jax.ShapeDtypeStruct((HALF_ROWS, LANES), F32)
    tail_shapes = (((16, TILE), F32),)
    flat = pltpu.VMEM((FLAT_ROWS + 8, LANES), F32)

    def places(kind):
        width = LANES * kind.in_size
        mask = jax.ShapeDtypeStruct((IN_ROWS, width), F32)
        return [mask, jax.ShapeDtypeStruct((width, LANES), BF16)]

    def spread(kind, nets):
        return pltpu.VMEM((2 * IN_ROWS * nets, LANES * kind.in_size), BF16)

    place_specs = [whole(None)] * 2
    net = scratch_of(Weights.shapes)
    back = scratch_of(Weights.back_shapes)
    sums = scratch_of(SUM_SHAPES)
    tails = pltpu.VMEM((32, LANES), F32)
    params = pltpu.CompilerParams(vmem_limit_bytes=STEP_VMEM)

    def call(
        kernel, steps, in_specs, out_specs, out_shape, scratch, name, flops, aliases=(), vmem=VMEM_BYTES
    ):
        return pl.pallas_call(
            kernel,
            grid_spec=pltpu.PrefetchScalarGridSpec(
                num_scalar_prefetch=1,
                grid=(steps,),
                in_specs=in_specs,
                out_specs=out_specs,
                scratch_shapes=scratch,
            ),
            out_shape=out_shape,
            input_output_aliases=dict(aliases),
            compiler_params=pltpu.CompilerParams(vmem_limit_bytes=vmem),
            cost_estimate=pl.CostEstimate(flops=flops, bytes_accessed=10**6, transcendentals=0),
            name=name,
        )

    unit_flops = 2 * HID * HID * TILE
    passed = Weights.shapes + Weights.back_shapes[0:2] + (((8, LANES), F32),)
    passed_specs = [whole(shape) for shape, dtype in passed]
    passed_shapes = [jax.ShapeDtypeStruct(shape, dtype) for shape, dtype in passed]
    next_joined, *places_actor = call(
        action_kernel,
        tiles,
        [mine(SDIM), mine(ADIM), actor_flat],
        [local(IN_ROWS)] + place_specs,
        [jax.ShapeDtypeStruct((IN_ROWS, local_rows // 2), BF16)] + places(ACTOR),
        [pltpu.VMEM((IN_ROWS, TILE), F32), flat, spread(ACTOR, 1), tails] + net,
        "next_action",
        2 * tiles * unit_flops,
    )(core, in_hbm(next_states), in_hbm(smoothing), target_actor)
    actor_passed = Weights.shapes + (((8, LANES), F32), Weights.back_shapes[0], Weights.back_shapes[3])
    actor_shapes = [jax.ShapeDtypeStruct(shape, dtype) for shape, dtype in actor_passed]
    target, keep_one, send_one, *rest = call(
        lambda *refs: target_kernel(row_total, *refs),
        local_rows // 2 // TARGET_TILE,
        [whole(None)] * 5
        + [critic_flat] * 4
        + [actor_flat]
        + place_specs,
        [whole(None), half, half]
        + place_specs
        + passed_specs
        + [whole(None)] * len(actor_shapes),
        [jax.ShapeDtypeStruct((1, local_rows // 2), F32), half_shape, half_shape]
        + places(CRITIC)
        + passed_shapes
        + actor_shapes,
        tile_scratch(TARGET_TILE)
        + [spread(CRITIC, 4), spread(ACTOR, 1), tails]
        + net * 3
        + back[0:2]
        + sums,
        "target_and_first_critic",
        14 * tiles * unit_flops,
    )(
        core,
        states,
        actions,
        rewards,
        done_flags,
        next_joined,
        target_critic,
        far_lagged,
        critic_weights,
        far_weights,
        actor_weights,
        *places_actor,
    )
    places_critic, critic_two, actor_net = rest[0:2], rest[2 : 2 + len(passed)], rest[2 + len(passed) :]
    kept_shapes = [
        pltpu.VMEM((tiles, rows, TILE), dtype)
        for rows, dtype in ((HID + 16, BF16), (HID, F32), (HID, BF16), (HID, F32), (8, F32))
    ]
    kept_specs = [whole(None)] * len(kept_shapes)

    columns = local_rows // 2
    step_columns = columns // 3 // 512 * 512
    pieces = [(columns - 2 * step_columns, 0)]
    pieces = pieces + [(step_columns, columns - i * step_columns) for i in (2, 1)]
    tail_shapes = (((16, pieces[0][0]), F32),)
    carried = SUM_SHAPES + tail_shapes
    carried_specs = [whole(shape) for shape, dtype in carried]
    carried_shapes = [jax.ShapeDtypeStruct(shape, dtype) for shape, dtype in carried]

    def second_critic(piece, tied_target, state):
        is_first, is_last = piece == 0, piece == len(pieces) - 1
        width, start = pieces[piece]
        operands = [core, states, actions, tied_target, *critic_two]
        scratch = tile_scratch(width)[0:2]
        out_shape = carried_shapes
        if is_last:
            operands = operands + places_critic
            out_shape = [half_shape, half_shape]
            scratch = scratch + sums + scratch_of(tail_shapes) + [flat]
        aliases = []
        if not is_first and not is_last:
            aliases = [(len(operands) + i, i) for i in range(len(state))]
        operands = operands + list(state)
        return call(
            lambda *refs: critic_kernel(row_total, start, width, is_first, is_last, *refs),
            1,
            [whole(None)] * (len(operands) - 1),
            [whole(None)] * len(out_shape),
            out_shape,
            scratch,
            "second_critic",
            8 * unit_flops,
            aliases,
        )(*operands)

    def actor_forward(tied_tail):
        return call(
            forward_kernel,
            tiles,
            [whole(None)] * 6,
            kept_specs,
            kept_shapes,
            [pltpu.VMEM((IN_ROWS, TILE), F32)],
            "actor_forward",
            12 * unit_flops,
            vmem=FORWARD_VMEM,
        )(core, states, *actor_net[0:4], tied_tail)

    masks = chip_masks()
    state = ()
    one = keep_one + twin_swap(send_one)
    piece = 0
    for mask, other in zip(masks, masks[len(masks) // 2 :] + masks[: len(masks) // 2]):
        moved = partner_by_core(one, (mask, other))
        if mask == masks[-1]:
            one, tied_tail = lax.optimization_barrier((one, actor_net[4]))
            kept = actor_forward(tied_tail)
            *kept, last = kept
            one, last = lax.optimization_barrier((plus(one, moved), last))
            kept = [*kept, last]
        elif piece < len(pieces):
            one, tied_target = lax.optimization_barrier((one, target))
            state = second_critic(piece, tied_target, state)
            piece += 1
            one, state = lax.optimization_barrier((one + moved, state))
        else:
            one = one + moved
    while piece < len(pieces):
        state = second_critic(piece, target, state)
        piece += 1
    keep_two, send_two = state
    one_other = twin_swap(one)
    two = plus(keep_two, twin_swap(send_two))
    two_moved = partner(two, masks[-1])
    two, one, one_other = lax.optimization_barrier((two, one, one_other))
    keep_actor, send_actor = call(
        lambda *refs: actor_kernel(row_total, *refs),
        tiles,
        [whole(None), half, half]
        + [critic_flat] * 6
        + place_specs * 2
        + [whole(None)] * 2
        + kept_specs,
        [half, half],
        [half_shape, half_shape],
        [tile_scratch(TILE)[i] for i in (0, 2, 3)]
        + [pltpu.VMEM((FLAT_ROWS, LANES), F32), spread(CRITIC, 1), tails]
        + net
        + back[0:3]
        + sums,
        "actor",
        8 * tiles * unit_flops,
        vmem=ACTOR_VMEM,
    )(
        core,
        states,
        one,
        one_other,
        critic_weights,
        far_weights,
        critic_first,
        far_first,
        critic_second,
        far_second,
        *places_actor,
        *places_critic,
        *actor_net[5:7],
        *[pltpu.with_memory_space_constraint(value, pltpu.VMEM) for value in kept],
    )
    actor_moved = twin_swap(send_actor)
    two = two + two_moved
    two, keep_actor, actor_moved = lax.optimization_barrier((two, keep_actor, actor_moved))
    actor = keep_actor + actor_moved
    turned = masks[len(masks) // 2 :] + masks[: len(masks) // 2]
    later = masks[:-1]
    for index, pair in enumerate(zip(masks, turned)):
        moved = partner_by_core(actor, pair)
        if index < len(later):
            two = two + partner(two, later[index - 1])
        actor = actor + moved
    actor_other = twin_swap(actor)
    two_other = to_second(two)

    def step(net, loss_lane, halves, sources, name):
        vector = pl.BlockSpec(memory_space=pltpu.VMEM)
        scalar = pl.BlockSpec(memory_space=pltpu.SMEM)
        return pl.pallas_call(
            lambda *refs: step_kernel(net, loss_lane, *refs),
            in_specs=[scalar] + [vector] * (len(halves) + len(sources)),
            out_specs=[vector] * len(sources) + [scalar],
            out_shape=[jax.ShapeDtypeStruct(source.shape, F32) for source in sources]
            + [jax.ShapeDtypeStruct((1,), F32)],
            scratch_shapes=[pltpu.VMEM((FLAT_ROWS, LANES), F32)] * 2,
            compiler_params=params,
            name=name,
        )(core, *halves, *sources)

    new_critic, new_critic_first, new_critic_second, new_target_critic, critic_loss = step(
        CRITIC,
        1,
        (one, one_other, two, two_other),
        (critic_weights, critic_first, critic_second, target_critic),
        "critic_step",
    )
    new_actor, new_actor_first, new_actor_second, new_target_actor, actor_loss = step(
        ACTOR,
        8,
        (actor, actor_other),
        (actor_weights, actor_first, actor_second, target_actor),
        "actor_step",
    )
    return (
        new_actor,
        new_actor_first,
        new_actor_second,
        new_critic,
        new_critic_first,
        new_critic_second,
        new_target_actor,
        new_target_critic,
        critic_loss,
        actor_loss.reshape(()),
    )


def solution(mesh):
    columns = P(None, "dp")
    critic = P("twin", None)
    return jax.shard_map(
        on_device,
        mesh=mesh,
        in_specs=(
            columns,
            columns,
            P("dp"),
            columns,
            P("dp"),
            columns,
            P(),
            P(),
            P(),
            critic,
            critic,
            critic,
            P(),
            critic,
        ),
        out_specs=(P(), P(), P(), critic, critic, critic, P(), critic, P("twin"), P()),
        check_vma=False,
    )
```
